512 devices in a mesh: band: 8 (over z), gx: 8 (over y_hi, core), gyz: 8 (over x, y_lo).
Axes of the slice: x: 4, y: 8 (y_hi: 4, y_lo: 2; y = y_hi * 2 + y_lo), z: 8, core: 2. Of those that a mesh axis runs over, the one named last changes fastest.
Arguments:
- orbitals: float32 [64, 64, 64, 128], P('band', 'gx', 'gyz'), may hold values from -14 to 14
- local_potential: float32 [64, 64, 128], P('gx', 'gyz'), may hold values from -2 to 0
- occupations: float32 [64], P('band'), may hold values from 0 to 2
- proj_values: float32 [64, 4, 512], replicated, may hold values from -0.25 to 0.25
- proj_strength: float32 [64, 4], replicated, may hold values from 0.5 to 3
- atom_block: int32 [64], replicated, may hold values from 0 to 63
- atom_offset: int32 [64, 3], replicated, may hold values from 0 to 120, as said below
Outputs:
- filtered: float32 [64, 64, 64, 128], P('band', 'gx', 'gyz')
- hartree: float32 [64, 64, 128], P('gx', 'gyz')
The draws below stay inside these ranges and needn't reach their ends.
Inputs may be any that keep to these rules, and one draw needn't show every extreme that they name: `atom_offset`: column 0 lies in 0 to 0, column 1 in 0 to 0, column 2 in 0 to 120.
All inputs are finite; a program needn't handle non-finite values.
Results may differ from the reference program's by a relative error of at most 0.0001.
Values sent between devices are 32-bit elements; how exact they have to be, the bound alone decides.
No kernel may reach another device: no remote copies, remote signals or barrier semaphores. Data moves between devices by JAX's collectives and lax.ppermute only.
A program may use at most 64 MiB of HBM per device.

```python
import math
import jax
import jax.numpy as jnp
from jax import lax

CX = 8
CY = 8
NZ = 128
NPROJ = 4
PB = 8
DEGREE = 8
LEVELS = 4
PRE = 2
POST = 2
COARSE = 4
BANDS = 64
NX = 64
NY = 64
BLOCKS = 64
ATOMS = 64
N_GYZ = 8


def draw_orbitals(key, part):
    key = jax.random.fold_in(key, 5)
    key_noise, key_phase, key_count = jax.random.split(key, 3)
    extent = (BANDS, NX, NY, NZ)
    noise_part = jnp.clip(jax.random.normal(key_noise, extent, jnp.float32), -6.0, 6.0)
    strength = 4.0
    phases = jax.random.uniform(key_phase, (4, BANDS, 1, 1, 1), jnp.float32, 0.0, 2.0 * jnp.pi)
    wave_counts = jax.random.randint(key_count, (2, BANDS, 1, 1, 1), 1, 3).astype(jnp.float32)
    cells_x = jnp.arange(NX).astype(jnp.int32).reshape(1, NX, 1, 1)
    cells_y = jnp.arange(NY).astype(jnp.int32).reshape(1, 1, NY, 1)
    cells_z = jnp.arange(NZ).astype(jnp.int32).reshape(1, 1, 1, NZ)
    place_x = cells_x.astype(jnp.float32)
    place_y = cells_y.astype(jnp.float32)
    place_z = cells_z.astype(jnp.float32)
    sign_x = 1.0 - 2.0 * (cells_x % 2).astype(jnp.float32)
    sign_y = 1.0 - 2.0 * (cells_y % 2).astype(jnp.float32)
    along_x = sign_x * jnp.cos(2.0 * jnp.pi * wave_counts[0] * place_y / NY + phases[0]) * jnp.cos(2.0 * jnp.pi * place_z / NZ + phases[1])
    along_y = sign_y * jnp.cos(2.0 * jnp.pi * wave_counts[1] * place_x / NX + phases[2]) * jnp.cos(2.0 * jnp.pi * place_z / NZ + phases[3])
    return noise_part + strength * (along_x + along_y)


def draw_occupations(key, part):
    key = jax.random.fold_in(key, 7)
    noise = 0.5 * jax.random.normal(key, (BANDS,), jnp.float32)
    position = jnp.arange(BANDS).astype(jnp.float32) / BANDS
    steepness = 6.0
    return 2.0 / (1.0 + jnp.exp(steepness * (position - 0.5) + noise))


def draw_atom_offset(key, part):
    key = jax.random.fold_in(key, 11)
    key_x, key_y, key_z, key_pick = jax.random.split(key, 4)
    offset_x = jax.random.randint(key_x, (ATOMS,), 0, CX - PB + 1)
    offset_y = jax.random.randint(key_y, (ATOMS,), 0, CY - PB + 1)
    offset_z = jax.random.randint(key_z, (ATOMS,), 0, NZ - PB + 1)
    chosen = jax.random.randint(key_pick, (), 0, ATOMS)
    marked = jnp.arange(ATOMS) == chosen
    offset_x = jnp.where(marked, CX - PB, offset_x)
    offset_y = jnp.where(marked, CY - PB, offset_y)
    offset_z = jnp.where(marked, NZ - PB, offset_z)
    return jnp.stack([offset_x, offset_y, offset_z], axis=1).astype(jnp.int32)


def with_ends(entries, key, smallest, high):
    spot = [jax.random.randint(jax.random.fold_in(key, axis), (), 0, length) for axis, length in enumerate(entries.shape)]
    widest = entries.shape.index(max(entries.shape))
    next_to = spot[:widest] + [(spot[widest] + 1) % entries.shape[widest]] + spot[widest + 1:]
    return entries.at[tuple(spot)].set(smallest).at[tuple(next_to)].set(high)


def levels(stream_key, shape, cuts, smallest, high):
    def one(dim, shards_of):
        draws = jax.random.uniform(jax.random.fold_in(jax.random.fold_in(stream_key, 6), dim), (shards_of,), jnp.float32, smallest / len(cuts), high / len(cuts))
        return jnp.repeat(jnp.exp(draws), shape[dim] // shards_of).reshape((-1,) + (1,) * (len(shape) - dim - 1))

    level = one(*cuts[0])
    for cut in cuts[1:]:
        level = level * one(*cut)
    return level


def centred(rng, dims, scale, reach, dtype=jnp.bfloat16):
    entries = scale * jax.random.normal(rng, dims, jnp.float32)
    return jnp.clip(entries, min=-reach, max=reach).astype(dtype)


def setup_inputs(seed: int = 0) -> dict:
    splits = jax.random.split(jax.random.key(seed), 8)
    return {
        "orbitals": draw_orbitals(jax.random.fold_in(splits[7], 71), 0),
        "local_potential": jnp.clip(-2.0 + 2.0 * jax.random.uniform(splits[1], (NX, NY, NZ), jnp.float32) ** levels(splits[1], (NX, NY, NZ), ((0, 8), (1, 8)), -0.2, 0.2), -2.0, 0.0),
        "occupations": draw_occupations(jax.random.fold_in(splits[7], 71), 0),
        "proj_values": centred(splits[3], (ATOMS, NPROJ, PB * PB * PB), (PB * PB * PB) ** -0.5, 0.25, jnp.float32),
        "proj_strength": jnp.clip(jnp.exp(jax.random.uniform(splits[4], (ATOMS, NPROJ), jnp.float32, math.log(0.5), math.log(3.0))), 0.5, 3.0),
        "atom_block": with_ends(jax.random.randint(splits[5], (ATOMS,), 0, BLOCKS), jax.random.fold_in(splits[5], 1), 0, BLOCKS - 1).astype(jnp.int32),
        "atom_offset": draw_atom_offset(jax.random.fold_in(splits[7], 71), 0),
    }


STENCIL = (-5369.0 / 1800.0, 12.0 / 7.0, -15.0 / 56.0, 10.0 / 189.0, -1.0 / 112.0, 2.0 / 1925.0, -1.0 / 16632.0)
stencil_reach = 6
center = 12.0
half_width = 8.0
spectrum_low = 0.0
damping = 0.8


def axis_second(padded, along, length):
    summed = STENCIL[1] * (lax.slice_in_dim(padded, stencil_reach + 1, stencil_reach + 1 + length, axis=along) + lax.slice_in_dim(padded, stencil_reach - 1, stencil_reach - 1 + length, axis=along))
    for offset in range(2, stencil_reach + 1):
        summed = summed + STENCIL[offset] * (lax.slice_in_dim(padded, stencil_reach + offset, stencil_reach + offset + length, axis=along) + lax.slice_in_dim(padded, stencil_reach - offset, stencil_reach - offset + length, axis=along))
    return summed


def laplacian(samples, padded_list, axes_list):
    summed = 3.0 * STENCIL[0] * samples
    for padded, along in zip(padded_list, axes_list):
        summed = summed + axis_second(padded, along, samples.shape[along])
    return summed


def chebyshev(orbital, apply_ham):
    sigma_now = half_width / (spectrum_low - center)
    tau_value = 2.0 / sigma_now
    previous = orbital
    current = (apply_ham(orbital) - center * orbital) * (sigma_now / half_width)
    for _ in range(DEGREE - 1):
        sigma_next = 1.0 / (tau_value - sigma_now)
        upcoming = (apply_ham(current) - center * current) * (2.0 * sigma_next / half_width) - (sigma_now * sigma_next) * previous
        previous = current
        current = upcoming
        sigma_now = sigma_next
    return current


def restrict_mean(residual):
    sx, sy, sz = residual.shape
    return residual.reshape(sx // 2, 2, sy // 2, 2, sz // 2, 2).mean(axis=(1, 3, 5))


def prolong_copy(coarse):
    sx, sy, sz = coarse.shape
    wide = jnp.broadcast_to(coarse[:, None, :, None, :, None], (sx, 2, sy, 2, sz, 2))
    return wide.reshape(2 * sx, 2 * sy, 2 * sz)


def cycle_level(grid_level, source, pad_cells):
    level_scale = 4.0 ** grid_level
    diagonal = 6.0 / level_scale

    def operate(iterate):
        padded = pad_cells(iterate)
        neighbours = padded[2:, 1:-1, 1:-1] + padded[:-2, 1:-1, 1:-1]
        neighbours = neighbours + padded[1:-1, 2:, 1:-1] + padded[1:-1, :-2, 1:-1]
        neighbours = neighbours + padded[1:-1, 1:-1, 2:] + padded[1:-1, 1:-1, :-2]
        return (6.0 * iterate - neighbours) / level_scale

    sweeps = COARSE if grid_level == LEVELS - 1 else PRE
    iterate = damping * source / diagonal
    for _ in range(sweeps - 1):
        iterate = iterate + damping * (source - operate(iterate)) / diagonal
    if grid_level < LEVELS - 1:
        residual = source - operate(iterate)
        correction = cycle_level(grid_level + 1, restrict_mean(residual), pad_cells)
        iterate = iterate + prolong_copy(correction)
        for _ in range(POST):
            iterate = iterate + damping * (source - operate(iterate)) / diagonal
    return iterate


def reference(orbitals, local_potential, occupations, proj_values, proj_strength, atom_block, atom_offset):
    anchor_x = (atom_block // N_GYZ) * CX + atom_offset[:, 0]
    anchor_y = (atom_block % N_GYZ) * CY + atom_offset[:, 1]
    anchor_z = atom_offset[:, 2]

    def nonlocal_term(orbital):
        def visit_atom(atom_index, accumulated):
            corner = (anchor_x[atom_index], anchor_y[atom_index], anchor_z[atom_index])
            window = lax.dynamic_slice(orbital, corner, (PB, PB, PB)).reshape(PB * PB * PB)
            shapes = proj_values[atom_index]
            weights = jnp.dot(shapes, window, precision=lax.Precision.HIGHEST) * proj_strength[atom_index]
            added_term = jnp.dot(weights, shapes, precision=lax.Precision.HIGHEST).reshape(PB, PB, PB)
            current = lax.dynamic_slice(accumulated, corner, (PB, PB, PB))
            return lax.dynamic_update_slice(accumulated, current + added_term, corner)
        return lax.fori_loop(0, ATOMS, visit_atom, jnp.zeros_like(orbital))

    def hamiltonian(orbital):
        x_padded = jnp.pad(orbital, ((stencil_reach, stencil_reach), (0, 0), (0, 0)))
        y_padded = jnp.pad(orbital, ((0, 0), (stencil_reach, stencil_reach), (0, 0)))
        z_padded = jnp.pad(orbital, ((0, 0), (0, 0), (stencil_reach, stencil_reach)))
        kinetic = laplacian(orbital, (x_padded, y_padded, z_padded), (0, 1, 2))
        return -0.5 * kinetic + local_potential * orbital + nonlocal_term(orbital)

    def one_band(density, inputs):
        orbital, occupation = inputs
        result = chebyshev(orbital, hamiltonian)
        return density + occupation * result * result, result

    density, filtered = lax.scan(one_band, jnp.zeros((NX, NY, NZ), jnp.float32), (orbitals, occupations))
    source = density / BANDS

    def pad_cells(iterate):
        return jnp.pad(iterate, 1)

    hartree = cycle_level(0, source, pad_cells)
    return filtered, hartree
```

```python
import functools

import jax
import jax.numpy as jnp
import numpy as np
from jax import lax
from jax.experimental import pallas as pl
from jax.experimental.pallas import tpu as pltpu
from jax.sharding import Mesh
from jax.sharding import PartitionSpec as P

DEGREE = 8
LEVELS = 4
PRE = 2
POST = 2
COARSE = 4
STENCIL = (
    -5369.0 / 1800.0,
    12.0 / 7.0,
    -15.0 / 56.0,
    10.0 / 189.0,
    -1.0 / 112.0,
    2.0 / 1925.0,
    -1.0 / 16632.0,
)
HALF = tuple(-0.5 * c for c in STENCIL)
REACH = 6
CENTER = 12.0
HALF_WIDTH = 8.0
DAMPING = 0.8
BAND = "z"
GX = ("yhi", "core")
GYZ = ("xhi", "xlo", "ylo")
PLANE = GX + GYZ
GROUP = ("core", "xlo", "ylo")
CHIPS = ((0, 0), (0, 1), (1, 1), (1, 0))
SLAB_DEVICE = [c * 4 + xl * 2 + yl for xl, yl in CHIPS for c in (0, 1)]
VMEM = pltpu.CompilerParams(vmem_limit_bytes=40 * 1024 * 1024)
F32 = jnp.float32
BF16 = jnp.bfloat16


def plane_index(band, slab):
    yhi, xhi = band // 2, band % 2
    xlo, ylo = CHIPS[slab // 2]
    return yhi * 16 + (slab % 2) * 8 + xhi * 4 + xlo * 2 + ylo


def coupling():
    own, xu, xd, yu, yd = (np.zeros((128, 128)) for _ in range(5))
    for zh in range(2):
        for xi in range(8):
            for yi in range(8):
                i = zh * 64 + xi * 8 + yi
                for o in range(8):
                    for m, k in ((own, abs(o - xi)), (xu, o + 8 - xi), (xd, xi + 8 - o)):
                        if 1 <= k <= REACH:
                            m[i, zh * 64 + o * 8 + yi] += HALF[k]
                    for m, k in ((own, abs(o - yi)), (yu, o + 8 - yi), (yd, yi + 8 - o)):
                        if 1 <= k <= REACH:
                            m[i, zh * 64 + xi * 8 + o] += HALF[k]
    whole = np.concatenate([own, xu, xd, yu, yd], axis=1).astype(np.float32)
    high = whole.astype(jnp.bfloat16)
    low = (whole - high.astype(np.float32)).astype(jnp.bfloat16)
    return np.concatenate([high, high], axis=0), low


def lanes_low(shape):
    return lax.broadcasted_iota(jnp.int32, shape, len(shape) - 1) < 64


def swap(x):
    return pltpu.roll(x, 64, x.ndim - 1)


def split3(x):
    a = x.astype(BF16)
    r = x - a.astype(F32)
    b = r.astype(BF16)
    c = (r - b.astype(F32)).astype(BF16)
    return a, b, c


def pack_kernel(orb_ref, pot_ref, proj_ref, pick_ref, out_ref, tiles_ref):
    low = lanes_low((8, 128))
    for q in range(4):
        turned = orb_ref[q * 128 : (q + 1) * 128, :].T
        for s in range(8):
            a = turned[s * 16 : s * 16 + 8, :]
            b = turned[s * 16 + 8 : s * 16 + 16, :]
            out_ref[plane_index(2 * q, s), 0:8, :] = jnp.where(low, a, swap(b))
            out_ref[plane_index(2 * q + 1, s), 0:8, :] = jnp.where(low, swap(a), b)
    pot = pot_ref[...]
    turned = jnp.concatenate([pot, pot], axis=0).T
    for s in range(8):
        piece = jnp.where(low, turned[s * 16 : s * 16 + 8, :], turned[s * 16 + 8 : s * 16 + 16, :])
        for b in range(8):
            out_ref[plane_index(b, s), 8:16, :] = piece

    keep = lax.broadcasted_iota(jnp.int32, (32, 8, 512), 2) % 8 == lax.broadcasted_iota(
        jnp.int32, (32, 8, 512), 1
    )

    def body(i, carry):
        rows = proj_ref[pl.ds(pl.multiple_of(i * 32, 32), 32), :]
        spread = jnp.where(keep, rows[:, None, :], 0.0).reshape(256, 512)
        pick = pick_ref[...]
        total = sum(jnp.dot(part, pick, preferred_element_type=F32) for part in split3(spread))
        tiles_ref[pl.ds(i * 8, 8), :, :, :] = total.reshape(8, 4, 8, 128)
        return carry

    lax.fori_loop(0, 8, body, 0)


def pack(orbitals, potential, proj):
    pick = (np.arange(512)[:, None] // 8 == np.arange(128)[None, :] % 64).astype(jnp.bfloat16)
    return pl.pallas_call(
        pack_kernel,
        out_shape=(
            jax.ShapeDtypeStruct((64, 16, 128), F32),
            jax.ShapeDtypeStruct((64, 4, 8, 128), F32),
        ),
        compiler_params=VMEM,
    )(orbitals.reshape(512, 128), potential.reshape(64, 128), proj.reshape(256, 512), pick)


ID, SRC, ROW, UPPER, ROW_L, ON_L, ROW_U, ON_U, META = range(9)


def double_kernel(
    first, last, coef1, coef2, lists, strength, prev_ref, own_ref, next_ref, *refs
):
    refs = list(refs)
    if first:
        older_ref = pot_ref = None
    else:
        older_ref, pot_ref = refs.pop(0), refs.pop(0)
    tiles_ref, mat_ref, mat_low_ref, ones_ref = refs[:4]
    refs = refs[4:]
    out_ref = refs.pop(0)
    if first:
        pot_ref = refs.pop(0)
    mid_ref = None if last else refs.pop(0)
    ext, mid, new, c_own, c_xu, c_xd, c_yu, c_yd, weights = refs
    low = lanes_low((8, 128))
    count = lists[META, 0]
    below = lists[META, 1] > 0
    above = lists[META, 2] > 0
    zero8 = jnp.zeros((8, 128), F32)

    def fill(i, carry):
        for u in range(4):
            src = i * 4 + u
            p, o, n = prev_ref[src, 0:8, :], own_ref[src, 0:8, :], next_ref[src, 0:8, :]
            ext[src, 0:8, :] = p
            ext[src, 8:16, :] = swap(jnp.where(low, o, p))
            ext[src, 16:24, :] = o
            ext[src, 24:32, :] = swap(jnp.where(low, n, o))
            ext[src, 32:40, :] = n
            if first:
                p, o, n = prev_ref[src, 8:16, :], own_ref[src, 8:16, :], next_ref[src, 8:16, :]
                shift = 3.0 * HALF[0] - CENTER
                pot_ref[src, 0:8, :] = swap(jnp.where(low, o, p)) + shift
                pot_ref[src, 8:16, :] = o + shift
                pot_ref[src, 16:24, :] = swap(jnp.where(low, n, o)) + shift
        return carry

    lax.fori_loop(0, 16, fill, 0)
    for t in range(3):
        for e in range(8):
            c_xu[t, e, :, :] = zero8
            c_xd[t, 64 + e, :, :] = zero8

    def products(f_ref, first_tile, n_tiles):
        def body(i, carry):
            t = first_tile + i // 2
            base = pl.multiple_of((i % 2) * 32, 32)
            rows = pl.multiple_of(t * 8 + 8, 8)
            x = f_ref[pl.ds(base, 32), pl.ds(rows, 8), :].reshape(256, 128)
            high = x.astype(BF16)
            rest = (x - high.astype(F32)).astype(BF16)
            y = jnp.dot(
                jnp.concatenate([high, rest], axis=1), mat_ref[...], preferred_element_type=F32
            ) + jnp.dot(high, mat_low_ref[...], preferred_element_type=F32)
            y = y.reshape(32, 8, 640)
            c_own[t, pl.ds(base, 32), :, :] = y[:, :, 0:128]
            c_xu[t, pl.ds(base + 8, 32), :, :] = y[:, :, 128:256]
            c_xd[t, pl.ds(base, 32), :, :] = y[:, :, 256:384]
            c_yu[t, pl.ds(base, 32), :, :] = y[:, :, 384:512]
            c_yd[t, pl.ds(base, 32), :, :] = y[:, :, 512:640]
            return carry

        lax.fori_loop(0, 2 * n_tiles, body, 0)

    def project(f_ref):
        def body(i, carry):
            found = []
            for u in range(8):
                ii = i * 8 + u
                w = f_ref[lists[SRC, ii], pl.ds(lists[ROW, ii], 8), :]
                w = jnp.where(low == (lists[UPPER, ii] == 0), w, 0.0)
                found.append(jnp.sum(tiles_ref[lists[ID, ii]] * w[None], axis=1))
            q = jnp.concatenate(found, axis=0)
            high = q.astype(BF16)
            rest = (q - high.astype(F32)).astype(BF16)
            weights[pl.ds(pl.multiple_of(i * 32, 32), 32), :] = jnp.dot(
                jnp.concatenate([high, rest], axis=1), ones_ref[...], preferred_element_type=F32
            )
            return carry

        lax.fori_loop(0, (count + 7) // 8, body, 0)

    def combine(f_ref, y_ref, older, t, coef):
        a, b = coef
        r = t * 8 + 8

        def body(xb, carry):
            for yb in range(8):
                src = xb * 8 + yb
                total = c_own[t, src] + c_xu[t, src] + c_xd[t, src + 8]
                if yb > 0:
                    total = total + c_yu[t, src - 1]
                if yb < 7:
                    total = total + c_yd[t, src + 1]
                for k in range(1, REACH + 1):
                    total = total + HALF[k] * (
                        f_ref[src, r + k : r + k + 8, :] + f_ref[src, r - k : r - k + 8, :]
                    )
                total = total + pot_ref[src, t * 8 : t * 8 + 8, :] * f_ref[src, r : r + 8, :]
                total = a * total
                if older is not None:
                    total = total - b * older(src)
                if t == 0:
                    total = jnp.where(jnp.logical_or(below, jnp.logical_not(low)), total, 0.0)
                if t == 2:
                    total = jnp.where(jnp.logical_or(above, low), total, 0.0)
                y_ref[src, r : r + 8, :] = total
            return carry

        lax.fori_loop(0, 8, body, 0)

    def spread(y_ref, a):
        def body(i, carry):
            w = weights[pl.ds(pl.multiple_of(i * 32, 32), 32), :]
            for u in range(8):
                ii = i * 8 + u
                atom, src = lists[ID, ii], lists[SRC, ii]
                t = zero8
                for p in range(4):
                    t = t + (strength[p, ii] * a) * w[u * 4 + p : u * 4 + p + 1, :] * tiles_ref[atom, p]
                rows = pl.ds(lists[ROW_L, ii], 8)
                on = jnp.logical_and(low, lists[ON_L, ii] > 0)
                y_ref[src, rows, :] = y_ref[src, rows, :] + jnp.where(on, t, 0.0)
                rows = pl.ds(lists[ROW_U, ii], 8)
                on = jnp.logical_and(jnp.logical_not(low), lists[ON_U, ii] > 0)
                y_ref[src, rows, :] = y_ref[src, rows, :] + jnp.where(on, t, 0.0)
            return carry

        lax.fori_loop(0, (count + 7) // 8, body, 0)

    products(ext, 0, 3)
    project(ext)
    for t in range(3):
        older = None if first else (lambda src, t=t: older_ref[src, t * 8 : t * 8 + 8, :])
        combine(ext, mid, older, t, coef1)
    spread(mid, coef1[0])
    products(mid, 1, 1)
    project(mid)
    combine(mid, new, lambda src: ext[src, 16:24, :], 1, coef2)
    spread(new, coef2[0])
    out_ref[...] = new[:, 16:24, :]
    if not last:
        mid_ref[...] = mid[:, 8:32, :]


def double_step(first, last, coef1, coef2, lists, strength, halo, own, older, pot, tiles, mats):
    smem = pl.BlockSpec(memory_space=pltpu.SMEM)
    vmem = pl.BlockSpec(memory_space=pltpu.VMEM)
    ins = [lists, strength, halo[0], own, halo[1]]
    if not first:
        ins += [older, pot]
    ins += [tiles, *mats]
    outs = [jax.ShapeDtypeStruct((64, 8, 128), F32)]
    if first:
        outs.append(jax.ShapeDtypeStruct((64, 24, 128), F32))
    if not last:
        outs.append(jax.ShapeDtypeStruct((64, 24, 128), F32))
    return pl.pallas_call(
        functools.partial(double_kernel, first, last, coef1, coef2),
        out_shape=tuple(outs),
        in_specs=[smem, smem] + [vmem] * (len(ins) - 2),
        out_specs=tuple([vmem] * len(outs)),
        scratch_shapes=[
            pltpu.VMEM((64, 40, 128), F32),
            pltpu.VMEM((64, 40, 128), F32),
            pltpu.VMEM((64, 40, 128), F32),
            pltpu.VMEM((3, 64, 8, 128), F32),
            pltpu.VMEM((3, 72, 8, 128), F32),
            pltpu.VMEM((3, 72, 8, 128), F32),
            pltpu.VMEM((3, 64, 8, 128), F32),
            pltpu.VMEM((3, 64, 8, 128), F32),
            pltpu.VMEM((256, 128), F32),
        ],
        compiler_params=VMEM,
    )(*ins)


def atom_lists(slab, proj_strength, atom_block, atom_offset):
    number = jnp.arange(64, dtype=jnp.int32)
    dz = atom_offset[:, 2] - 16 * slab
    near = jnp.logical_and(dz >= -15, dz <= 23)
    before = jnp.sum(
        jnp.logical_and(near[None, :], number[None, :] < number[:, None]).astype(jnp.int32), axis=1
    )
    pick = jnp.logical_and(near[None, :], before[None, :] == number[:, None])

    def listed(values, empty):
        return jnp.sum(jnp.where(pick, values[None, :], 0), axis=1) + jnp.where(
            jnp.any(pick, axis=1), 0, empty
        )

    at = listed(dz, 0)
    valid = jnp.any(pick, axis=1)
    source = listed(jnp.clip(atom_block, 0, 63), 0)
    upper = at > 8
    meta = jnp.zeros((64,), jnp.int32).at[0].set(jnp.sum(near.astype(jnp.int32)))
    meta = meta.at[1].set(slab).at[2].set(7 - slab)
    lists = jnp.stack(
        [
            listed(number, 0),
            source,
            jnp.where(upper, at - 8, at) + 16,
            upper.astype(jnp.int32),
            jnp.clip(at, -16, 16) + 16,
            jnp.logical_and(valid, at <= 15).astype(jnp.int32),
            jnp.clip(at - 8, -16, 16) + 16,
            jnp.logical_and(valid, at >= -7).astype(jnp.int32),
            meta,
        ]
    )
    strength = jnp.sum(jnp.where(pick[None], proj_strength.T[:, None, :], 0.0), axis=2)
    return lists, strength


def unpack_kernel(occ, in_ref, out_ref, density_ref):
    low = lanes_low((8, 128))
    density = jnp.zeros((64, 128), F32)
    for q in range(4):
        rows = []
        for s in range(8):
            a = in_ref[plane_index(2 * q, s)]
            b = in_ref[plane_index(2 * q + 1, s)]
            rows += [jnp.where(low, a, swap(b)), jnp.where(low, swap(a), b)]
        block = jnp.concatenate(rows, axis=0).T
        out_ref[q * 128 : (q + 1) * 128, :] = block
        for e in range(2):
            part = block[e * 64 : (e + 1) * 64, :]
            density = density + occ[2 * q + e] * part * part
    density_ref[...] = density


def unpack(occupations, slabs):
    smem = pl.BlockSpec(memory_space=pltpu.SMEM)
    vmem = pl.BlockSpec(memory_space=pltpu.VMEM)
    return pl.pallas_call(
        unpack_kernel,
        out_shape=(jax.ShapeDtypeStruct((512, 128), F32), jax.ShapeDtypeStruct((64, 128), F32)),
        in_specs=[smem, vmem],
        out_specs=(vmem, vmem),
        compiler_params=VMEM,
    )(occupations, slabs)


def neighbours_sum(v):
    z = jnp.pad(v[1:-1, 1:-1], ((0, 0), (0, 0), (1, 1)))
    total = v[2:, 1:-1] + v[:-2, 1:-1] + v[1:-1, 2:] + v[1:-1, :-2]
    return total + z[:, :, 2:] + z[:, :, :-2]


def restrict_mean(r):
    sx, sy, sz = r.shape
    r = r.reshape(sx // 2, 2, sy, sz).sum(axis=1)
    r = r.reshape(sx // 2, sy // 2, 2, sz).sum(axis=2)
    halve = np.zeros((sz, sz // 2), np.float32)
    halve[np.arange(sz), np.arange(sz) // 2] = 0.125
    return jnp.einsum("xyz,zw->xyw", r, halve, precision=lax.Precision.HIGHEST)


def prolong_copy(e):
    sx, sy, sz = e.shape
    double = np.zeros((sz, 2 * sz), np.float32)
    double[np.arange(2 * sz) // 2, np.arange(2 * sz)] = 1.0
    e = jnp.einsum("xyz,zw->xyw", e, double, precision=lax.Precision.HIGHEST)
    e = jnp.broadcast_to(e[:, None, :, None, :], (sx, 2, sy, 2, 2 * sz))
    return e.reshape(2 * sx, 2 * sy, 2 * sz)


def coarse_cycle(level, source):
    scale = 4.0**level
    diagonal = 6.0 / scale

    def operate(v):
        padded = jnp.pad(v, ((1, 1), (1, 1), (0, 0)))
        return (6.0 * v - neighbours_sum(padded)) / scale

    v = DAMPING * source / diagonal
    for _ in range((COARSE if level == LEVELS - 1 else PRE) - 1):
        v = v + DAMPING * (source - operate(v)) / diagonal
    if level < LEVELS - 1:
        v = v + prolong_copy(coarse_cycle(level + 1, restrict_mean(source - operate(v))))
        for _ in range(POST):
            v = v + DAMPING * (source - operate(v)) / diagonal
    return v


def exchange(value, axes, dim, width, order=None):
    order = order or list(range(8))
    up = [(order[i], order[i + 1]) for i in range(7)]
    down = [(j, i) for i, j in up]
    length = value.shape[dim]
    before = lax.ppermute(lax.slice_in_dim(value, length - width, length, axis=dim), axes, up)
    after = lax.ppermute(lax.slice_in_dim(value, 0, width, axis=dim), axes, down)
    return before, after


def hartree_of(density):
    gx, gyz = lax.axis_index(GX), lax.axis_index(GYZ)
    before, after = exchange(density, GX, 0, 3)
    f = jnp.concatenate([before, density, after], axis=0)
    before, after = exchange(f, GYZ, 1, 3)
    f = jnp.concatenate([before, f, after], axis=1)

    def inside(width):
        def along(index):
            cell = jnp.arange(8 + 2 * width) - width + 8 * index
            return jnp.logical_and(cell >= 0, cell < 64)

        return jnp.logical_and(along(gx)[:, None, None], along(gyz)[None, :, None])

    def sweep(v, source):
        centre = v[1:-1, 1:-1]
        return centre + (DAMPING / 6.0) * (source - (6.0 * centre - neighbours_sum(v)))

    v = (DAMPING / 6.0) * f
    v = jnp.where(inside(2), sweep(v, f[1:-1, 1:-1]), 0.0)
    inner = v[1:-1, 1:-1]
    residual = f[2:-2, 2:-2] - (6.0 * inner - neighbours_sum(v))
    coarse = restrict_mean(residual[1:-1, 1:-1])
    sent = jnp.broadcast_to(coarse.reshape(1, 8, 128), (64, 8, 128))
    got = lax.all_to_all(sent, PLANE, 0, 0, tiled=True)
    whole = got.reshape(8, 8, 4, 4, 64).transpose(0, 2, 1, 3, 4).reshape(32, 32, 64)
    error = jnp.pad(coarse_cycle(1, whole), ((1, 1), (1, 1), (0, 0)))
    error = lax.dynamic_slice(error, (4 * gx, 4 * gyz, 0), (6, 6, 64))
    v = v + prolong_copy(error)
    v = jnp.where(inside(1), sweep(v, f[2:-2, 2:-2]), 0.0)
    return sweep(v, f[3:-3, 3:-3])


def local(
    orbitals, local_potential, occupations, proj_values, proj_strength, atom_block, atom_offset
):
    core, xlo, ylo = (lax.axis_index(a) for a in GROUP)
    slab = 2 * (xlo * (3 - ylo) + (1 - xlo) * ylo) + core
    lists, strength = atom_lists(slab, proj_strength, atom_block, atom_offset)
    high, low = coupling()
    mats = (jnp.asarray(high), jnp.asarray(low), jnp.ones((256, 128), BF16))

    packed, tiles = pack(orbitals, local_potential, proj_values)
    own = lax.all_to_all(packed, PLANE, 0, 0, tiled=True)

    sigma = HALF_WIDTH / (0.0 - CENTER)
    tau = 2.0 / sigma
    coefs = [(sigma / HALF_WIDTH, 0.0)]
    for _ in range(DEGREE - 1):
        following = 1.0 / (tau - sigma)
        coefs.append((2.0 * following / HALF_WIDTH, sigma * following))
        sigma = following
    older = pot = None
    for k in range(0, DEGREE, 2):
        first, last = k == 0, k == DEGREE - 2
        halo = exchange(own, GROUP, 1, own.shape[1], SLAB_DEVICE)
        outs = list(
            double_step(
                first, last, coefs[k], coefs[k + 1], lists, strength, halo, own, older, pot, tiles, mats
            )
        )
        own = outs.pop(0)
        if first:
            pot = outs.pop(0)
        if not last:
            older = outs.pop(0)

    back = lax.all_to_all(own, PLANE, 0, 0, tiled=True)
    filtered, density = unpack(occupations, back)
    sent = jnp.broadcast_to(density[None], (8, 64, 128))
    density = jnp.sum(lax.all_to_all(sent, BAND, 0, 0, tiled=True), axis=0) / 64.0
    hartree = hartree_of(density.reshape(8, 8, 128))
    return filtered.reshape(8, 8, 8, 128), hartree


def solution(mesh):
    fine = Mesh(
        mesh.devices.reshape(8, 4, 2, 2, 2, 2), (BAND, "yhi", "core", "xhi", "xlo", "ylo")
    )
    bands, grid = P(BAND, GX, GYZ, None), P(GX, GYZ, None)
    return jax.shard_map(
        local,
        mesh=fine,
        in_specs=(bands, grid, P(BAND), P(), P(), P(), P()),
        out_specs=(bands, grid),
        check_vma=False,
    )
```

```python
import functools

import jax
import jax.numpy as jnp
import numpy as np
from jax import lax
from jax.experimental import pallas as pl
from jax.experimental.pallas import tpu as pltpu
from jax.sharding import Mesh
from jax.sharding import PartitionSpec as P

DEGREE = 8
POST = 2
COARSE = 4
STENCIL = (
    -5369.0 / 1800.0,
    12.0 / 7.0,
    -15.0 / 56.0,
    10.0 / 189.0,
    -1.0 / 112.0,
    2.0 / 1925.0,
    -1.0 / 16632.0,
)
HALF = tuple(-0.5 * c for c in STENCIL)
REACH = 6
CENTER = 12.0
HALF_WIDTH = 8.0
DAMPING = 0.8
BAND = "z"
GX = ("yhi", "core")
GYZ = ("xhi", "xlo", "ylo")
PLANE = GX + GYZ
GROUP = ("core", "xlo", "ylo")
CHIPS = ((0, 0), (0, 1), (1, 1), (1, 0))
SLAB_DEVICE = [c * 4 + xl * 2 + yl for xl, yl in CHIPS for c in (0, 1)]
VMEM = pltpu.CompilerParams(vmem_limit_bytes=40 * 1024 * 1024)
F32 = jnp.float32
BF16 = jnp.bfloat16


def plane_index(band, slab):
    yhi, xhi = band // 2, band % 2
    xlo, ylo = CHIPS[slab // 2]
    return yhi * 16 + (slab % 2) * 8 + xhi * 4 + xlo * 2 + ylo


def coupling(weights):
    own, xu, xd, yu, yd = (np.zeros((128, 128)) for _ in range(5))
    for zh in range(2):
        for xi in range(8):
            for yi in range(8):
                i = zh * 64 + xi * 8 + yi
                for o in range(8):
                    for m, k in ((own, abs(o - xi)), (xu, o + 8 - xi), (xd, xi + 8 - o)):
                        if 1 <= k < len(weights):
                            m[i, zh * 64 + o * 8 + yi] += weights[k]
                    for m, k in ((own, abs(o - yi)), (yu, o + 8 - yi), (yd, yi + 8 - o)):
                        if 1 <= k < len(weights):
                            m[i, zh * 64 + xi * 8 + o] += weights[k]
    whole = np.concatenate([own, xu, xd, yu, yd], axis=1).astype(np.float32)
    high = whole.astype(jnp.bfloat16)
    low = (whole - high.astype(np.float32)).astype(jnp.bfloat16)
    return np.concatenate([high, high], axis=0), low


def halves(x, axis):
    high = x.astype(BF16)
    return jnp.concatenate([high, (x - high.astype(F32)).astype(BF16)], axis=axis)


def lanes_low(shape):
    return lax.broadcasted_iota(jnp.int32, shape, len(shape) - 1) < 64


def swap(x):
    return pltpu.roll(x, 64, x.ndim - 1)


def split3(x):
    a = x.astype(BF16)
    r = x - a.astype(F32)
    b = r.astype(BF16)
    c = (r - b.astype(F32)).astype(BF16)
    return a, b, c


def pack_kernel(orb_ref, pot_ref, proj_ref, pick_ref, out_ref, tiles_ref):
    low = lanes_low((8, 128))
    for q in range(4):
        turned = orb_ref[q * 128 : (q + 1) * 128, :].T
        for s in range(8):
            a = turned[s * 16 : s * 16 + 8, :]
            b = turned[s * 16 + 8 : s * 16 + 16, :]
            out_ref[plane_index(2 * q, s), 0:8, :] = jnp.where(low, a, swap(b))
            out_ref[plane_index(2 * q + 1, s), 0:8, :] = jnp.where(low, swap(a), b)
    pot = pot_ref[...]
    turned = jnp.concatenate([pot, pot], axis=0).T
    for s in range(8):
        piece = jnp.where(low, turned[s * 16 : s * 16 + 8, :], turned[s * 16 + 8 : s * 16 + 16, :])
        for b in range(8):
            out_ref[plane_index(b, s), 8:16, :] = piece

    keep = lax.broadcasted_iota(jnp.int32, (32, 8, 512), 2) % 8 == lax.broadcasted_iota(
        jnp.int32, (32, 8, 512), 1
    )

    def body(i, carry):
        rows = proj_ref[pl.ds(pl.multiple_of(i * 32, 32), 32), :]
        spread = jnp.where(keep, rows[:, None, :], 0.0).reshape(256, 512)
        pick = pick_ref[...]
        total = sum(jnp.dot(part, pick, preferred_element_type=F32) for part in split3(spread))
        tiles_ref[pl.ds(i * 8, 8), :, :, :] = total.reshape(8, 4, 8, 128)
        return carry

    lax.fori_loop(0, 8, body, 0)


def pack(orbitals, potential, proj):
    pick = (np.arange(512)[:, None] // 8 == np.arange(128)[None, :] % 64).astype(jnp.bfloat16)
    return pl.pallas_call(
        pack_kernel,
        out_shape=(
            jax.ShapeDtypeStruct((64, 16, 128), F32),
            jax.ShapeDtypeStruct((64, 4, 8, 128), F32),
        ),
        compiler_params=VMEM,
    )(orbitals.reshape(512, 128), potential.reshape(64, 128), proj.reshape(256, 512), pick)


ID, SRC, ROW, UPPER, ROW_L, ON_L, ROW_U, ON_U, META = range(9)


def double_kernel(
    first, last, coef1, coef2, lists, strength, prev_ref, own_ref, next_ref, *refs
):
    refs = list(refs)
    if first:
        older_ref = pot_ref = None
    else:
        older_ref, pot_ref = refs.pop(0), refs.pop(0)
    tiles_ref, mat_ref, mat_low_ref, ones_ref = refs[:4]
    refs = refs[4:]
    out_ref = refs.pop(0)
    if first:
        pot_ref = refs.pop(0)
    mid_ref = None if last else refs.pop(0)
    ext, mid, new, c_own, c_xu, c_xd, c_yu, c_yd, weights = refs
    low = lanes_low((8, 128))
    count = lists[META, 0]
    below = lists[META, 1] > 0
    above = lists[META, 2] > 0
    zero8 = jnp.zeros((8, 128), F32)

    def fill(i, carry):
        for u in range(4):
            src = i * 4 + u
            p, o, n = prev_ref[src, 0:8, :], own_ref[src, 0:8, :], next_ref[src, 0:8, :]
            ext[src, 0:8, :] = p
            ext[src, 8:16, :] = swap(jnp.where(low, o, p))
            ext[src, 16:24, :] = o
            ext[src, 24:32, :] = swap(jnp.where(low, n, o))
            ext[src, 32:40, :] = n
            if first:
                p, o, n = prev_ref[src, 8:16, :], own_ref[src, 8:16, :], next_ref[src, 8:16, :]
                shift = 3.0 * HALF[0] - CENTER
                pot_ref[src, 0:8, :] = swap(jnp.where(low, o, p)) + shift
                pot_ref[src, 8:16, :] = o + shift
                pot_ref[src, 16:24, :] = swap(jnp.where(low, n, o)) + shift
        return carry

    lax.fori_loop(0, 16, fill, 0)
    for t in range(3):
        for e in range(8):
            c_xu[t, e, :, :] = zero8
            c_xd[t, 64 + e, :, :] = zero8

    def products(f_ref, first_tile, n_tiles):
        def body(i, carry):
            t = first_tile + i // 2
            base = pl.multiple_of((i % 2) * 32, 32)
            rows = pl.multiple_of(t * 8 + 8, 8)
            x = f_ref[pl.ds(base, 32), pl.ds(rows, 8), :].reshape(256, 128)
            high = x.astype(BF16)
            rest = (x - high.astype(F32)).astype(BF16)
            y = jnp.dot(
                jnp.concatenate([high, rest], axis=1), mat_ref[...], preferred_element_type=F32
            ) + jnp.dot(high, mat_low_ref[...], preferred_element_type=F32)
            y = y.reshape(32, 8, 640)
            c_own[t, pl.ds(base, 32), :, :] = y[:, :, 0:128]
            c_xu[t, pl.ds(base + 8, 32), :, :] = y[:, :, 128:256]
            c_xd[t, pl.ds(base, 32), :, :] = y[:, :, 256:384]
            c_yu[t, pl.ds(base, 32), :, :] = y[:, :, 384:512]
            c_yd[t, pl.ds(base, 32), :, :] = y[:, :, 512:640]
            return carry

        lax.fori_loop(0, 2 * n_tiles, body, 0)

    def project(f_ref):
        def body(i, carry):
            found = []
            for u in range(8):
                ii = i * 8 + u
                w = f_ref[lists[SRC, ii], pl.ds(lists[ROW, ii], 8), :]
                w = jnp.where(low == (lists[UPPER, ii] == 0), w, 0.0)
                found.append(jnp.sum(tiles_ref[lists[ID, ii]] * w[None], axis=1))
            q = jnp.concatenate(found, axis=0)
            high = q.astype(BF16)
            rest = (q - high.astype(F32)).astype(BF16)
            weights[pl.ds(pl.multiple_of(i * 32, 32), 32), :] = jnp.dot(
                jnp.concatenate([high, rest], axis=1), ones_ref[...], preferred_element_type=F32
            )
            return carry

        lax.fori_loop(0, (count + 7) // 8, body, 0)

    def combine(f_ref, y_ref, older, t, coef):
        a, b = coef
        r = t * 8 + 8

        def body(xb, carry):
            for yb in range(8):
                src = xb * 8 + yb
                total = c_own[t, src] + c_xu[t, src] + c_xd[t, src + 8]
                if yb > 0:
                    total = total + c_yu[t, src - 1]
                if yb < 7:
                    total = total + c_yd[t, src + 1]
                for k in range(1, REACH + 1):
                    total = total + HALF[k] * (
                        f_ref[src, r + k : r + k + 8, :] + f_ref[src, r - k : r - k + 8, :]
                    )
                total = total + pot_ref[src, t * 8 : t * 8 + 8, :] * f_ref[src, r : r + 8, :]
                total = a * total
                if older is not None:
                    total = total - b * older(src)
                if t == 0:
                    total = jnp.where(jnp.logical_or(below, jnp.logical_not(low)), total, 0.0)
                if t == 2:
                    total = jnp.where(jnp.logical_or(above, low), total, 0.0)
                y_ref[src, r : r + 8, :] = total
            return carry

        lax.fori_loop(0, 8, body, 0)

    def spread(y_ref, a):
        def body(i, carry):
            w = weights[pl.ds(pl.multiple_of(i * 32, 32), 32), :]
            for u in range(8):
                ii = i * 8 + u
                atom, src = lists[ID, ii], lists[SRC, ii]
                t = zero8
                for p in range(4):
                    t = t + (strength[p, ii] * a) * w[u * 4 + p : u * 4 + p + 1, :] * tiles_ref[atom, p]
                rows = pl.ds(lists[ROW_L, ii], 8)
                on = jnp.logical_and(low, lists[ON_L, ii] > 0)
                y_ref[src, rows, :] = y_ref[src, rows, :] + jnp.where(on, t, 0.0)
                rows = pl.ds(lists[ROW_U, ii], 8)
                on = jnp.logical_and(jnp.logical_not(low), lists[ON_U, ii] > 0)
                y_ref[src, rows, :] = y_ref[src, rows, :] + jnp.where(on, t, 0.0)
            return carry

        lax.fori_loop(0, (count + 7) // 8, body, 0)

    products(ext, 0, 3)
    project(ext)
    for t in range(3):
        older = None if first else (lambda src, t=t: older_ref[src, t * 8 : t * 8 + 8, :])
        combine(ext, mid, older, t, coef1)
    spread(mid, coef1[0])
    products(mid, 1, 1)
    project(mid)
    combine(mid, new, lambda src: ext[src, 16:24, :], 1, coef2)
    spread(new, coef2[0])
    out_ref[...] = new[:, 16:24, :]
    if not last:
        mid_ref[...] = mid[:, 8:32, :]


def double_step(first, last, coef1, coef2, lists, strength, halo, own, older, pot, tiles, mats):
    smem = pl.BlockSpec(memory_space=pltpu.SMEM)
    vmem = pl.BlockSpec(memory_space=pltpu.VMEM)
    ins = [lists, strength, halo[0], own, halo[1]]
    if not first:
        ins += [older, pot]
    ins += [tiles, *mats]
    outs = [jax.ShapeDtypeStruct((64, 8, 128), F32)]
    if first:
        outs.append(jax.ShapeDtypeStruct((64, 24, 128), F32))
    if not last:
        outs.append(jax.ShapeDtypeStruct((64, 24, 128), F32))
    return pl.pallas_call(
        functools.partial(double_kernel, first, last, coef1, coef2),
        out_shape=tuple(outs),
        in_specs=[smem, smem] + [vmem] * (len(ins) - 2),
        out_specs=tuple([vmem] * len(outs)),
        scratch_shapes=[
            pltpu.VMEM((64, 40, 128), F32),
            pltpu.VMEM((64, 40, 128), F32),
            pltpu.VMEM((64, 40, 128), F32),
            pltpu.VMEM((3, 64, 8, 128), F32),
            pltpu.VMEM((3, 72, 8, 128), F32),
            pltpu.VMEM((3, 72, 8, 128), F32),
            pltpu.VMEM((3, 64, 8, 128), F32),
            pltpu.VMEM((3, 64, 8, 128), F32),
            pltpu.VMEM((256, 128), F32),
        ],
        compiler_params=VMEM,
    )(*ins)


def atom_lists(slab, proj_strength, atom_block, atom_offset):
    number = jnp.arange(64, dtype=jnp.int32)
    dz = atom_offset[:, 2] - 16 * slab
    near = jnp.logical_and(dz >= -15, dz <= 23)
    before = jnp.sum(
        jnp.logical_and(near[None, :], number[None, :] < number[:, None]).astype(jnp.int32), axis=1
    )
    pick = jnp.logical_and(near[None, :], before[None, :] == number[:, None])

    def listed(values, empty):
        return jnp.sum(jnp.where(pick, values[None, :], 0), axis=1) + jnp.where(
            jnp.any(pick, axis=1), 0, empty
        )

    at = listed(dz, 0)
    valid = jnp.any(pick, axis=1)
    source = listed(jnp.clip(atom_block, 0, 63), 0)
    upper = at > 8
    meta = jnp.zeros((64,), jnp.int32).at[0].set(jnp.sum(near.astype(jnp.int32)))
    meta = meta.at[1].set(slab).at[2].set(7 - slab)
    lists = jnp.stack(
        [
            listed(number, 0),
            source,
            jnp.where(upper, at - 8, at) + 16,
            upper.astype(jnp.int32),
            jnp.clip(at, -16, 16) + 16,
            jnp.logical_and(valid, at <= 15).astype(jnp.int32),
            jnp.clip(at - 8, -16, 16) + 16,
            jnp.logical_and(valid, at >= -7).astype(jnp.int32),
            meta,
        ]
    )
    strength = jnp.sum(jnp.where(pick[None], proj_strength.T[:, None, :], 0.0), axis=2)
    return lists, strength


def unpack_kernel(in_ref, out_ref, hartree_ref):
    low = lanes_low((8, 128))

    def block(pairs):
        rows = []
        for a, b in pairs:
            rows += [jnp.where(low, a, swap(b)), jnp.where(low, swap(a), b)]
        return jnp.concatenate(rows, axis=0).T

    for q in range(4):
        out_ref[q * 128 : (q + 1) * 128, :] = block(
            [
                (in_ref[plane_index(2 * q, s), 0:8, :], in_ref[plane_index(2 * q + 1, s), 0:8, :])
                for s in range(8)
            ]
        )
    pairs = []
    for s in range(8):
        total = in_ref[plane_index(0, s), 8:16, :]
        for b in range(1, 8):
            total = total + in_ref[plane_index(b, s), 8:16, :]
        pairs.append((total, total))
    part = block(pairs)[0:64, :]
    for e in range(8):
        hartree_ref[e] = part


def unpack(slabs):
    return pl.pallas_call(
        unpack_kernel,
        out_shape=(
            jax.ShapeDtypeStruct((512, 128), F32),
            jax.ShapeDtypeStruct((8, 64, 128), F32),
        ),
        compiler_params=VMEM,
    )(slabs)


OMEGA = DAMPING / 6.0


def cell_index(shape):
    return np.indices(shape).reshape(len(shape), -1)


def placing(rows, columns, weight):
    same = np.all(rows[:, :, None] == columns[:, None, :], axis=0)
    return (weight * same).astype(jnp.bfloat16)


def level_matrices():
    yb, zh, x, y = cell_index((8, 2, 8, 8))
    fine = np.stack([zh, x // 2, yb * 4 + y // 2])
    coarse = np.stack(cell_index((2, 4, 32)))
    down0 = placing(fine, coarse, 0.5)
    up0 = placing(np.stack(cell_index((4, 32))), np.stack([x // 2, yb * 4 + y // 2]), 1.0)
    x, y = cell_index((16, 32))
    fine, coarse = np.stack([x // 2, y // 2]), np.stack(cell_index((8, 16)))
    down1, up1 = placing(fine, coarse, 0.5), placing(coarse, fine, 1.0)
    x, y = cell_index((16, 16))
    fine, coarse = np.stack([x // 2, y // 2]), np.stack(cell_index((16, 8)))
    down2, up2 = placing(fine, coarse, 0.5), placing(coarse, fine, 1.0)

    def beside(nx, ny, used):
        x, y = cell_index((nx, ny))
        dx, dy = x[None, :] - x[:, None], y[None, :] - y[:, None]
        live = np.logical_and(x[None, :] < used, x[:, None] < used)
        own = np.logical_and(np.abs(dx) + np.abs(dy) == 1, live)
        to_next = np.logical_and(dx == 1 - nx, dy == 0)
        to_last = np.logical_and(dx == nx - 1, dy == 0)
        return [m.astype(jnp.bfloat16) for m in (own, to_next, to_last)]

    def twice(m):
        return np.concatenate([m, m], axis=0)

    near1 = twice(np.concatenate(beside(4, 32, 4), axis=1))
    near2 = twice(np.concatenate(beside(8, 16, 8), axis=1))
    near3 = twice(beside(16, 8, 8)[0])
    return down0, twice(up0), down1, twice(up1), down2, twice(up2), near1, near2, near3


def xy_products(ref, r, mat_ref, couplings, t):
    c_own, c_xu, c_xd, c_yu, c_yd = couplings
    for base in (0, 32):
        x = ref[base : base + 32, r : r + 8, :].reshape(256, 128)
        y = jnp.dot(halves(x, 1), mat_ref[...], preferred_element_type=F32).reshape(32, 8, 640)
        c_own[t, base : base + 32, :, :] = y[:, :, 0:128]
        c_xu[t, base + 8 : base + 40, :, :] = y[:, :, 128:256]
        c_xd[t, base : base + 32, :, :] = y[:, :, 256:384]
        c_yu[t, base : base + 32, :, :] = y[:, :, 384:512]
        c_yd[t, base : base + 32, :, :] = y[:, :, 512:640]


def xy_sum(couplings, t, xb, yb):
    c_own, c_xu, c_xd, c_yu, c_yd = couplings
    src = xb * 8 + yb
    total = c_own[t, src] + c_xu[t, src] + c_xd[t, src + 8]
    if yb > 0:
        total = total + c_yu[t, src - 1]
    if yb < 7:
        total = total + c_yd[t, src + 1]
    return total


def clear_borders(couplings, tiles):
    zero = jnp.zeros((8, 8, 128), F32)
    for t in range(tiles):
        couplings[1][t, 0:8] = zero
        couplings[2][t, 64:72] = zero


COUPLINGS = [
    pltpu.VMEM((2, n, 8, 128), F32) for n in (64, 72, 72, 64, 64)
]


def inside_slab_range(slab, r):
    z = (
        lax.broadcasted_iota(jnp.int32, (8, 128), 0)
        + jnp.where(lanes_low((8, 128)), 0, 8)
        + (16 * slab + (r - 16))
    )
    return jnp.logical_and(z >= 0, z < 128)


def relax(ref, out_ref, rows, mat_ref, couplings, update):
    for t, r in enumerate(rows):
        xy_products(ref, r, mat_ref, couplings, t)
    for t, r in enumerate(rows):

        def body(xb, carry, t=t, r=r):
            for yb in range(8):
                src = xb * 8 + yb
                near = xy_sum(couplings, t, xb, yb)
                near = near + ref[src, r - 1 : r + 7, :] + ref[src, r + 1 : r + 9, :]
                out_ref[src, r : r + 8, :] = update(src, r, ref[src, r : r + 8, :], near)
            return carry

        lax.fori_loop(0, 8, body, 0)


def source_kernel(scalars, occ, own_ref, mat_ref, down_ref, f_ref, sent_ref, v, w, r0, *couplings):
    low = lanes_low((8, 128))
    slab, occupation = scalars[0], occ[scalars[1]] / 64.0
    zero = jnp.zeros((8, 128), F32)

    def fill(i, carry):
        for u in range(16):
            src = i * 16 + u
            y = own_ref[src]
            o = occupation * y * y
            f_ref[src] = o
            o = OMEGA * o
            v[src, 0:8, :] = zero
            v[src, 8:16, :] = swap(jnp.where(low, o, 0.0))
            v[src, 16:24, :] = o
            v[src, 24:32, :] = swap(jnp.where(low, 0.0, o))
            v[src, 32:40, :] = zero
            w[src, 8:16, :] = zero
            w[src, 24:32, :] = zero
        return carry

    lax.fori_loop(0, 4, fill, 0)
    clear_borders(couplings, 2)
    keep = {r: inside_slab_range(slab, r) for r in (13, 19)}
    relax(
        v,
        w,
        (13, 19),
        mat_ref,
        couplings,
        lambda src, r, c, near: jnp.where(keep[r], 1.2 * c + OMEGA * near, 0.0),
    )
    relax(
        w,
        r0,
        (14, 18),
        mat_ref,
        couplings,
        lambda src, r, c, near: v[src, r : r + 8, :] * (1.0 / OMEGA) - 6.0 * c + near,
    )
    rows = []
    for xb in range(8):
        parts = []
        for yb in range(8):
            src = xb * 8 + yb
            parts.append(r0[src, pl.ds(14, 8, stride=2), :] + r0[src, pl.ds(15, 8, stride=2), :])
        rows.append(jnp.concatenate(parts, axis=1))
    summed = jnp.concatenate(rows, axis=0)
    coarse = jnp.dot(halves(summed, 0), down_ref[...], preferred_element_type=F32)
    coarse = coarse[0:64] + coarse[64:128]
    below, above = [], []
    own = []
    for xb in range(8):
        part = coarse[xb * 8 : xb * 8 + 8]
        own.append(part[1:5, 0:128])
        own.append(part[1:5, 128:256])
        below.append(part[0:1, 0:128])
        above.append(part[5:6, 128:256])
    sent = jnp.concatenate(own + below + above, axis=0)
    for e in range(8):
        sent_ref[e] = sent


def source_step(scalars, occupations, own, mat, down):
    smem = pl.BlockSpec(memory_space=pltpu.SMEM)
    vmem = pl.BlockSpec(memory_space=pltpu.VMEM)
    return pl.pallas_call(
        source_kernel,
        out_shape=(
            jax.ShapeDtypeStruct((64, 8, 128), F32),
            jax.ShapeDtypeStruct((8, 80, 128), F32),
        ),
        in_specs=[smem, smem, vmem, vmem, vmem],
        out_specs=(vmem, vmem),
        scratch_shapes=[pltpu.VMEM((64, 40, 128), F32)] * 3 + COUPLINGS,
        compiler_params=VMEM,
    )(scalars, occupations, own, mat, down)


def double_rows(scratch, value, n):
    scratch[:, pl.ds(0, n, stride=2), :] = value
    scratch[:, pl.ds(1, n, stride=2), :] = value


def coarse_solve(g, v, r1, v2, r2, v3, r3, mats):
    down1, up1, down2, up2, near1, near2, near3 = mats

    def near(ref, blocks, planes, mat):
        rows = ref[:, 8 : 8 + planes, :]
        y = jnp.dot(
            halves(rows.reshape(blocks * planes, 128), 1), mat[...], preferred_element_type=F32
        )
        y = y.reshape(blocks, planes, -1)
        total = y[:, :, 0:128] + ref[:, 7 : 7 + planes, :] + ref[:, 9 : 9 + planes, :]
        if blocks > 1:
            none = jnp.zeros((1, planes, 128), F32)
            total = total + jnp.concatenate([none, y[:-1, :, 128:256]], axis=0)
            total = total + jnp.concatenate([y[1:, :, 256:384], none], axis=0)
        return rows, total

    def sweep(ref, source, blocks, planes, mat):
        rows, total = near(ref, blocks, planes, mat)
        ref[:, 8 : 8 + planes, :] = rows + OMEGA * (source() - 6.0 * rows + total)

    def residual(ref, source, blocks, planes, mat):
        rows, total = near(ref, blocks, planes, mat)
        return source() - 6.0 * rows + total

    for ref, planes in ((v, 64), (v2, 32), (v3, 16)):
        border = jnp.zeros((ref.shape[0], 8, 128), F32)
        ref[:, 0:8, :] = border
        ref[:, 8 + planes : 16 + planes, :] = border
    g1 = lambda: g[:, 8:72, :]
    v[:, 8:72, :] = OMEGA * g1()
    sweep(v, g1, 8, 64, near1)
    r1[...] = residual(v, g1, 8, 64, near1)
    pair = r1[:, pl.ds(0, 32, stride=2), :] + r1[:, pl.ds(1, 32, stride=2), :]
    rows = [jnp.concatenate([pair[4 * b + e] for e in range(4)], axis=1) for b in range(2)]
    d = jnp.dot(halves(jnp.concatenate(rows, axis=0), 0), down1[...], preferred_element_type=F32)
    s2 = (d[0:64] + d[64:128]).reshape(2, 32, 128)
    g2 = lambda: s2
    v2[:, 8:40, :] = OMEGA * s2
    sweep(v2, g2, 2, 32, near2)
    r2[...] = residual(v2, g2, 2, 32, near2)
    pair = r2[:, pl.ds(0, 16, stride=2), :] + r2[:, pl.ds(1, 16, stride=2), :]
    both = jnp.concatenate([pair[0], pair[1]], axis=1)
    d = jnp.dot(halves(both, 0), down2[...], preferred_element_type=F32)
    s3 = (d[0:16] + d[16:32]).reshape(1, 16, 128)
    g3 = lambda: s3
    v3[:, 8:24, :] = OMEGA * s3
    for _ in range(COARSE - 1):
        sweep(v3, g3, 1, 16, near3)
    double_rows(r3, v3[:, 8:24, :], 16)
    up = jnp.dot(halves(r3[0], 1), up2[...], preferred_element_type=F32)
    for b in range(2):
        v2[b, 8:40, :] = v2[b, 8:40, :] + up[:, b * 128 : b * 128 + 128]
    for _ in range(POST):
        sweep(v2, g2, 2, 32, near2)
    double_rows(r1.at[0:2], v2[:, 8:40, :], 32)
    up = jnp.dot(halves(r1[0:2].reshape(128, 128), 1), up1[...], preferred_element_type=F32)
    for b in range(8):
        part = up[(b // 4) * 64 : (b // 4) * 64 + 64, (b % 4) * 128 : (b % 4) * 128 + 128]
        v[b, 8:72, :] = v[b, 8:72, :] + part
    for _ in range(POST):
        sweep(v, g1, 8, 64, near1)


def finish_kernel(scalars, got_ref, prev_ref, f_ref, next_ref, y_ref, mat_ref, up_ref, *refs):
    refs = list(refs)
    mats, out_ref, refs = refs[:7], refs[7], refs[8:]
    fx, va, vb, up, g, v, r1, v2, r2, v3, r3, wide = refs[:12]
    couplings = refs[12:]
    low = lanes_low((8, 128))
    slab = scalars[0]

    for s in range(8):
        g[:, 8 + 8 * s : 16 + 8 * s, :] = got_ref[SLAB_DEVICE[s], 0:64, :].reshape(8, 8, 128)
    for s in range(8):
        for xb in range(8):
            if s > 0:
                row = 8 + 8 * s - 1
                g[xb, row : row + 1, :] = g[xb, row : row + 1, :] + got_ref[SLAB_DEVICE[s], 64 + xb : 65 + xb, :]
            if s < 7:
                row = 8 + 8 * s + 8
                g[xb, row : row + 1, :] = g[xb, row : row + 1, :] + got_ref[SLAB_DEVICE[s], 72 + xb : 73 + xb, :]
    coarse_solve(g, v, r1, v2, r2, v3, r3, mats)
    double_rows(wide, v[:, pl.ds(8 * slab + 4, 16), :], 16)
    up[...] = jnp.dot(
        halves(wide[...].reshape(256, 128), 1), up_ref[...], preferred_element_type=F32
    ).reshape(8, 32, 1024)

    def fill(i, carry):
        for u in range(16):
            src = i * 16 + u
            p, o, n = prev_ref[src], f_ref[src], next_ref[src]
            fx[src, 8:16, :] = OMEGA * swap(jnp.where(low, o, p))
            fx[src, 16:24, :] = OMEGA * o
            fx[src, 24:32, :] = OMEGA * swap(jnp.where(low, n, o))
        return carry

    lax.fori_loop(0, 4, fill, 0)
    clear_borders(couplings, 2)
    keep = {r: inside_slab_range(slab, r) for r in (14, 18, 15, 17)}

    def to_third(src, r, c, near):
        return jnp.where(keep[r], 1.2 * c + OMEGA * near, 0.0)

    relax(fx, va, (14, 18), mat_ref, couplings, to_third)

    def add_up(xb, carry):
        for yb in range(8):
            src = xb * 8 + yb
            for r in (14, 22):
                n = 8 if r == 14 else 4
                e = jnp.where(
                    lanes_low((n, 128)),
                    up[xb, r - 8 : r - 8 + n, yb * 128 : yb * 128 + 128],
                    up[xb, r : r + n, yb * 128 : yb * 128 + 128],
                )
                va[src, r : r + n, :] = va[src, r : r + n, :] + e
        return carry

    lax.fori_loop(0, 8, add_up, 0)

    def swept(src, r, c, near):
        return c + (fx[src, r : r + 8, :] - DAMPING * c + OMEGA * near)

    relax(
        va,
        vb,
        (15, 17),
        mat_ref,
        couplings,
        lambda src, r, c, near: jnp.where(keep[r], swept(src, r, c, near), 0.0),
    )
    relax(vb, va, (16,), mat_ref, couplings, swept)
    out_ref[:, 0:8, :] = y_ref[...]
    out_ref[:, 8:16, :] = va[:, 16:24, :]


def finish_step(scalars, got, halo, f, own, mat, levels):
    smem = pl.BlockSpec(memory_space=pltpu.SMEM)
    vmem = pl.BlockSpec(memory_space=pltpu.VMEM)
    ins = [scalars, got, halo[0], f, halo[1], own, mat, levels[1], *levels[2:]]
    big = pltpu.VMEM((64, 40, 128), F32)
    return pl.pallas_call(
        finish_kernel,
        out_shape=jax.ShapeDtypeStruct((64, 16, 128), F32),
        in_specs=[smem] + [vmem] * (len(ins) - 1),
        out_specs=vmem,
        scratch_shapes=[
            big,
            big,
            big,
            pltpu.VMEM((8, 32, 1024), F32),
            pltpu.VMEM((8, 80, 128), F32),
            pltpu.VMEM((8, 80, 128), F32),
            pltpu.VMEM((8, 64, 128), F32),
            pltpu.VMEM((2, 48, 128), F32),
            pltpu.VMEM((2, 32, 128), F32),
            pltpu.VMEM((1, 32, 128), F32),
            pltpu.VMEM((1, 32, 128), F32),
            pltpu.VMEM((8, 32, 128), F32),
        ]
        + COUPLINGS,
        compiler_params=VMEM,
    )(*ins)


def exchange(value, axes, dim, width, order=None):
    order = order or list(range(8))
    up = [(order[i], order[i + 1]) for i in range(7)]
    down = [(j, i) for i, j in up]
    length = value.shape[dim]
    before = lax.ppermute(lax.slice_in_dim(value, length - width, length, axis=dim), axes, up)
    after = lax.ppermute(lax.slice_in_dim(value, 0, width, axis=dim), axes, down)
    return before, after


def local(
    orbitals, local_potential, occupations, proj_values, proj_strength, atom_block, atom_offset
):
    core, xlo, ylo = (lax.axis_index(a) for a in GROUP)
    slab = 2 * (xlo * (3 - ylo) + (1 - xlo) * ylo) + core
    lists, strength = atom_lists(slab, proj_strength, atom_block, atom_offset)
    high, low = coupling(HALF)
    mats = (jnp.asarray(high), jnp.asarray(low), jnp.ones((256, 128), BF16))

    packed, tiles = pack(orbitals, local_potential, proj_values)
    own = lax.all_to_all(packed, PLANE, 0, 0, tiled=True)

    sigma = HALF_WIDTH / (0.0 - CENTER)
    tau = 2.0 / sigma
    coefs = [(sigma / HALF_WIDTH, 0.0)]
    for _ in range(DEGREE - 1):
        following = 1.0 / (tau - sigma)
        coefs.append((2.0 * following / HALF_WIDTH, sigma * following))
        sigma = following
    older = pot = None
    for k in range(0, DEGREE, 2):
        first, last = k == 0, k == DEGREE - 2
        halo = exchange(own, GROUP, 1, own.shape[1], SLAB_DEVICE)
        outs = list(
            double_step(
                first, last, coefs[k], coefs[k + 1], lists, strength, halo, own, older, pot, tiles, mats
            )
        )
        own = outs.pop(0)
        if first:
            pot = outs.pop(0)
        if not last:
            older = outs.pop(0)

    scalars = jnp.stack([slab, 2 * lax.axis_index("yhi") + lax.axis_index("xhi")]).astype(jnp.int32)
    near, _ = coupling((0.0, 1.0))
    near = jnp.asarray(near)
    levels = [jnp.asarray(m) for m in level_matrices()]
    f, sent = source_step(scalars, occupations, own, near, levels[0])
    halo = exchange(f, GROUP, 1, 8, SLAB_DEVICE)
    got = lax.all_to_all(sent, GROUP, 0, 0, tiled=True)
    packed = finish_step(scalars, got, halo, f, own, near, levels)
    back = lax.all_to_all(packed, PLANE, 0, 0, tiled=True)
    filtered, part = unpack(back)
    hartree = jnp.sum(lax.all_to_all(part, BAND, 0, 0, tiled=True), axis=0)
    return filtered.reshape(8, 8, 8, 128), hartree.reshape(8, 8, 128)


def solution(mesh):
    fine = Mesh(
        mesh.devices.reshape(8, 4, 2, 2, 2, 2), (BAND, "yhi", "core", "xhi", "xlo", "ylo")
    )
    bands, grid = P(BAND, GX, GYZ, None), P(GX, GYZ, None)
    return jax.shard_map(
        local,
        mesh=fine,
        in_specs=(bands, grid, P(BAND), P(), P(), P(), P()),
        out_specs=(bands, grid),
        check_vma=False,
    )
```

```python
import functools

import jax
import jax.numpy as jnp
import numpy as np
from jax import lax
from jax.experimental import pallas as pl
from jax.experimental.pallas import tpu as pltpu
from jax.sharding import Mesh
from jax.sharding import PartitionSpec as P

DEGREE = 8
POST = 2
COARSE = 4
STENCIL = (
    -5369.0 / 1800.0,
    12.0 / 7.0,
    -15.0 / 56.0,
    10.0 / 189.0,
    -1.0 / 112.0,
    2.0 / 1925.0,
    -1.0 / 16632.0,
)
HALF = tuple(-0.5 * c for c in STENCIL)
REACH = 6
CENTER = 12.0
HALF_WIDTH = 8.0
DAMPING = 0.8
BAND = "z"
GX = ("yhi", "core")
GYZ = ("xhi", "xlo", "ylo")
PLANE = GX + GYZ
GROUP = ("core", "xlo", "ylo")
CHIPS = ((0, 0), (0, 1), (1, 1), (1, 0))
SLAB_DEVICE = [c * 4 + xl * 2 + yl for xl, yl in CHIPS for c in (0, 1)]
VMEM = pltpu.CompilerParams(vmem_limit_bytes=12 * 1024 * 1024)
FILL = 16
HEAD = 3
F32 = jnp.float32
BF16 = jnp.bfloat16


def plane_index(band, slab):
    yhi, xhi = band // 2, band % 2
    xlo, ylo = CHIPS[slab // 2]
    return yhi * 16 + (slab % 2) * 8 + xhi * 4 + xlo * 2 + ylo


def coupling(weights):
    own, xu, xd, yu, yd = (np.zeros((128, 128)) for _ in range(5))
    for zh in range(2):
        for xi in range(8):
            for yi in range(8):
                i = zh * 64 + xi * 8 + yi
                for o in range(8):
                    for m, k in ((own, abs(o - xi)), (xu, o + 8 - xi), (xd, xi + 8 - o)):
                        if 1 <= k < len(weights):
                            m[i, zh * 64 + o * 8 + yi] += weights[k]
                    for m, k in ((own, abs(o - yi)), (yu, o + 8 - yi), (yd, yi + 8 - o)):
                        if 1 <= k < len(weights):
                            m[i, zh * 64 + xi * 8 + o] += weights[k]
    whole = np.concatenate([own, xu, xd, yu, yd], axis=1).astype(np.float32)
    high = whole.astype(jnp.bfloat16)
    low = (whole - high.astype(np.float32)).astype(jnp.bfloat16)
    return high, low


def halves(x, axis):
    high = x.astype(BF16)
    return jnp.concatenate([high, (x - high.astype(F32)).astype(BF16)], axis=axis)


def lanes_low(shape):
    return lax.broadcasted_iota(jnp.int32, shape, len(shape) - 1) < 64


def dot2(x, m):
    return jnp.dot(halves(x, 1), jnp.concatenate([m, m], axis=0), preferred_element_type=F32)


def swap(x):
    return pltpu.roll(x, 64, x.ndim - 1)


def split3(x):
    a = x.astype(BF16)
    r = x - a.astype(F32)
    b = r.astype(BF16)
    c = (r - b.astype(F32)).astype(BF16)
    return a, b, c


def pack_kernel(orb_ref, pot_ref, out_ref):
    low = lanes_low((8, 128))
    for q in range(4):
        turned = orb_ref[q * 128 : (q + 1) * 128, :].T
        for s in range(8):
            a = turned[s * 16 : s * 16 + 8, :]
            b = turned[s * 16 + 8 : s * 16 + 16, :]
            out_ref[plane_index(2 * q, s), 0:8, :] = jnp.where(low, a, swap(b))
            out_ref[plane_index(2 * q + 1, s), 0:8, :] = jnp.where(low, swap(a), b)
    pot = pot_ref[...]
    turned = jnp.concatenate([pot, pot], axis=0).T
    for s in range(8):
        piece = jnp.where(low, turned[s * 16 : s * 16 + 8, :], turned[s * 16 + 8 : s * 16 + 16, :])
        for b in range(8):
            out_ref[plane_index(b, s), 8:16, :] = piece


def pack(orbitals, potential):
    return pl.pallas_call(
        pack_kernel,
        out_shape=jax.ShapeDtypeStruct((64, 16, 128), F32),
        compiler_params=VMEM,
    )(orbitals.reshape(512, 128), potential.reshape(64, 128))


def tiles_kernel(proj_ref, pick_ref, tiles_ref):
    keep = lax.broadcasted_iota(jnp.int32, (4, 8, 512), 2) % 8 == lax.broadcasted_iota(
        jnp.int32, (4, 8, 512), 1
    )

    def body(i, carry):
        parts = [
            jnp.where(keep, proj_ref[i * 8 + u][:, None, :], 0.0).reshape(32, 512)
            for u in range(8)
        ]
        spread = jnp.concatenate(parts, axis=0)
        pick = pick_ref[...]
        total = sum(jnp.dot(part, pick, preferred_element_type=F32) for part in split3(spread))
        tiles_ref[pl.ds(i * 8, 8), :, :, :] = total.reshape(8, 4, 8, 128)
        return carry

    lax.fori_loop(0, 8, body, 0)


def projector_tiles(proj):
    pick = (np.arange(512)[:, None] // 8 == np.arange(128)[None, :] % 64).astype(jnp.bfloat16)
    return pl.pallas_call(
        tiles_kernel,
        out_shape=jax.ShapeDtypeStruct((64, 4, 8, 128), F32),
        compiler_params=VMEM,
    )(proj, pick)


ID, SRC, ROW, UPPER, ROW_L, ON_L, ROW_U, ON_U, META = range(9)


def double_kernel(
    first, last, coef1, coef2, lists, strength, prev_ref, own_ref, next_ref, *refs
):
    refs = list(refs)
    if first:
        older_ref = pot_ref = None
    else:
        older_ref, pot_ref = refs.pop(0), refs.pop(0)
    tiles_ref, mat_ref, mat_low_ref = refs[:3]
    refs = refs[3:]
    out_ref = refs.pop(0)
    if first:
        pot_ref = refs.pop(0)
    mid_ref = None if last else refs.pop(0)
    ext, mid, new, c_own, c_xu, c_xd, c_yu, c_yd, weights = refs
    low = lanes_low((8, 128))
    count = lists[META, 0]
    below = lists[META, 1] > 0
    above = lists[META, 2] > 0
    zero8 = jnp.zeros((8, 128), F32)

    def fill(i, carry):
        for u in range(FILL):
            src = i * FILL + u
            p, o, n = prev_ref[src, 0:8, :], own_ref[src, 0:8, :], next_ref[src, 0:8, :]
            ext[src, 0:8, :] = p
            ext[src, 8:16, :] = swap(jnp.where(low, o, p))
            ext[src, 16:24, :] = o
            ext[src, 24:32, :] = swap(jnp.where(low, n, o))
            ext[src, 32:40, :] = n
            if first:
                p, o, n = prev_ref[src, 8:16, :], own_ref[src, 8:16, :], next_ref[src, 8:16, :]
                shift = 3.0 * HALF[0] - CENTER
                pot_ref[src, 0:8, :] = swap(jnp.where(low, o, p)) + shift
                pot_ref[src, 8:16, :] = o + shift
                pot_ref[src, 16:24, :] = swap(jnp.where(low, n, o)) + shift
        return carry

    lax.fori_loop(0, 64 // FILL, fill, 0)
    for t in range(3):
        for e in range(8):
            c_xu[t, e, :, :] = zero8
            c_xd[t, 64 + e, :, :] = zero8

    def products(f_ref, tiles):
        for t in tiles:
            x = f_ref[:, t * 8 + 8 : t * 8 + 16, :].reshape(512, 128)
            both = halves(x, 1)
            m = mat_ref[...]
            y = jnp.dot(both, jnp.concatenate([m, m], axis=0), preferred_element_type=F32)
            y = y + jnp.dot(both[:, 0:128], mat_low_ref[...], preferred_element_type=F32)
            y = y.reshape(64, 8, 640)
            c_own[t, :, :, :] = y[:, :, 0:128]
            c_xu[t, 8:72, :, :] = y[:, :, 128:256]
            c_xd[t, 0:64, :, :] = y[:, :, 256:384]
            c_yu[t, :, :, :] = y[:, :, 384:512]
            c_yd[t, :, :, :] = y[:, :, 512:640]

    def project(f_ref):
        def chunk(i):
            found = []
            for u in range(8):
                ii = i * 8 + u
                w = f_ref[lists[SRC, ii], pl.ds(lists[ROW, ii], 8), :]
                w = jnp.where(low == (lists[UPPER, ii] == 0), w, 0.0)
                found.append(jnp.sum(tiles_ref[lists[ID, ii]] * w[None], axis=1))
            return jnp.concatenate(found, axis=0)

        def summed(q):
            return dot2(q, jnp.ones((128, 128), BF16))

        head = jnp.concatenate([chunk(i) for i in range(HEAD)], axis=0)
        weights[0 : HEAD * 32, :] = summed(head)

        def body(i, carry):
            weights[pl.ds(pl.multiple_of(i * 32, 32), 32), :] = summed(chunk(i))
            return carry

        lax.fori_loop(HEAD, (count + 7) // 8, body, 0)

    def combine(f_ref, y_ref, older, t, coef):
        a, b = coef
        r = t * 8 + 8

        def body(xb, carry):
            for yb in range(8):
                src = xb * 8 + yb
                total = c_own[t, src] + c_xu[t, src] + c_xd[t, src + 8]
                if yb > 0:
                    total = total + c_yu[t, src - 1]
                if yb < 7:
                    total = total + c_yd[t, src + 1]
                for k in range(1, REACH + 1):
                    total = total + HALF[k] * (
                        f_ref[src, r + k : r + k + 8, :] + f_ref[src, r - k : r - k + 8, :]
                    )
                total = total + pot_ref[src, t * 8 : t * 8 + 8, :] * f_ref[src, r : r + 8, :]
                total = a * total
                if older is not None:
                    total = total - b * older(src)
                if t == 0:
                    total = jnp.where(jnp.logical_or(below, jnp.logical_not(low)), total, 0.0)
                if t == 2:
                    total = jnp.where(jnp.logical_or(above, low), total, 0.0)
                y_ref[src, r : r + 8, :] = total
            return carry

        lax.fori_loop(0, 8, body, 0)

    def spread(y_ref, a):
        def term(i, u, w):
            ii = i * 8 + u
            atom = lists[ID, ii]
            t = zero8
            for p in range(4):
                t = t + (strength[p, ii] * a) * w[u * 4 + p : u * 4 + p + 1, :] * tiles_ref[atom, p]
            return t

        def add(i, u, t):
            ii = i * 8 + u
            src = lists[SRC, ii]
            rows = pl.ds(lists[ROW_L, ii], 8)
            on = jnp.logical_and(low, lists[ON_L, ii] > 0)
            y_ref[src, rows, :] = y_ref[src, rows, :] + jnp.where(on, t, 0.0)
            rows = pl.ds(lists[ROW_U, ii], 8)
            on = jnp.logical_and(jnp.logical_not(low), lists[ON_U, ii] > 0)
            y_ref[src, rows, :] = y_ref[src, rows, :] + jnp.where(on, t, 0.0)

        for i in range(HEAD):
            w = weights[i * 32 : i * 32 + 32, :]
            terms = [term(i, u, w) for u in range(8)]
            for u in range(8):
                add(i, u, terms[u])

        def body(i, carry):
            w = weights[pl.ds(pl.multiple_of(i * 32, 32), 32), :]
            terms = [term(i, u, w) for u in range(8)]
            for u in range(8):
                add(i, u, terms[u])
            return carry

        lax.fori_loop(HEAD, (count + 7) // 8, body, 0)

    products(ext, range(3))
    project(ext)
    for t in range(3):
        older = None if first else (lambda src, t=t: older_ref[src, t * 8 : t * 8 + 8, :])
        combine(ext, mid, older, t, coef1)
    spread(mid, coef1[0])
    products(mid, (1,))
    project(mid)
    combine(mid, new, lambda src: ext[src, 16:24, :], 1, coef2)
    spread(new, coef2[0])
    out_ref[...] = new[:, 16:24, :]
    if not last:
        mid_ref[...] = mid[:, 8:32, :]


def double_step(first, last, coef1, coef2, lists, strength, halo, own, older, pot, tiles, mats):
    smem = pl.BlockSpec(memory_space=pltpu.SMEM)
    vmem = pl.BlockSpec(memory_space=pltpu.VMEM)
    ins = [lists, strength, halo[0], own, halo[1]]
    if not first:
        ins += [older, pot]
    ins += [tiles, *mats]
    outs = [jax.ShapeDtypeStruct((64, 8, 128), F32)]
    if first:
        outs.append(jax.ShapeDtypeStruct((64, 24, 128), F32))
    if not last:
        outs.append(jax.ShapeDtypeStruct((64, 24, 128), F32))
    return pl.pallas_call(
        functools.partial(double_kernel, first, last, coef1, coef2),
        out_shape=tuple(outs),
        in_specs=[smem, smem] + [vmem] * (len(ins) - 2),
        out_specs=tuple([vmem] * len(outs)),
        scratch_shapes=[
            pltpu.VMEM((64, 40, 128), F32),
            pltpu.VMEM((64, 40, 128), F32),
            pltpu.VMEM((64, 40, 128), F32),
            pltpu.VMEM((3, 64, 8, 128), F32),
            pltpu.VMEM((3, 72, 8, 128), F32),
            pltpu.VMEM((3, 72, 8, 128), F32),
            pltpu.VMEM((3, 64, 8, 128), F32),
            pltpu.VMEM((3, 64, 8, 128), F32),
            pltpu.VMEM((256, 128), F32),
        ],
        compiler_params=VMEM,
    )(*ins)


def atom_lists(slab, proj_strength, atom_block, atom_offset):
    number = jnp.arange(64, dtype=jnp.int32)
    dz = atom_offset[:, 2] - 16 * slab
    near = jnp.logical_and(dz >= -15, dz <= 23)
    before = jnp.sum(
        jnp.logical_and(near[None, :], number[None, :] < number[:, None]).astype(jnp.int32), axis=1
    )
    pick = jnp.logical_and(near[None, :], before[None, :] == number[:, None])

    def listed(values, empty):
        return jnp.sum(jnp.where(pick, values[None, :], 0), axis=1) + jnp.where(
            jnp.any(pick, axis=1), 0, empty
        )

    at = listed(dz, 0)
    valid = jnp.any(pick, axis=1)
    source = listed(jnp.clip(atom_block, 0, 63), 0)
    upper = at > 8
    meta = jnp.zeros((64,), jnp.int32).at[0].set(jnp.sum(near.astype(jnp.int32)))
    meta = meta.at[1].set(slab).at[2].set(7 - slab)
    lists = jnp.stack(
        [
            listed(number, 0),
            source,
            jnp.where(upper, at - 8, at) + 16,
            upper.astype(jnp.int32),
            jnp.clip(at, -16, 16) + 16,
            jnp.logical_and(valid, at <= 15).astype(jnp.int32),
            jnp.clip(at - 8, -16, 16) + 16,
            jnp.logical_and(valid, at >= -7).astype(jnp.int32),
            meta,
        ]
    )
    strength = jnp.sum(jnp.where(pick[None], proj_strength.T[:, None, :], 0.0), axis=2)
    return lists, strength


def unpack_kernel(in_ref, out_ref, hartree_ref):
    low = lanes_low((8, 128))

    def block(pairs):
        rows = []
        for a, b in pairs:
            rows += [jnp.where(low, a, swap(b)), jnp.where(low, swap(a), b)]
        return jnp.concatenate(rows, axis=0).T

    for q in range(4):
        out_ref[q * 128 : (q + 1) * 128, :] = block(
            [
                (in_ref[plane_index(2 * q, s), 0:8, :], in_ref[plane_index(2 * q + 1, s), 0:8, :])
                for s in range(8)
            ]
        )
    pairs = []
    for s in range(8):
        total = in_ref[plane_index(0, s), 8:16, :]
        for b in range(1, 8):
            total = total + in_ref[plane_index(b, s), 8:16, :]
        pairs.append((total, total))
    part = block(pairs)[0:64, :]
    for e in range(8):
        hartree_ref[e] = part


def unpack(slabs):
    return pl.pallas_call(
        unpack_kernel,
        out_shape=(
            jax.ShapeDtypeStruct((512, 128), F32),
            jax.ShapeDtypeStruct((8, 64, 128), F32),
        ),
        compiler_params=VMEM,
    )(slabs)


OMEGA = DAMPING / 6.0


def cell_index(shape):
    return np.indices(shape).reshape(len(shape), -1)


def placing(rows, columns, weight):
    same = np.all(rows[:, :, None] == columns[:, None, :], axis=0)
    return (weight * same).astype(jnp.bfloat16)


def level_matrices():
    x, y = cell_index((16, 32))
    fine, coarse = np.stack([x // 2, y // 2]), np.stack(cell_index((8, 16)))
    down1, up1 = placing(fine, coarse, 0.5), placing(coarse, fine, 1.0)
    x, y = cell_index((16, 16))
    fine, coarse = np.stack([x // 2, y // 2]), np.stack(cell_index((16, 8)))
    down2, up2 = placing(fine, coarse, 0.5), placing(coarse, fine, 1.0)

    def beside(nx, ny, used):
        x, y = cell_index((nx, ny))
        dx, dy = x[None, :] - x[:, None], y[None, :] - y[:, None]
        live = np.logical_and(x[None, :] < used, x[:, None] < used)
        own = np.logical_and(np.abs(dx) + np.abs(dy) == 1, live)
        to_next = np.logical_and(dx == 1 - nx, dy == 0)
        to_last = np.logical_and(dx == nx - 1, dy == 0)
        return [m.astype(jnp.bfloat16) for m in (own, to_next, to_last)]

    near1 = np.concatenate(beside(4, 32, 4), axis=1)
    near2 = np.concatenate(beside(8, 16, 8), axis=1)
    near3 = beside(16, 8, 8)[0]
    return down1, up1, down2, up2, near1, near2, near3


def xy_products(ref, r, mat_ref, couplings, t):
    c_own, c_xu, c_xd, c_yu, c_yd = couplings
    x = ref[:, r : r + 8, :].reshape(512, 128)
    y = dot2(x, mat_ref[...]).reshape(64, 8, 640)
    c_own[t, :, :, :] = y[:, :, 0:128]
    c_xu[t, 8:72, :, :] = y[:, :, 128:256]
    c_xd[t, 0:64, :, :] = y[:, :, 256:384]
    c_yu[t, :, :, :] = y[:, :, 384:512]
    c_yd[t, :, :, :] = y[:, :, 512:640]


def xy_sum(couplings, t, xb, yb):
    c_own, c_xu, c_xd, c_yu, c_yd = couplings
    src = xb * 8 + yb
    total = c_own[t, src] + c_xu[t, src] + c_xd[t, src + 8]
    if yb > 0:
        total = total + c_yu[t, src - 1]
    if yb < 7:
        total = total + c_yd[t, src + 1]
    return total


def clear_borders(couplings, tiles):
    zero = jnp.zeros((8, 8, 128), F32)
    for t in range(tiles):
        couplings[1][t, 0:8] = zero
        couplings[2][t, 64:72] = zero


COUPLINGS = [
    pltpu.VMEM((2, n, 8, 128), F32) for n in (64, 72, 72, 64, 64)
]


def inside_slab_range(slab, r):
    z = (
        lax.broadcasted_iota(jnp.int32, (8, 128), 0)
        + jnp.where(lanes_low((8, 128)), 0, 8)
        + (16 * slab + (r - 16))
    )
    return jnp.logical_and(z >= 0, z < 128)


def relax(ref, rows, mat_ref, couplings, update):
    for t, r in enumerate(rows):
        xy_products(ref, r, mat_ref, couplings, t)
    for t, r in enumerate(rows):

        def body(xb, carry, t=t, r=r):
            for yb in range(8):
                src = xb * 8 + yb
                near = xy_sum(couplings, t, xb, yb)
                near = near + ref[src, r - 1 : r + 7, :] + ref[src, r + 1 : r + 9, :]
                update(src, r, ref[src, r : r + 8, :], near)
            return carry

        lax.fori_loop(0, 8, body, 0)


def source_kernel(scalars, occ, own_ref, mat_ref, sent_ref, v, w, r0, *couplings):
    low = lanes_low((8, 128))
    slab, occupation = scalars[0], occ[scalars[1]] / 64.0
    zero = jnp.zeros((8, 128), F32)

    def fill(i, carry):
        for u in range(16):
            src = i * 16 + u
            y = own_ref[src]
            o = OMEGA * (occupation * y * y)
            v[src, 0:8, :] = zero
            v[src, 8:16, :] = swap(jnp.where(low, o, 0.0))
            v[src, 16:24, :] = o
            v[src, 24:32, :] = swap(jnp.where(low, 0.0, o))
            v[src, 32:40, :] = zero
            w[src, 8:16, :] = zero
            w[src, 24:32, :] = zero
        return carry

    lax.fori_loop(0, 4, fill, 0)
    clear_borders(couplings, 2)
    keep = {r: inside_slab_range(slab, r) for r in (13, 19)}

    def second(src, r, c, near):
        w[src, r : r + 8, :] = jnp.where(keep[r], 1.2 * c + OMEGA * near, 0.0)

    def residual(src, r, c, near):
        r0[src, r : r + 8, :] = v[src, r : r + 8, :] * (1.0 / OMEGA) - 6.0 * c + near

    relax(v, (13, 19), mat_ref, couplings, second)
    relax(w, (14, 18), mat_ref, couplings, residual)
    rows = []
    for xb in range(8):
        parts = []
        for yb in range(8):
            src = xb * 8 + yb
            parts.append(r0[src, pl.ds(14, 8, stride=2), :] + r0[src, pl.ds(15, 8, stride=2), :])
        rows.append(jnp.concatenate(parts, axis=1))
    summed = jnp.concatenate(rows, axis=0)

    i = lax.broadcasted_iota(jnp.int32, (128, 256), 0)
    o = lax.broadcasted_iota(jnp.int32, (128, 256), 1)
    apart = (o // 128) * 1000 + o % 128 - (i // 64) * 1000 - ((i // 16) % 4) * 32 - (i % 8) // 2
    down = [jnp.where(apart == 4 * yb, 0.5, 0.0).astype(BF16) for yb in range(8)]
    coarse = jnp.dot(
        halves(summed, 0), jnp.concatenate(down, axis=0), preferred_element_type=F32
    )
    coarse = coarse[0:64] + coarse[64:128]
    below, above = [], []
    own = []
    for xb in range(8):
        part = coarse[xb * 8 : xb * 8 + 8]
        own.append(part[1:5, 0:128])
        own.append(part[1:5, 128:256])
        below.append(part[0:1, 0:128])
        above.append(part[5:6, 128:256])
    sent = jnp.concatenate(own + below + above, axis=0)
    for e in range(8):
        sent_ref[e] = sent


def source_step(scalars, occupations, own, near):
    smem = pl.BlockSpec(memory_space=pltpu.SMEM)
    vmem = pl.BlockSpec(memory_space=pltpu.VMEM)
    return pl.pallas_call(
        source_kernel,
        out_shape=jax.ShapeDtypeStruct((8, 80, 128), F32),
        in_specs=[smem, smem, vmem, vmem],
        out_specs=vmem,
        scratch_shapes=[pltpu.VMEM((64, 40, 128), F32)] * 3 + COUPLINGS,
        compiler_params=VMEM,
    )(scalars, occupations, own, near)


def double_rows(scratch, value, n):
    scratch[:, pl.ds(0, n, stride=2), :] = value
    scratch[:, pl.ds(1, n, stride=2), :] = value


def coarse_solve(g, v, r1, v2, r2, v3, r3, mats):
    down1, up1, down2, up2, near1, near2, near3 = mats

    def near(ref, blocks, planes, mat):
        rows = ref[:, 8 : 8 + planes, :]
        y = dot2(rows.reshape(blocks * planes, 128), mat[...])
        y = y.reshape(blocks, planes, -1)
        total = y[:, :, 0:128] + ref[:, 7 : 7 + planes, :] + ref[:, 9 : 9 + planes, :]
        if blocks > 1:
            none = jnp.zeros((1, planes, 128), F32)
            total = total + jnp.concatenate([none, y[:-1, :, 128:256]], axis=0)
            total = total + jnp.concatenate([y[1:, :, 256:384], none], axis=0)
        return rows, total

    def sweep(ref, source, blocks, planes, mat):
        rows, total = near(ref, blocks, planes, mat)
        ref[:, 8 : 8 + planes, :] = rows + OMEGA * (source() - 6.0 * rows + total)

    def residual(ref, source, blocks, planes, mat):
        rows, total = near(ref, blocks, planes, mat)
        return source() - 6.0 * rows + total

    for ref, planes in ((v, 64), (v2, 32), (v3, 16)):
        border = jnp.zeros((ref.shape[0], 8, 128), F32)
        ref[:, 0:8, :] = border
        ref[:, 8 + planes : 16 + planes, :] = border
    g1 = lambda: g[:, 8:72, :]
    v[:, 8:72, :] = OMEGA * g1()
    sweep(v, g1, 8, 64, near1)
    r1[...] = residual(v, g1, 8, 64, near1)
    pair = r1[:, pl.ds(0, 32, stride=2), :] + r1[:, pl.ds(1, 32, stride=2), :]
    rows = [jnp.concatenate([pair[4 * b + e] for e in range(4)], axis=1) for b in range(2)]
    d = jnp.dot(halves(jnp.concatenate(rows, axis=0), 0), down1[...], preferred_element_type=F32)
    s2 = (d[0:64] + d[64:128]).reshape(2, 32, 128)
    g2 = lambda: s2
    v2[:, 8:40, :] = OMEGA * s2
    sweep(v2, g2, 2, 32, near2)
    r2[...] = residual(v2, g2, 2, 32, near2)
    pair = r2[:, pl.ds(0, 16, stride=2), :] + r2[:, pl.ds(1, 16, stride=2), :]
    both = jnp.concatenate([pair[0], pair[1]], axis=1)
    d = jnp.dot(halves(both, 0), down2[...], preferred_element_type=F32)
    s3 = (d[0:16] + d[16:32]).reshape(1, 16, 128)
    g3 = lambda: s3
    v3[:, 8:24, :] = OMEGA * s3
    for _ in range(COARSE - 1):
        sweep(v3, g3, 1, 16, near3)
    double_rows(r3, v3[:, 8:24, :], 16)
    up = dot2(r3[0], up2[...])
    for b in range(2):
        v2[b, 8:40, :] = v2[b, 8:40, :] + up[:, b * 128 : b * 128 + 128]
    for _ in range(POST):
        sweep(v2, g2, 2, 32, near2)
    double_rows(r1.at[0:2], v2[:, 8:40, :], 32)
    up = dot2(r1[0:2].reshape(128, 128), up1[...])
    for b in range(8):
        part = up[(b // 4) * 64 : (b // 4) * 64 + 64, (b % 4) * 128 : (b % 4) * 128 + 128]
        v[b, 8:72, :] = v[b, 8:72, :] + part
    for _ in range(POST):
        sweep(v, g1, 8, 64, near1)


def finish_kernel(scalars, occ, got_ref, prev_ref, y_ref, next_ref, mat_ref, *refs):
    mats, out_ref = refs[:7], refs[7]
    fx, va, vb, up, g, v, r1, v2, r2, v3, r3, wide = refs[8:20]
    couplings = refs[20:]
    low = lanes_low((8, 128))
    slab, factor = scalars[0], OMEGA * (occ[scalars[1]] / 64.0)

    for s in range(8):
        g[:, 8 + 8 * s : 16 + 8 * s, :] = got_ref[SLAB_DEVICE[s], 0:64, :].reshape(8, 8, 128)
    for s in range(8):
        for xb in range(8):
            if s > 0:
                row = 8 + 8 * s - 1
                g[xb, row : row + 1, :] = g[xb, row : row + 1, :] + got_ref[SLAB_DEVICE[s], 64 + xb : 65 + xb, :]
            if s < 7:
                row = 8 + 8 * s + 8
                g[xb, row : row + 1, :] = g[xb, row : row + 1, :] + got_ref[SLAB_DEVICE[s], 72 + xb : 73 + xb, :]
    coarse_solve(g, v, r1, v2, r2, v3, r3, mats)
    double_rows(wide, v[:, pl.ds(8 * slab + 4, 16), :], 16)
    i = lax.broadcasted_iota(jnp.int32, (128, 128), 0)
    o = lax.broadcasted_iota(jnp.int32, (128, 128), 1)
    apart = i - ((o // 16) % 4) * 32 - (o % 8) // 2
    spread = jnp.concatenate(
        [jnp.where(apart == 4 * yb, 1.0, 0.0).astype(BF16) for yb in range(8)], axis=1
    )
    up[...] = dot2(wide[...].reshape(256, 128), spread).reshape(8, 32, 1024)

    def fill(i, carry):
        for u in range(16):
            src = i * 16 + u
            p, o, n = (factor * jnp.square(ref[src]) for ref in (prev_ref, y_ref, next_ref))
            fx[src, 8:16, :] = swap(jnp.where(low, o, p))
            fx[src, 16:24, :] = o
            fx[src, 24:32, :] = swap(jnp.where(low, n, o))
            out_ref[src, 0:8, :] = y_ref[src]
        return carry

    lax.fori_loop(0, 4, fill, 0)
    clear_borders(couplings, 2)
    keep = {r: inside_slab_range(slab, r) for r in (14, 18, 15, 17)}

    def second(src, r, c, near):
        va[src, r : r + 8, :] = jnp.where(keep[r], 1.2 * c + OMEGA * near, 0.0)

    def add_up(xb, carry):
        for yb in range(8):
            src = xb * 8 + yb
            for r, n in ((14, 8), (22, 4)):
                e = jnp.where(
                    lanes_low((n, 128)),
                    up[xb, r - 8 : r - 8 + n, yb * 128 : yb * 128 + 128],
                    up[xb, r : r + n, yb * 128 : yb * 128 + 128],
                )
                va[src, r : r + n, :] = va[src, r : r + n, :] + e
        return carry

    def swept(src, r, c, near):
        return c + (fx[src, r : r + 8, :] - DAMPING * c + OMEGA * near)

    def fourth(src, r, c, near):
        vb[src, r : r + 8, :] = jnp.where(keep[r], swept(src, r, c, near), 0.0)

    def fifth(src, r, c, near):
        out_ref[src, 8:16, :] = swept(src, r, c, near)

    relax(fx, (14, 18), mat_ref, couplings, second)
    lax.fori_loop(0, 8, add_up, 0)
    relax(va, (15, 17), mat_ref, couplings, fourth)
    relax(vb, (16,), mat_ref, couplings, fifth)


def finish_step(scalars, occupations, got, halo, own, near, levels):
    smem = pl.BlockSpec(memory_space=pltpu.SMEM)
    vmem = pl.BlockSpec(memory_space=pltpu.VMEM)
    ins = [scalars, occupations, got, halo[0], own, halo[1], near, *levels]
    return pl.pallas_call(
        finish_kernel,
        out_shape=jax.ShapeDtypeStruct((64, 16, 128), F32),
        in_specs=[smem, smem] + [vmem] * (len(ins) - 2),
        out_specs=vmem,
        scratch_shapes=[
            pltpu.VMEM((64, 40, 128), F32),
            pltpu.VMEM((64, 40, 128), F32),
            pltpu.VMEM((64, 40, 128), F32),
            pltpu.VMEM((8, 32, 1024), F32),
            pltpu.VMEM((8, 80, 128), F32),
            pltpu.VMEM((8, 80, 128), F32),
            pltpu.VMEM((8, 64, 128), F32),
            pltpu.VMEM((2, 48, 128), F32),
            pltpu.VMEM((2, 32, 128), F32),
            pltpu.VMEM((1, 32, 128), F32),
            pltpu.VMEM((1, 32, 128), F32),
            pltpu.VMEM((8, 32, 128), F32),
        ]
        + COUPLINGS,
        compiler_params=VMEM,
    )(*ins)


def exchange(value, axes, dim, width, order=None):
    order = order or list(range(8))
    up = [(order[i], order[i + 1]) for i in range(7)]
    down = [(j, i) for i, j in up]
    length = value.shape[dim]
    before = lax.ppermute(lax.slice_in_dim(value, length - width, length, axis=dim), axes, up)
    after = lax.ppermute(lax.slice_in_dim(value, 0, width, axis=dim), axes, down)
    return before, after


def local(
    orbitals, local_potential, occupations, proj_values, proj_strength, atom_block, atom_offset
):
    core, xlo, ylo = (lax.axis_index(a) for a in GROUP)
    slab = 2 * (xlo * (3 - ylo) + (1 - xlo) * ylo) + core
    lists, strength = atom_lists(slab, proj_strength, atom_block, atom_offset)
    high, low = coupling(HALF)
    mats = (jnp.asarray(high), jnp.asarray(low))

    packed = pack(orbitals, local_potential)
    tiles = projector_tiles(proj_values)
    own = lax.all_to_all(packed, PLANE, 0, 0, tiled=True)

    sigma = HALF_WIDTH / (0.0 - CENTER)
    tau = 2.0 / sigma
    coefs = [(sigma / HALF_WIDTH, 0.0)]
    for _ in range(DEGREE - 1):
        following = 1.0 / (tau - sigma)
        coefs.append((2.0 * following / HALF_WIDTH, sigma * following))
        sigma = following
    older = pot = None
    for k in range(0, DEGREE, 2):
        first, last = k == 0, k == DEGREE - 2
        halo = exchange(own, GROUP, 1, own.shape[1], SLAB_DEVICE)
        outs = list(
            double_step(
                first, last, coefs[k], coefs[k + 1], lists, strength, halo, own, older, pot, tiles, mats
            )
        )
        own = outs.pop(0)
        if first:
            pot = outs.pop(0)
        if not last:
            older = outs.pop(0)

    scalars = jnp.stack([slab, 2 * lax.axis_index("yhi") + lax.axis_index("xhi")]).astype(jnp.int32)
    near = jnp.asarray(coupling((0.0, 1.0))[0])
    levels = [jnp.asarray(m) for m in level_matrices()]
    halo = exchange(own, GROUP, 1, 8, SLAB_DEVICE)
    sent = source_step(scalars, occupations, own, near)
    got = lax.all_to_all(sent, GROUP, 0, 0, tiled=True)
    packed = finish_step(scalars, occupations, got, halo, own, near, levels)
    back = lax.all_to_all(packed, PLANE, 0, 0, tiled=True)
    filtered, part = unpack(back)
    hartree = jnp.sum(lax.all_to_all(part, BAND, 0, 0, tiled=True), axis=0)
    return filtered.reshape(8, 8, 8, 128), hartree.reshape(8, 8, 128)


def solution(mesh):
    fine = Mesh(
        mesh.devices.reshape(8, 4, 2, 2, 2, 2), (BAND, "yhi", "core", "xhi", "xlo", "ylo")
    )
    bands, grid = P(BAND, GX, GYZ, None), P(GX, GYZ, None)
    return jax.shard_map(
        local,
        mesh=fine,
        in_specs=(bands, grid, P(BAND), P(), P(), P(), P()),
        out_specs=(bands, grid),
        check_vma=False,
    )
```

```python
import functools

import jax
import jax.numpy as jnp
import numpy as np
from jax import lax
from jax.experimental import pallas as pl
from jax.experimental.pallas import tpu as pltpu
from jax.sharding import Mesh
from jax.sharding import PartitionSpec as P

DEGREE = 8
POST = 2
COARSE = 4
STENCIL = (
    -5369.0 / 1800.0,
    12.0 / 7.0,
    -15.0 / 56.0,
    10.0 / 189.0,
    -1.0 / 112.0,
    2.0 / 1925.0,
    -1.0 / 16632.0,
)
HALF = tuple(-0.5 * c for c in STENCIL)
REACH = 6
CENTER = 12.0
HALF_WIDTH = 8.0
DAMPING = 0.8
BAND = "z"
GX = ("yhi", "core")
GYZ = ("xhi", "xlo", "ylo")
PLANE = GX + GYZ
GROUP = ("core", "xlo", "ylo")
CHIPS = ((0, 0), (0, 1), (1, 1), (1, 0))
SLAB_DEVICE = [c * 4 + xl * 2 + yl for xl, yl in CHIPS for c in (0, 1)]
VMEM = pltpu.CompilerParams(vmem_limit_bytes=12 * 1024 * 1024)
FILL = 64
HEAD = 3
F32 = jnp.float32
BF16 = jnp.bfloat16


def plane_index(band, slab):
    yhi, xhi = band // 2, band % 2
    xlo, ylo = CHIPS[slab // 2]
    return yhi * 16 + (slab % 2) * 8 + xhi * 4 + xlo * 2 + ylo


def coupling(weights):
    own, xu, xd, yu, yd = (np.zeros((128, 128)) for _ in range(5))
    for zh in range(2):
        for xi in range(8):
            for yi in range(8):
                i = zh * 64 + xi * 8 + yi
                for o in range(8):
                    for m, k in ((own, abs(o - xi)), (xu, o + 8 - xi), (xd, xi + 8 - o)):
                        if 1 <= k < len(weights):
                            m[i, zh * 64 + o * 8 + yi] += weights[k]
                    for m, k in ((own, abs(o - yi)), (yu, o + 8 - yi), (yd, yi + 8 - o)):
                        if 1 <= k < len(weights):
                            m[i, zh * 64 + xi * 8 + o] += weights[k]
    whole = np.concatenate([own, xu, xd, yu, yd], axis=1).astype(np.float32)
    high = whole.astype(jnp.bfloat16)
    low = (whole - high.astype(np.float32)).astype(jnp.bfloat16)
    return high, low


def halves(x, axis):
    high = x.astype(BF16)
    return jnp.concatenate([high, (x - high.astype(F32)).astype(BF16)], axis=axis)


def lanes_low(shape):
    return lax.broadcasted_iota(jnp.int32, shape, len(shape) - 1) < 64


def dot2(x, m):
    return jnp.dot(halves(x, 1), jnp.concatenate([m, m], axis=0), preferred_element_type=F32)


def swap(x):
    return pltpu.roll(x, 64, x.ndim - 1)


def split3(x):
    a = x.astype(BF16)
    r = x - a.astype(F32)
    b = r.astype(BF16)
    c = (r - b.astype(F32)).astype(BF16)
    return a, b, c


def pack_kernel(orb_ref, pot_ref, out_ref):
    low = lanes_low((8, 128))
    for q in range(4):
        turned = orb_ref[q * 128 : (q + 1) * 128, :].T
        for s in range(8):
            a = turned[s * 16 : s * 16 + 8, :]
            b = turned[s * 16 + 8 : s * 16 + 16, :]
            out_ref[plane_index(2 * q, s), 0:8, :] = jnp.where(low, a, swap(b))
            out_ref[plane_index(2 * q + 1, s), 0:8, :] = jnp.where(low, swap(a), b)
    pot = pot_ref[...]
    turned = jnp.concatenate([pot, pot], axis=0).T
    for s in range(8):
        piece = jnp.where(low, turned[s * 16 : s * 16 + 8, :], turned[s * 16 + 8 : s * 16 + 16, :])
        for b in range(8):
            out_ref[plane_index(b, s), 8:16, :] = piece


def pack(orbitals, potential):
    return pl.pallas_call(
        pack_kernel,
        out_shape=jax.ShapeDtypeStruct((64, 16, 128), F32),
        compiler_params=VMEM,
    )(orbitals.reshape(512, 128), potential.reshape(64, 128))


def tiles_kernel(proj_ref, pick_ref, tiles_ref):
    low = lanes_low((8, 2, 8, 128))
    keep = lax.broadcasted_iota(jnp.int32, (4, 8, 512), 2) % 8 == lax.broadcasted_iota(
        jnp.int32, (4, 8, 512), 1
    )

    def body(i, carry):
        parts = [
            jnp.where(keep, proj_ref[i * 8 + u][:, None, :], 0.0).reshape(32, 512)
            for u in range(8)
        ]
        spread = jnp.concatenate(parts, axis=0)
        pick = pick_ref[...]
        total = sum(jnp.dot(part, pick, preferred_element_type=F32) for part in split3(spread))
        total = total.reshape(8, 2, 2, 8, 128)
        tiles_ref[pl.ds(i * 8, 8), :, :, :] = jnp.where(low, total[:, :, 0], total[:, :, 1])
        return carry

    lax.fori_loop(0, 8, body, 0)


def projector_tiles(proj):
    pick = (np.arange(512)[:, None] // 8 == np.arange(128)[None, :] % 64).astype(jnp.bfloat16)
    return pl.pallas_call(
        tiles_kernel,
        out_shape=jax.ShapeDtypeStruct((64, 2, 8, 128), F32),
        compiler_params=VMEM,
    )(proj, pick)


ID, SRC, ROW, UPPER, ROW_L, ON_L, ROW_U, ON_U, META = range(9)


def double_kernel(
    first, last, coef1, coef2, lists, strength, prev_ref, own_ref, next_ref, *refs
):
    refs = list(refs)
    if first:
        older_ref = pot_ref = None
    else:
        older_ref, pot_ref = refs.pop(0), refs.pop(0)
    tiles_ref, mat_ref, mat_low_ref = refs[:3]
    refs = refs[3:]
    out_ref = refs.pop(0)
    if first:
        pot_ref = refs.pop(0)
    mid_ref = None if last else refs.pop(0)
    ext, mid, new, c_own, c_xu, c_xd, c_yu, c_yd, weights = refs
    low = lanes_low((8, 128))
    count = lists[META, 0]
    below = lists[META, 1] > 0
    above = lists[META, 2] > 0
    zero8 = jnp.zeros((8, 128), F32)

    for t in range(3):
        for e in range(8):
            c_xu[t, e, :, :] = zero8
            c_xd[t, 64 + e, :, :] = zero8
    def fill(i, carry):
        for u in range(FILL):
            src = i * FILL + u
            p, o, n = prev_ref[src, 0:8, :], own_ref[src, 0:8, :], next_ref[src, 0:8, :]
            ext[src, 0:8, :] = p
            ext[src, 8:16, :] = swap(jnp.where(low, o, p))
            ext[src, 16:24, :] = o
            ext[src, 24:32, :] = swap(jnp.where(low, n, o))
            ext[src, 32:40, :] = n
            if first:
                p, o, n = prev_ref[src, 8:16, :], own_ref[src, 8:16, :], next_ref[src, 8:16, :]
                shift = 3.0 * HALF[0] - CENTER
                pot_ref[src, 0:8, :] = swap(jnp.where(low, o, p)) + shift
                pot_ref[src, 8:16, :] = o + shift
                pot_ref[src, 16:24, :] = swap(jnp.where(low, n, o)) + shift
        return carry

    lax.fori_loop(0, 64 // FILL, fill, 0)

    def products(f_ref, tiles):
        for t in tiles:
            x = f_ref[:, t * 8 + 8 : t * 8 + 16, :].reshape(512, 128)
            both = halves(x, 1)
            m = mat_ref[...]
            y = jnp.dot(both, jnp.concatenate([m, m], axis=0), preferred_element_type=F32)
            y = y + jnp.dot(both[:, 0:128], mat_low_ref[...], preferred_element_type=F32)
            y = y.reshape(64, 8, 640)
            c_own[t, :, :, :] = y[:, :, 0:128]
            c_xu[t, 8:72, :, :] = y[:, :, 128:256]
            c_xd[t, 0:64, :, :] = y[:, :, 256:384]
            c_yu[t, :, :, :] = y[:, :, 384:512]
            c_yd[t, :, :, :] = y[:, :, 512:640]

    def project(f_ref):
        def chunk(i):
            found = []
            for u in range(8):
                ii = i * 8 + u
                w = f_ref[lists[SRC, ii], pl.ds(lists[ROW, ii], 8), :]
                w = jnp.where(low == (lists[UPPER, ii] == 0), w, 0.0)
                w = w + swap(w)
                found.append(jnp.sum(tiles_ref[lists[ID, ii]] * w[None], axis=1))
            return jnp.concatenate(found, axis=0)

        i, o = lane_pairs(128, 128)
        same_half = filled(i // 64 == o // 64, 1.0)
        head = jnp.concatenate([chunk(i) for i in range(HEAD)], axis=0)
        weights[0 : HEAD * 16, :] = dot2(head, same_half)

        def body(i, carry):
            weights[pl.ds(pl.multiple_of(i * 16, 16), 16), :] = dot2(chunk(i), same_half)
            return carry

        lax.fori_loop(HEAD, (count + 7) // 8, body, 0)

    def combine(f_ref, y_ref, older, tiles, coef):
        a, b = coef

        def body(xb, carry):
            for yb in range(8):
                src = xb * 8 + yb
                rows = {}
                for t in tiles:
                    for o in range(t * 8 + 8 - REACH, t * 8 + 9 + REACH):
                        if o not in rows:
                            rows[o] = f_ref[src, o : o + 8, :]
                done = []
                for t in tiles:
                    r = t * 8 + 8
                    total = c_own[t, src] + c_xu[t, src] + c_xd[t, src + 8]
                    if yb > 0:
                        total = total + c_yu[t, src - 1]
                    if yb < 7:
                        total = total + c_yd[t, src + 1]
                    for k in range(1, REACH + 1):
                        total = total + HALF[k] * (rows[r + k] + rows[r - k])
                    total = a * (total + pot_ref[src, t * 8 : t * 8 + 8, :] * rows[r])
                    if older is not None:
                        total = total - b * older(src, t)
                    if t == 0:
                        total = jnp.where(jnp.logical_or(below, jnp.logical_not(low)), total, 0.0)
                    if t == 2:
                        total = jnp.where(jnp.logical_or(above, low), total, 0.0)
                    done.append(total)
                for t, total in zip(tiles, done):
                    y_ref[src, t * 8 + 8 : t * 8 + 16, :] = total
            return carry

        lax.fori_loop(0, 8, body, 0)

    def spread(y_ref, a):
        low_row = lanes_low((1, 128))

        def term(i, u, w):
            ii = i * 8 + u
            atom = lists[ID, ii]
            t = zero8
            for q in range(2):
                scale = jnp.where(low_row, strength[2 * q, ii] * a, strength[2 * q + 1, ii] * a)
                t = t + (scale * w[u * 2 + q : u * 2 + q + 1, :]) * tiles_ref[atom, q]
            return t + swap(t)

        def add(i, u, t):
            ii = i * 8 + u
            src = lists[SRC, ii]
            rows = pl.ds(lists[ROW_L, ii], 8)
            on = jnp.logical_and(low, lists[ON_L, ii] > 0)
            y_ref[src, rows, :] = y_ref[src, rows, :] + jnp.where(on, t, 0.0)
            rows = pl.ds(lists[ROW_U, ii], 8)
            on = jnp.logical_and(jnp.logical_not(low), lists[ON_U, ii] > 0)
            y_ref[src, rows, :] = y_ref[src, rows, :] + jnp.where(on, t, 0.0)

        for i in range(HEAD):
            w = weights[i * 16 : i * 16 + 16, :]
            terms = [term(i, u, w) for u in range(8)]
            for u in range(8):
                add(i, u, terms[u])

        def body(i, carry):
            w = weights[pl.ds(pl.multiple_of(i * 16, 16), 16), :]
            terms = [term(i, u, w) for u in range(8)]
            for u in range(8):
                add(i, u, terms[u])
            return carry

        lax.fori_loop(HEAD, (count + 7) // 8, body, 0)

    products(ext, range(3))
    project(ext)
    older = None if first else (lambda src, t: older_ref[src, t * 8 : t * 8 + 8, :])
    combine(ext, mid, older, (0, 1, 2), coef1)
    spread(mid, coef1[0])
    products(mid, (1,))
    project(mid)
    combine(mid, new, lambda src, t: ext[src, 16:24, :], (1,), coef2)
    spread(new, coef2[0])
    out_ref[...] = new[:, 16:24, :]
    if not last:
        mid_ref[...] = mid[:, 8:32, :]


def double_step(first, last, coef1, coef2, lists, strength, halo, own, older, pot, tiles, mats):
    smem = pl.BlockSpec(memory_space=pltpu.SMEM)
    vmem = pl.BlockSpec(memory_space=pltpu.VMEM)
    ins = [lists, strength, halo[0], own, halo[1]]
    if not first:
        ins += [older, pot]
    ins += [tiles, *mats]
    outs = [jax.ShapeDtypeStruct((64, 8, 128), F32)]
    if first:
        outs.append(jax.ShapeDtypeStruct((64, 24, 128), F32))
    if not last:
        outs.append(jax.ShapeDtypeStruct((64, 24, 128), F32))
    return pl.pallas_call(
        functools.partial(double_kernel, first, last, coef1, coef2),
        out_shape=tuple(outs),
        in_specs=[smem, smem] + [vmem] * (len(ins) - 2),
        out_specs=tuple([vmem] * len(outs)),
        scratch_shapes=[
            pltpu.VMEM((64, 40, 128), F32),
            pltpu.VMEM((64, 40, 128), F32),
            pltpu.VMEM((64, 40, 128), F32),
            pltpu.VMEM((3, 64, 8, 128), F32),
            pltpu.VMEM((3, 72, 8, 128), F32),
            pltpu.VMEM((3, 72, 8, 128), F32),
            pltpu.VMEM((3, 64, 8, 128), F32),
            pltpu.VMEM((3, 64, 8, 128), F32),
            pltpu.VMEM((128, 128), F32),
        ],
        compiler_params=VMEM,
    )(*ins)


def atom_lists(slab, proj_strength, atom_block, atom_offset):
    number = jnp.arange(64, dtype=jnp.int32)
    dz = atom_offset[:, 2] - 16 * slab
    near = jnp.logical_and(dz >= -15, dz <= 23)
    before = jnp.sum(
        jnp.logical_and(near[None, :], number[None, :] < number[:, None]).astype(jnp.int32), axis=1
    )
    pick = jnp.logical_and(near[None, :], before[None, :] == number[:, None])

    def listed(values, empty):
        return jnp.sum(jnp.where(pick, values[None, :], 0), axis=1) + jnp.where(
            jnp.any(pick, axis=1), 0, empty
        )

    at = listed(dz, 0)
    valid = jnp.any(pick, axis=1)
    source = listed(jnp.clip(atom_block, 0, 63), 0)
    upper = at > 8
    meta = jnp.zeros((64,), jnp.int32).at[0].set(jnp.sum(near.astype(jnp.int32)))
    meta = meta.at[1].set(slab).at[2].set(7 - slab)
    lists = jnp.stack(
        [
            listed(number, 0),
            source,
            jnp.where(upper, at - 8, at) + 16,
            upper.astype(jnp.int32),
            jnp.clip(at, -16, 16) + 16,
            jnp.logical_and(valid, at <= 15).astype(jnp.int32),
            jnp.clip(at - 8, -16, 16) + 16,
            jnp.logical_and(valid, at >= -7).astype(jnp.int32),
            meta,
        ]
    )
    strength = jnp.sum(jnp.where(pick[None], proj_strength.T[:, None, :], 0.0), axis=2)
    return lists, strength


def unpack_kernel(in_ref, out_ref, hartree_ref):
    low = lanes_low((8, 128))

    def block(pairs):
        rows = []
        for a, b in pairs:
            rows += [jnp.where(low, a, swap(b)), jnp.where(low, swap(a), b)]
        return jnp.concatenate(rows, axis=0).T

    for q in range(4):
        out_ref[q * 128 : (q + 1) * 128, :] = block(
            [
                (in_ref[plane_index(2 * q, s), 0:8, :], in_ref[plane_index(2 * q + 1, s), 0:8, :])
                for s in range(8)
            ]
        )
    pairs = []
    for s in range(8):
        total = in_ref[plane_index(0, s), 8:16, :]
        for b in range(1, 8):
            total = total + in_ref[plane_index(b, s), 8:16, :]
        pairs.append((total, total))
    part = block(pairs)[0:64, :]
    for e in range(8):
        hartree_ref[e] = part


def unpack(slabs):
    return pl.pallas_call(
        unpack_kernel,
        out_shape=(
            jax.ShapeDtypeStruct((512, 128), F32),
            jax.ShapeDtypeStruct((8, 64, 128), F32),
        ),
        compiler_params=VMEM,
    )(slabs)


OMEGA = DAMPING / 6.0


def lane_pairs(rows, columns):
    shape = (rows, columns)
    return lax.broadcasted_iota(jnp.int32, shape, 0), lax.broadcasted_iota(jnp.int32, shape, 1)


def filled(where, value):
    return jnp.where(where, value, 0.0).astype(BF16)


def both(*conditions):
    return functools.reduce(jnp.logical_and, conditions)


def transfers(fine_x, fine_y, down):
    fine, coarse = fine_x * fine_y, 128
    i, o = lane_pairs(fine, coarse) if down else lane_pairs(coarse, fine)
    f, c = (i, o) if down else (o, i)
    same = both(
        (f // fine_y) // 2 == c // (fine_y // 2), (f % fine_y) // 2 == c % (fine_y // 2)
    )
    return filled(same, 0.5 if down else 1.0)


def beside(nx, ny, used):
    i, o = lane_pairs(128, 128)
    dx, dy = o // ny - i // ny, o % ny - i % ny
    parts = [filled(both(jnp.abs(dx) + jnp.abs(dy) == 1, i // ny < used, o // ny < used), 1.0)]
    if used == nx:
        parts += [filled(both(dx == d, dy == 0), 1.0) for d in (1 - nx, nx - 1)]
    return jnp.concatenate(parts, axis=1)


def block_neighbours():
    i, o = lane_pairs(128, 128)
    half = i // 64 == o // 64
    dx, dy = (o // 8) % 8 - (i // 8) % 8, o % 8 - i % 8
    parts = [both(half, jnp.abs(dx) + jnp.abs(dy) == 1)]
    parts += [both(half, dx == d, dy == 0) for d in (-7, 7)]
    parts += [both(half, dx == 0, dy == d) for d in (-7, 7)]
    return jnp.concatenate([filled(p, 1.0) for p in parts], axis=1)


def xy_products(ref, r, mat, couplings, t):
    c_own, c_xu, c_xd, c_yu, c_yd = couplings
    x = ref[:, r : r + 8, :].reshape(512, 128)
    y = dot2(x, mat).reshape(64, 8, 640)
    c_own[t, :, :, :] = y[:, :, 0:128]
    c_xu[t, 8:72, :, :] = y[:, :, 128:256]
    c_xd[t, 0:64, :, :] = y[:, :, 256:384]
    c_yu[t, :, :, :] = y[:, :, 384:512]
    c_yd[t, :, :, :] = y[:, :, 512:640]


def xy_sum(couplings, t, xb, yb):
    c_own, c_xu, c_xd, c_yu, c_yd = couplings
    src = xb * 8 + yb
    total = c_own[t, src] + c_xu[t, src] + c_xd[t, src + 8]
    if yb > 0:
        total = total + c_yu[t, src - 1]
    if yb < 7:
        total = total + c_yd[t, src + 1]
    return total


def clear_borders(couplings, tiles):
    zero = jnp.zeros((8, 8, 128), F32)
    for t in range(tiles):
        couplings[1][t, 0:8] = zero
        couplings[2][t, 64:72] = zero


COUPLINGS = [
    pltpu.VMEM((2, n, 8, 128), F32) for n in (64, 72, 72, 64, 64)
]


def inside_slab_range(slab, r):
    z = (
        lax.broadcasted_iota(jnp.int32, (8, 128), 0)
        + jnp.where(lanes_low((8, 128)), 0, 8)
        + (16 * slab + (r - 16))
    )
    return jnp.logical_and(z >= 0, z < 128)


def relax(ref, rows, mat, couplings, update):
    for t, r in enumerate(rows):
        xy_products(ref, r, mat, couplings, t)
    for t, r in enumerate(rows):

        def body(xb, carry, t=t, r=r):
            for yb in range(8):
                src = xb * 8 + yb
                near = xy_sum(couplings, t, xb, yb)
                near = near + ref[src, r - 1 : r + 7, :] + ref[src, r + 1 : r + 9, :]
                update(src, r, ref[src, r : r + 8, :], near)
            return carry

        lax.fori_loop(0, 8, body, 0)


def source_kernel(scalars, occ, own_ref, sent_ref, v, w, r0, *couplings):
    mat = block_neighbours()
    low = lanes_low((8, 128))
    slab, occupation = scalars[0], occ[scalars[1]] / 64.0
    zero = jnp.zeros((8, 128), F32)

    def fill(i, carry):
        for u in range(16):
            src = i * 16 + u
            y = own_ref[src]
            o = OMEGA * (occupation * y * y)
            v[src, 0:8, :] = zero
            v[src, 8:16, :] = swap(jnp.where(low, o, 0.0))
            v[src, 16:24, :] = o
            v[src, 24:32, :] = swap(jnp.where(low, 0.0, o))
            v[src, 32:40, :] = zero
            w[src, 8:16, :] = zero
            w[src, 24:32, :] = zero
        return carry

    lax.fori_loop(0, 4, fill, 0)
    clear_borders(couplings, 2)
    keep = {r: inside_slab_range(slab, r) for r in (13, 19)}

    def second(src, r, c, near):
        w[src, r : r + 8, :] = jnp.where(keep[r], 1.2 * c + OMEGA * near, 0.0)

    def residual(src, r, c, near):
        r0[src, r : r + 8, :] = v[src, r : r + 8, :] * (1.0 / OMEGA) - 6.0 * c + near

    relax(v, (13, 19), mat, couplings, second)
    relax(w, (14, 18), mat, couplings, residual)
    rows = []
    for xb in range(8):
        parts = []
        for yb in range(8):
            src = xb * 8 + yb
            parts.append(r0[src, pl.ds(14, 8, stride=2), :] + r0[src, pl.ds(15, 8, stride=2), :])
        rows.append(jnp.concatenate(parts, axis=1))
    summed = jnp.concatenate(rows, axis=0)

    i = lax.broadcasted_iota(jnp.int32, (128, 256), 0)
    o = lax.broadcasted_iota(jnp.int32, (128, 256), 1)
    apart = (o // 128) * 1000 + o % 128 - (i // 64) * 1000 - ((i // 16) % 4) * 32 - (i % 8) // 2
    down = [jnp.where(apart == 4 * yb, 0.5, 0.0).astype(BF16) for yb in range(8)]
    coarse = jnp.dot(
        halves(summed, 0), jnp.concatenate(down, axis=0), preferred_element_type=F32
    )
    coarse = coarse[0:64] + coarse[64:128]
    below, above = [], []
    own = []
    for xb in range(8):
        part = coarse[xb * 8 : xb * 8 + 8]
        own.append(part[1:5, 0:128])
        own.append(part[1:5, 128:256])
        below.append(part[0:1, 0:128])
        above.append(part[5:6, 128:256])
    sent = jnp.concatenate(own + below + above, axis=0)
    for e in range(8):
        sent_ref[e] = sent


def source_step(scalars, occupations, own):
    smem = pl.BlockSpec(memory_space=pltpu.SMEM)
    vmem = pl.BlockSpec(memory_space=pltpu.VMEM)
    return pl.pallas_call(
        source_kernel,
        out_shape=jax.ShapeDtypeStruct((8, 80, 128), F32),
        in_specs=[smem, smem, vmem],
        out_specs=vmem,
        scratch_shapes=[pltpu.VMEM((64, 40, 128), F32)] * 3 + COUPLINGS,
        compiler_params=VMEM,
    )(scalars, occupations, own)


def double_rows(scratch, value, n):
    scratch[:, pl.ds(0, n, stride=2), :] = value
    scratch[:, pl.ds(1, n, stride=2), :] = value


def coarse_solve(g, v, r1, v2, r2, v3, r3):
    near1, near2, near3 = beside(4, 32, 4), beside(8, 16, 8), beside(16, 8, 8)

    def near(ref, blocks, planes, mat):
        rows = ref[:, 8 : 8 + planes, :]
        y = dot2(rows.reshape(blocks * planes, 128), mat)
        y = y.reshape(blocks, planes, -1)
        total = y[:, :, 0:128] + ref[:, 7 : 7 + planes, :] + ref[:, 9 : 9 + planes, :]
        if blocks > 1:
            none = jnp.zeros((1, planes, 128), F32)
            total = total + jnp.concatenate([none, y[:-1, :, 128:256]], axis=0)
            total = total + jnp.concatenate([y[1:, :, 256:384], none], axis=0)
        return rows, total

    def sweep(ref, source, blocks, planes, mat):
        rows, total = near(ref, blocks, planes, mat)
        ref[:, 8 : 8 + planes, :] = rows + OMEGA * (source() - 6.0 * rows + total)

    def residual(ref, source, blocks, planes, mat):
        rows, total = near(ref, blocks, planes, mat)
        return source() - 6.0 * rows + total

    for ref, planes in ((v, 64), (v2, 32), (v3, 16)):
        border = jnp.zeros((ref.shape[0], 8, 128), F32)
        ref[:, 0:8, :] = border
        ref[:, 8 + planes : 16 + planes, :] = border
    g1 = lambda: g[:, 8:72, :]
    v[:, 8:72, :] = OMEGA * g1()
    sweep(v, g1, 8, 64, near1)
    r1[...] = residual(v, g1, 8, 64, near1)
    pair = r1[:, pl.ds(0, 32, stride=2), :] + r1[:, pl.ds(1, 32, stride=2), :]
    rows = [jnp.concatenate([pair[4 * b + e] for e in range(4)], axis=1) for b in range(2)]
    d = jnp.dot(halves(jnp.concatenate(rows, axis=0), 0), transfers(16, 32, True), preferred_element_type=F32)
    s2 = (d[0:64] + d[64:128]).reshape(2, 32, 128)
    g2 = lambda: s2
    v2[:, 8:40, :] = OMEGA * s2
    sweep(v2, g2, 2, 32, near2)
    r2[...] = residual(v2, g2, 2, 32, near2)
    pair = r2[:, pl.ds(0, 16, stride=2), :] + r2[:, pl.ds(1, 16, stride=2), :]
    both = jnp.concatenate([pair[0], pair[1]], axis=1)
    d = jnp.dot(halves(both, 0), transfers(16, 16, True), preferred_element_type=F32)
    s3 = (d[0:16] + d[16:32]).reshape(1, 16, 128)
    g3 = lambda: s3
    v3[:, 8:24, :] = OMEGA * s3
    for _ in range(COARSE - 1):
        sweep(v3, g3, 1, 16, near3)
    double_rows(r3, v3[:, 8:24, :], 16)
    up = dot2(r3[0], transfers(16, 16, False))
    for b in range(2):
        v2[b, 8:40, :] = v2[b, 8:40, :] + up[:, b * 128 : b * 128 + 128]
    for _ in range(POST):
        sweep(v2, g2, 2, 32, near2)
    double_rows(r1.at[0:2], v2[:, 8:40, :], 32)
    up = dot2(r1[0:2].reshape(128, 128), transfers(16, 32, False))
    for b in range(8):
        part = up[(b // 4) * 64 : (b // 4) * 64 + 64, (b % 4) * 128 : (b % 4) * 128 + 128]
        v[b, 8:72, :] = v[b, 8:72, :] + part
    for _ in range(POST):
        sweep(v, g1, 8, 64, near1)


def finish_kernel(scalars, occ, got_ref, prev_ref, y_ref, next_ref, *refs):
    mat = block_neighbours()
    out_ref = refs[0]
    fx, va, vb, up, g, v, r1, v2, r2, v3, r3, wide = refs[1:13]
    couplings = refs[13:]
    low = lanes_low((8, 128))
    slab, factor = scalars[0], OMEGA * (occ[scalars[1]] / 64.0)

    for s in range(8):
        g[:, 8 + 8 * s : 16 + 8 * s, :] = got_ref[SLAB_DEVICE[s], 0:64, :].reshape(8, 8, 128)
    for s in range(8):
        for xb in range(8):
            if s > 0:
                row = 8 + 8 * s - 1
                g[xb, row : row + 1, :] = g[xb, row : row + 1, :] + got_ref[SLAB_DEVICE[s], 64 + xb : 65 + xb, :]
            if s < 7:
                row = 8 + 8 * s + 8
                g[xb, row : row + 1, :] = g[xb, row : row + 1, :] + got_ref[SLAB_DEVICE[s], 72 + xb : 73 + xb, :]
    coarse_solve(g, v, r1, v2, r2, v3, r3)
    double_rows(wide, v[:, pl.ds(8 * slab + 4, 16), :], 16)
    i = lax.broadcasted_iota(jnp.int32, (128, 128), 0)
    o = lax.broadcasted_iota(jnp.int32, (128, 128), 1)
    apart = i - ((o // 16) % 4) * 32 - (o % 8) // 2
    spread = jnp.concatenate(
        [jnp.where(apart == 4 * yb, 1.0, 0.0).astype(BF16) for yb in range(8)], axis=1
    )
    up[...] = dot2(wide[...].reshape(256, 128), spread).reshape(8, 32, 1024)

    def fill(i, carry):
        for u in range(16):
            src = i * 16 + u
            p, o, n = (factor * jnp.square(ref[src]) for ref in (prev_ref, y_ref, next_ref))
            fx[src, 8:16, :] = swap(jnp.where(low, o, p))
            fx[src, 16:24, :] = o
            fx[src, 24:32, :] = swap(jnp.where(low, n, o))
            out_ref[src, 0:8, :] = y_ref[src]
        return carry

    lax.fori_loop(0, 4, fill, 0)
    clear_borders(couplings, 2)
    keep = {r: inside_slab_range(slab, r) for r in (14, 18, 15, 17)}

    def second(src, r, c, near):
        va[src, r : r + 8, :] = jnp.where(keep[r], 1.2 * c + OMEGA * near, 0.0)

    def add_up(xb, carry):
        for yb in range(8):
            src = xb * 8 + yb
            for r, n in ((14, 8), (22, 4)):
                e = jnp.where(
                    lanes_low((n, 128)),
                    up[xb, r - 8 : r - 8 + n, yb * 128 : yb * 128 + 128],
                    up[xb, r : r + n, yb * 128 : yb * 128 + 128],
                )
                va[src, r : r + n, :] = va[src, r : r + n, :] + e
        return carry

    def swept(src, r, c, near):
        return c + (fx[src, r : r + 8, :] - DAMPING * c + OMEGA * near)

    def fourth(src, r, c, near):
        vb[src, r : r + 8, :] = jnp.where(keep[r], swept(src, r, c, near), 0.0)

    def fifth(src, r, c, near):
        out_ref[src, 8:16, :] = swept(src, r, c, near)

    relax(fx, (14, 18), mat, couplings, second)
    lax.fori_loop(0, 8, add_up, 0)
    relax(va, (15, 17), mat, couplings, fourth)
    relax(vb, (16,), mat, couplings, fifth)


def finish_step(scalars, occupations, got, halo, own):
    smem = pl.BlockSpec(memory_space=pltpu.SMEM)
    vmem = pl.BlockSpec(memory_space=pltpu.VMEM)
    ins = [scalars, occupations, got, halo[0], own, halo[1]]
    return pl.pallas_call(
        finish_kernel,
        out_shape=jax.ShapeDtypeStruct((64, 16, 128), F32),
        in_specs=[smem, smem] + [vmem] * (len(ins) - 2),
        out_specs=vmem,
        scratch_shapes=[
            pltpu.VMEM((64, 40, 128), F32),
            pltpu.VMEM((64, 40, 128), F32),
            pltpu.VMEM((64, 40, 128), F32),
            pltpu.VMEM((8, 32, 1024), F32),
            pltpu.VMEM((8, 80, 128), F32),
            pltpu.VMEM((8, 80, 128), F32),
            pltpu.VMEM((8, 64, 128), F32),
            pltpu.VMEM((2, 48, 128), F32),
            pltpu.VMEM((2, 32, 128), F32),
            pltpu.VMEM((1, 32, 128), F32),
            pltpu.VMEM((1, 32, 128), F32),
            pltpu.VMEM((8, 32, 128), F32),
        ]
        + COUPLINGS,
        compiler_params=VMEM,
    )(*ins)


def exchange(value, axes, dim, width, order=None):
    order = order or list(range(8))
    up = [(order[i], order[i + 1]) for i in range(7)]
    down = [(j, i) for i, j in up]
    length = value.shape[dim]
    before = lax.ppermute(lax.slice_in_dim(value, length - width, length, axis=dim), axes, up)
    after = lax.ppermute(lax.slice_in_dim(value, 0, width, axis=dim), axes, down)
    return before, after


def local(
    orbitals, local_potential, occupations, proj_values, proj_strength, atom_block, atom_offset
):
    core, xlo, ylo = (lax.axis_index(a) for a in GROUP)
    slab = 2 * (xlo * (3 - ylo) + (1 - xlo) * ylo) + core
    lists, strength = atom_lists(slab, proj_strength, atom_block, atom_offset)
    high, low = coupling(HALF)
    mats = (jnp.asarray(high), jnp.asarray(low))

    packed = pack(orbitals, local_potential)
    tiles = projector_tiles(proj_values)
    own = lax.all_to_all(packed, PLANE, 0, 0, tiled=True)

    sigma = HALF_WIDTH / (0.0 - CENTER)
    tau = 2.0 / sigma
    coefs = [(sigma / HALF_WIDTH, 0.0)]
    for _ in range(DEGREE - 1):
        following = 1.0 / (tau - sigma)
        coefs.append((2.0 * following / HALF_WIDTH, sigma * following))
        sigma = following
    older = pot = None
    for k in range(0, DEGREE, 2):
        first, last = k == 0, k == DEGREE - 2
        halo = exchange(own, GROUP, 1, own.shape[1], SLAB_DEVICE)
        outs = list(
            double_step(
                first, last, coefs[k], coefs[k + 1], lists, strength, halo, own, older, pot, tiles, mats
            )
        )
        own = outs.pop(0)
        if first:
            pot = outs.pop(0)
        if not last:
            older = outs.pop(0)

    scalars = jnp.stack([slab, 2 * lax.axis_index("yhi") + lax.axis_index("xhi")]).astype(jnp.int32)
    halo = exchange(own, GROUP, 1, 8, SLAB_DEVICE)
    sent = source_step(scalars, occupations, own)
    got = lax.all_to_all(sent, GROUP, 0, 0, tiled=True)
    packed = finish_step(scalars, occupations, got, halo, own)
    back = lax.all_to_all(packed, PLANE, 0, 0, tiled=True)
    filtered, part = unpack(back)
    hartree = jnp.sum(lax.all_to_all(part, BAND, 0, 0, tiled=True), axis=0)
    return filtered.reshape(8, 8, 8, 128), hartree.reshape(8, 8, 128)


def solution(mesh):
    fine = Mesh(
        mesh.devices.reshape(8, 4, 2, 2, 2, 2), (BAND, "yhi", "core", "xhi", "xlo", "ylo")
    )
    bands, grid = P(BAND, GX, GYZ, None), P(GX, GYZ, None)
    return jax.shard_map(
        local,
        mesh=fine,
        in_specs=(bands, grid, P(BAND), P(), P(), P(), P()),
        out_specs=(bands, grid),
        check_vma=False,
    )
```

```python
import functools

import jax
import jax.numpy as jnp
import numpy as np
from jax import lax
from jax.experimental import pallas as pl
from jax.experimental.pallas import tpu as pltpu
from jax.sharding import Mesh
from jax.sharding import PartitionSpec as P

DEGREE = 8
POST = 2
COARSE = 4
STENCIL = (
    -5369.0 / 1800.0,
    12.0 / 7.0,
    -15.0 / 56.0,
    10.0 / 189.0,
    -1.0 / 112.0,
    2.0 / 1925.0,
    -1.0 / 16632.0,
)
HALF = tuple(-0.5 * c for c in STENCIL)
REACH = 6
CENTER = 12.0
HALF_WIDTH = 8.0
DAMPING = 0.8
BAND = "z"
GX = ("yhi", "core")
GYZ = ("xhi", "xlo", "ylo")
PLANE = GX + GYZ
GROUP = ("core", "xlo", "ylo")
CHIPS = ((0, 0), (0, 1), (1, 1), (1, 0))
SLAB_DEVICE = [c * 4 + xl * 2 + yl for xl, yl in CHIPS for c in (0, 1)]
VMEM = pltpu.CompilerParams(vmem_limit_bytes=12 * 1024 * 1024)
HEAD = 3
F32 = jnp.float32
BF16 = jnp.bfloat16


def plane_index(band, slab):
    yhi, xhi = band // 2, band % 2
    xlo, ylo = CHIPS[slab // 2]
    return yhi * 16 + (slab % 2) * 8 + xhi * 4 + xlo * 2 + ylo


def coupling(weights):
    own, xu, xd, yu, yd = (np.zeros((128, 128)) for _ in range(5))
    for zh in range(2):
        for xi in range(8):
            for yi in range(8):
                i = zh * 64 + xi * 8 + yi
                for o in range(8):
                    for m, k in ((own, abs(o - xi)), (xu, o + 8 - xi), (xd, xi + 8 - o)):
                        if 1 <= k < len(weights):
                            m[i, zh * 64 + o * 8 + yi] += weights[k]
                    for m, k in ((own, abs(o - yi)), (yu, o + 8 - yi), (yd, yi + 8 - o)):
                        if 1 <= k < len(weights):
                            m[i, zh * 64 + xi * 8 + o] += weights[k]
    whole = np.concatenate([own, xu, xd, yu, yd], axis=1).astype(np.float32)
    high = whole.astype(jnp.bfloat16)
    low = (whole - high.astype(np.float32)).astype(jnp.bfloat16)
    return high, low


def halves(x, axis):
    high = x.astype(BF16)
    return jnp.concatenate([high, (x - high.astype(F32)).astype(BF16)], axis=axis)


def lanes_low(shape):
    return lax.broadcasted_iota(jnp.int32, shape, len(shape) - 1) < 64


def dot2(x, m):
    return jnp.dot(halves(x, 1), jnp.concatenate([m, m], axis=0), preferred_element_type=F32)


def swap(x):
    return pltpu.roll(x, 64, x.ndim - 1)


def split3(x):
    a = x.astype(BF16)
    r = x - a.astype(F32)
    b = r.astype(BF16)
    c = (r - b.astype(F32)).astype(BF16)
    return a, b, c


def pack_kernel(orb_ref, pot_ref, out_ref):
    low = lanes_low((8, 128))
    for q in range(4):
        turned = orb_ref[q * 128 : (q + 1) * 128, :].T
        for s in range(8):
            a = turned[s * 16 : s * 16 + 8, :]
            b = turned[s * 16 + 8 : s * 16 + 16, :]
            out_ref[plane_index(2 * q, s), 0:8, :] = jnp.where(low, a, swap(b))
            out_ref[plane_index(2 * q + 1, s), 0:8, :] = jnp.where(low, swap(a), b)
    pot = pot_ref[...]
    turned = jnp.concatenate([pot, pot], axis=0).T
    for s in range(8):
        piece = jnp.where(low, turned[s * 16 : s * 16 + 8, :], turned[s * 16 + 8 : s * 16 + 16, :])
        for b in range(8):
            out_ref[plane_index(b, s), 8:16, :] = piece


def pack(orbitals, potential):
    return pl.pallas_call(
        pack_kernel,
        out_shape=jax.ShapeDtypeStruct((64, 16, 128), F32),
        compiler_params=VMEM,
    )(orbitals.reshape(512, 128), potential.reshape(64, 128))


def tiles_kernel(proj_ref, pick_ref, tiles_ref):
    low = lanes_low((8, 2, 8, 128))
    keep = lax.broadcasted_iota(jnp.int32, (4, 8, 512), 2) % 8 == lax.broadcasted_iota(
        jnp.int32, (4, 8, 512), 1
    )

    def body(i, carry):
        parts = [
            jnp.where(keep, proj_ref[i * 8 + u][:, None, :], 0.0).reshape(32, 512)
            for u in range(8)
        ]
        spread = jnp.concatenate(parts, axis=0)
        pick = pick_ref[...]
        total = sum(jnp.dot(part, pick, preferred_element_type=F32) for part in split3(spread))
        total = total.reshape(8, 2, 2, 8, 128)
        tiles_ref[pl.ds(i * 8, 8), :, :, :] = jnp.where(low, total[:, :, 0], total[:, :, 1])
        return carry

    lax.fori_loop(0, 8, body, 0)


def projector_tiles(proj):
    pick = (np.arange(512)[:, None] // 8 == np.arange(128)[None, :] % 64).astype(jnp.bfloat16)
    return pl.pallas_call(
        tiles_kernel,
        out_shape=jax.ShapeDtypeStruct((64, 2, 8, 128), F32),
        compiler_params=VMEM,
    )(proj, pick)


def keep_couplings(couplings, t, y):
    y = y.reshape(64, 8, 640)
    for e, ref in enumerate(couplings):
        ref[t] = y[:, :, e * 128 : e * 128 + 128]


def xy_sum(couplings, t, src):
    own, from_x, to_x, from_y, to_y = couplings
    total = own[t, src]
    if src >= 8:
        total = total + from_x[t, src - 8]
    if src < 56:
        total = total + to_x[t, src + 8]
    if src % 8 > 0:
        total = total + from_y[t, src - 1]
    if src % 8 < 7:
        total = total + to_y[t, src + 1]
    return total


ID, SRC, ROW, UPPER, ROW_L, ON_L, ROW_U, ON_U, META = range(9)


def double_kernel(
    first, last, coef1, coef2, lists, strength, prev_ref, own_ref, next_ref, *refs
):
    refs = list(refs)
    if first:
        older_ref = pot_ref = None
    else:
        older_ref, pot_ref = refs.pop(0), refs.pop(0)
    tiles_ref, mat_ref, mat_low_ref = refs[:3]
    refs = refs[3:]
    out_ref = refs.pop(0)
    if first:
        pot_ref = refs.pop(0)
    mid_ref = None if last else refs.pop(0)
    ext, mid, new, *couplings, weights = refs
    low = lanes_low((8, 128))
    count = lists[META, 0]
    below = lists[META, 1] > 0
    above = lists[META, 2] > 0
    zero8 = jnp.zeros((8, 128), F32)

    def fill():
        for src in range(64):
            p, o, n = prev_ref[src, 0:8, :], own_ref[src, 0:8, :], next_ref[src, 0:8, :]
            ext[src, 0:8, :] = p
            ext[src, 8:16, :] = swap(jnp.where(low, o, p))
            ext[src, 16:24, :] = o
            ext[src, 24:32, :] = swap(jnp.where(low, n, o))
            ext[src, 32:40, :] = n
            if first:
                p, o, n = prev_ref[src, 8:16, :], own_ref[src, 8:16, :], next_ref[src, 8:16, :]
                shift = 3.0 * HALF[0] - CENTER
                pot_ref[src, 0:8, :] = swap(jnp.where(low, o, p)) + shift
                pot_ref[src, 8:16, :] = o + shift
                pot_ref[src, 16:24, :] = swap(jnp.where(low, n, o)) + shift

    fill()

    def products(f_ref, tiles):
        for t in tiles:
            x = halves(f_ref[:, t * 8 + 8 : t * 8 + 16, :].reshape(512, 128), 1)
            m = mat_ref[...]
            y = jnp.dot(x, jnp.concatenate([m, m], axis=0), preferred_element_type=F32)
            y = y + jnp.dot(x[:, 0:128], mat_low_ref[...], preferred_element_type=F32)
            keep_couplings(couplings, t, y)

    def project(f_ref):
        def chunk(i):
            found = []
            for u in range(8):
                ii = i * 8 + u
                w = f_ref[lists[SRC, ii], pl.ds(lists[ROW, ii], 8), :]
                w = jnp.where(low == (lists[UPPER, ii] == 0), w, 0.0)
                w = w + swap(w)
                found.append(jnp.sum(tiles_ref[lists[ID, ii]] * w[None], axis=1))
            return jnp.concatenate(found, axis=0)

        i, o = lane_pairs(128, 128)
        same_half = filled(i // 64 == o // 64, 1.0)
        head = jnp.concatenate([chunk(i) for i in range(HEAD)], axis=0)
        weights[0 : HEAD * 16, :] = dot2(head, same_half)

        def body(i, carry):
            weights[pl.ds(pl.multiple_of(i * 16, 16), 16), :] = dot2(chunk(i), same_half)
            return carry

        lax.fori_loop(HEAD, (count + 7) // 8, body, 0)

    def combine(f_ref, y_ref, older, tiles, coef):
        a, b = coef

        for src in range(64):
            rows = {}
            for t in tiles:
                for o in range(t * 8 + 8 - REACH, t * 8 + 9 + REACH):
                    if o not in rows:
                        rows[o] = f_ref[src, o : o + 8, :]
            for t in tiles:
                r = t * 8 + 8
                total = xy_sum(couplings, t, src)
                for k in range(1, REACH + 1):
                    total = total + HALF[k] * (rows[r + k] + rows[r - k])
                total = a * (total + pot_ref[src, t * 8 : t * 8 + 8, :] * rows[r])
                if older is not None:
                    total = total - b * older(src, t)
                if t == 0:
                    total = jnp.where(jnp.logical_or(below, jnp.logical_not(low)), total, 0.0)
                if t == 2:
                    total = jnp.where(jnp.logical_or(above, low), total, 0.0)
                y_ref[src, r : r + 8, :] = total

    def spread(y_ref, a):
        low_row = lanes_low((1, 128))

        def term(i, u, w):
            ii = i * 8 + u
            atom = lists[ID, ii]
            t = zero8
            for q in range(2):
                scale = jnp.where(low_row, strength[2 * q, ii] * a, strength[2 * q + 1, ii] * a)
                t = t + (scale * w[u * 2 + q : u * 2 + q + 1, :]) * tiles_ref[atom, q]
            return t + swap(t)

        def add(i, u, t):
            ii = i * 8 + u
            src = lists[SRC, ii]
            rows = pl.ds(lists[ROW_L, ii], 8)
            on = jnp.logical_and(low, lists[ON_L, ii] > 0)
            y_ref[src, rows, :] = y_ref[src, rows, :] + jnp.where(on, t, 0.0)
            rows = pl.ds(lists[ROW_U, ii], 8)
            on = jnp.logical_and(jnp.logical_not(low), lists[ON_U, ii] > 0)
            y_ref[src, rows, :] = y_ref[src, rows, :] + jnp.where(on, t, 0.0)

        for i in range(HEAD):
            w = weights[i * 16 : i * 16 + 16, :]
            terms = [term(i, u, w) for u in range(8)]
            for u in range(8):
                add(i, u, terms[u])

        def body(i, carry):
            w = weights[pl.ds(pl.multiple_of(i * 16, 16), 16), :]
            terms = [term(i, u, w) for u in range(8)]
            for u in range(8):
                add(i, u, terms[u])
            return carry

        lax.fori_loop(HEAD, (count + 7) // 8, body, 0)

    products(ext, range(3))
    project(ext)
    older = None if first else (lambda src, t: older_ref[src, t * 8 : t * 8 + 8, :])
    combine(ext, mid, older, (0, 1, 2), coef1)
    spread(mid, coef1[0])
    products(mid, (1,))
    project(mid)
    combine(mid, new, lambda src, t: ext[src, 16:24, :], (1,), coef2)
    spread(new, coef2[0])
    out_ref[...] = new[:, 16:24, :]
    if not last:
        mid_ref[...] = mid[:, 8:32, :]


def double_step(first, last, coef1, coef2, lists, strength, halo, own, older, pot, tiles, mats):
    smem = pl.BlockSpec(memory_space=pltpu.SMEM)
    vmem = pl.BlockSpec(memory_space=pltpu.VMEM)
    ins = [lists, strength, halo[0], own, halo[1]]
    if not first:
        ins += [older, pot]
    ins += [tiles, *mats]
    outs = [jax.ShapeDtypeStruct((64, 8, 128), F32)]
    if first:
        outs.append(jax.ShapeDtypeStruct((64, 24, 128), F32))
    if not last:
        outs.append(jax.ShapeDtypeStruct((64, 24, 128), F32))
    return pl.pallas_call(
        functools.partial(double_kernel, first, last, coef1, coef2),
        out_shape=tuple(outs),
        in_specs=[smem, smem] + [vmem] * (len(ins) - 2),
        out_specs=tuple([vmem] * len(outs)),
        scratch_shapes=[
            pltpu.VMEM((64, 40, 128), F32),
            pltpu.VMEM((64, 40, 128), F32),
            pltpu.VMEM((64, 40, 128), F32),
            *[pltpu.VMEM((3, 64, 8, 128), F32)] * 5,
            pltpu.VMEM((128, 128), F32),
        ],
        compiler_params=VMEM,
    )(*ins)


def atom_lists(slab, proj_strength, atom_block, atom_offset):
    number = jnp.arange(64, dtype=jnp.int32)
    dz = atom_offset[:, 2] - 16 * slab
    near = jnp.logical_and(dz >= -15, dz <= 23)
    before = jnp.sum(
        jnp.logical_and(near[None, :], number[None, :] < number[:, None]).astype(jnp.int32), axis=1
    )
    pick = jnp.logical_and(near[None, :], before[None, :] == number[:, None])

    def listed(values, empty):
        return jnp.sum(jnp.where(pick, values[None, :], 0), axis=1) + jnp.where(
            jnp.any(pick, axis=1), 0, empty
        )

    at = listed(dz, 0)
    valid = jnp.any(pick, axis=1)
    source = listed(jnp.clip(atom_block, 0, 63), 0)
    upper = at > 8
    meta = jnp.zeros((64,), jnp.int32).at[0].set(jnp.sum(near.astype(jnp.int32)))
    meta = meta.at[1].set(slab).at[2].set(7 - slab)
    lists = jnp.stack(
        [
            listed(number, 0),
            source,
            jnp.where(upper, at - 8, at) + 16,
            upper.astype(jnp.int32),
            jnp.clip(at, -16, 16) + 16,
            jnp.logical_and(valid, at <= 15).astype(jnp.int32),
            jnp.clip(at - 8, -16, 16) + 16,
            jnp.logical_and(valid, at >= -7).astype(jnp.int32),
            meta,
        ]
    )
    strength = jnp.sum(jnp.where(pick[None], proj_strength.T[:, None, :], 0.0), axis=2)
    return lists, strength


def unpack_kernel(in_ref, out_ref, hartree_ref):
    low = lanes_low((8, 128))

    def block(pairs):
        rows = []
        for a, b in pairs:
            rows += [jnp.where(low, a, swap(b)), jnp.where(low, swap(a), b)]
        return jnp.concatenate(rows, axis=0).T

    for q in range(4):
        out_ref[q * 128 : (q + 1) * 128, :] = block(
            [
                (in_ref[plane_index(2 * q, s), 0:8, :], in_ref[plane_index(2 * q + 1, s), 0:8, :])
                for s in range(8)
            ]
        )
    pairs = []
    for s in range(8):
        total = in_ref[plane_index(0, s), 8:16, :]
        for b in range(1, 8):
            total = total + in_ref[plane_index(b, s), 8:16, :]
        pairs.append((total, total))
    part = block(pairs)[0:64, :]
    for e in range(8):
        hartree_ref[e] = part


def unpack(slabs):
    return pl.pallas_call(
        unpack_kernel,
        out_shape=(
            jax.ShapeDtypeStruct((512, 128), F32),
            jax.ShapeDtypeStruct((8, 64, 128), F32),
        ),
        compiler_params=VMEM,
    )(slabs)


OMEGA = DAMPING / 6.0


def lane_pairs(rows, columns):
    shape = (rows, columns)
    return lax.broadcasted_iota(jnp.int32, shape, 0), lax.broadcasted_iota(jnp.int32, shape, 1)


def filled(where, value):
    return jnp.where(where, value, 0.0).astype(BF16)


def both(*conditions):
    return functools.reduce(jnp.logical_and, conditions)


def transfers(fine_x, fine_y, down):
    fine, coarse = fine_x * fine_y, 128
    i, o = lane_pairs(fine, coarse) if down else lane_pairs(coarse, fine)
    f, c = (i, o) if down else (o, i)
    same = both(
        (f // fine_y) // 2 == c // (fine_y // 2), (f % fine_y) // 2 == c % (fine_y // 2)
    )
    return filled(same, 0.5 if down else 1.0)


def beside(nx, ny, used):
    i, o = lane_pairs(128, 128)
    dx, dy = o // ny - i // ny, o % ny - i % ny
    parts = [filled(both(jnp.abs(dx) + jnp.abs(dy) == 1, i // ny < used, o // ny < used), 1.0)]
    if used == nx:
        parts += [filled(both(dx == d, dy == 0), 1.0) for d in (1 - nx, nx - 1)]
    return jnp.concatenate(parts, axis=1)


def block_neighbours():
    i, o = lane_pairs(128, 128)
    half = i // 64 == o // 64
    dx, dy = (o // 8) % 8 - (i // 8) % 8, o % 8 - i % 8
    parts = [both(half, jnp.abs(dx) + jnp.abs(dy) == 1)]
    parts += [both(half, dx == d, dy == 0) for d in (-7, 7)]
    parts += [both(half, dx == 0, dy == d) for d in (-7, 7)]
    return jnp.concatenate([filled(p, 1.0) for p in parts], axis=1)


COUPLINGS = [pltpu.VMEM((2, 64, 8, 128), F32)] * 5


def inside_slab_range(slab, r):
    z = (
        lax.broadcasted_iota(jnp.int32, (8, 128), 0)
        + jnp.where(lanes_low((8, 128)), 0, 8)
        + (16 * slab + (r - 16))
    )
    return jnp.logical_and(z >= 0, z < 128)


def relax(ref, rows, mat, couplings, update):
    for t, r in enumerate(rows):
        keep_couplings(couplings, t, dot2(ref[:, r : r + 8, :].reshape(512, 128), mat))
    for src in range(64):
        for t, r in enumerate(rows):
            near = xy_sum(couplings, t, src)
            near = near + ref[src, r - 1 : r + 7, :] + ref[src, r + 1 : r + 9, :]
            update(src, r, ref[src, r : r + 8, :], near)


def source_kernel(scalars, occ, own_ref, sent_ref, v, w, r0, *couplings):
    mat = block_neighbours()
    low = lanes_low((8, 128))
    slab, occupation = scalars[0], occ[scalars[1]] / 64.0
    zero = jnp.zeros((8, 128), F32)

    def fill():
        for src in range(64):
            y = own_ref[src]
            o = OMEGA * (occupation * y * y)
            v[src, 0:8, :] = zero
            v[src, 8:16, :] = swap(jnp.where(low, o, 0.0))
            v[src, 16:24, :] = o
            v[src, 24:32, :] = swap(jnp.where(low, 0.0, o))
            v[src, 32:40, :] = zero
            w[src, 8:16, :] = zero
            w[src, 24:32, :] = zero

    fill()
    keep = {r: inside_slab_range(slab, r) for r in (13, 19)}

    def second(src, r, c, near):
        w[src, r : r + 8, :] = jnp.where(keep[r], 1.2 * c + OMEGA * near, 0.0)

    def residual(src, r, c, near):
        r0[src, r : r + 8, :] = v[src, r : r + 8, :] * (1.0 / OMEGA) - 6.0 * c + near

    relax(v, (13, 19), mat, couplings, second)
    relax(w, (14, 18), mat, couplings, residual)
    rows = []
    for xb in range(8):
        parts = []
        for yb in range(8):
            src = xb * 8 + yb
            parts.append(r0[src, pl.ds(14, 8, stride=2), :] + r0[src, pl.ds(15, 8, stride=2), :])
        rows.append(jnp.concatenate(parts, axis=1))
    summed = jnp.concatenate(rows, axis=0)

    i = lax.broadcasted_iota(jnp.int32, (128, 256), 0)
    o = lax.broadcasted_iota(jnp.int32, (128, 256), 1)
    apart = (o // 128) * 1000 + o % 128 - (i // 64) * 1000 - ((i // 16) % 4) * 32 - (i % 8) // 2
    down = [jnp.where(apart == 4 * yb, 0.5, 0.0).astype(BF16) for yb in range(8)]
    coarse = jnp.dot(
        halves(summed, 0), jnp.concatenate(down, axis=0), preferred_element_type=F32
    )
    coarse = coarse[0:64] + coarse[64:128]
    below, above = [], []
    own = []
    for xb in range(8):
        part = coarse[xb * 8 : xb * 8 + 8]
        own.append(part[1:5, 0:128])
        own.append(part[1:5, 128:256])
        below.append(part[0:1, 0:128])
        above.append(part[5:6, 128:256])
    sent = jnp.concatenate(own + below + above, axis=0)
    for e in range(8):
        sent_ref[e] = sent


def source_step(scalars, occupations, own):
    smem = pl.BlockSpec(memory_space=pltpu.SMEM)
    vmem = pl.BlockSpec(memory_space=pltpu.VMEM)
    return pl.pallas_call(
        source_kernel,
        out_shape=jax.ShapeDtypeStruct((8, 80, 128), F32),
        in_specs=[smem, smem, vmem],
        out_specs=vmem,
        scratch_shapes=[pltpu.VMEM((64, 40, 128), F32)] * 3 + COUPLINGS,
        compiler_params=VMEM,
    )(scalars, occupations, own)


def double_rows(scratch, value, n):
    scratch[:, pl.ds(0, n, stride=2), :] = value
    scratch[:, pl.ds(1, n, stride=2), :] = value


def coarse_solve(g, v, r1, v2, r2, v3, r3):
    near1, near2, near3 = beside(4, 32, 4), beside(8, 16, 8), beside(16, 8, 8)

    def near(ref, blocks, planes, mat):
        rows = ref[:, 8 : 8 + planes, :]
        y = dot2(rows.reshape(blocks * planes, 128), mat)
        y = y.reshape(blocks, planes, -1)
        total = y[:, :, 0:128] + ref[:, 7 : 7 + planes, :] + ref[:, 9 : 9 + planes, :]
        if blocks > 1:
            none = jnp.zeros((1, planes, 128), F32)
            total = total + jnp.concatenate([none, y[:-1, :, 128:256]], axis=0)
            total = total + jnp.concatenate([y[1:, :, 256:384], none], axis=0)
        return rows, total

    def sweep(ref, source, blocks, planes, mat):
        rows, total = near(ref, blocks, planes, mat)
        ref[:, 8 : 8 + planes, :] = rows + OMEGA * (source() - 6.0 * rows + total)

    def residual(ref, source, blocks, planes, mat):
        rows, total = near(ref, blocks, planes, mat)
        return source() - 6.0 * rows + total

    for ref, planes in ((v, 64), (v2, 32), (v3, 16)):
        border = jnp.zeros((ref.shape[0], 8, 128), F32)
        ref[:, 0:8, :] = border
        ref[:, 8 + planes : 16 + planes, :] = border
    g1 = lambda: g[:, 8:72, :]
    v[:, 8:72, :] = OMEGA * g1()
    sweep(v, g1, 8, 64, near1)
    r1[...] = residual(v, g1, 8, 64, near1)
    pair = r1[:, pl.ds(0, 32, stride=2), :] + r1[:, pl.ds(1, 32, stride=2), :]
    rows = [jnp.concatenate([pair[4 * b + e] for e in range(4)], axis=1) for b in range(2)]
    d = jnp.dot(halves(jnp.concatenate(rows, axis=0), 0), transfers(16, 32, True), preferred_element_type=F32)
    s2 = (d[0:64] + d[64:128]).reshape(2, 32, 128)
    g2 = lambda: s2
    v2[:, 8:40, :] = OMEGA * s2
    sweep(v2, g2, 2, 32, near2)
    r2[...] = residual(v2, g2, 2, 32, near2)
    pair = r2[:, pl.ds(0, 16, stride=2), :] + r2[:, pl.ds(1, 16, stride=2), :]
    both = jnp.concatenate([pair[0], pair[1]], axis=1)
    d = jnp.dot(halves(both, 0), transfers(16, 16, True), preferred_element_type=F32)
    s3 = (d[0:16] + d[16:32]).reshape(1, 16, 128)
    g3 = lambda: s3
    v3[:, 8:24, :] = OMEGA * s3
    for _ in range(COARSE - 1):
        sweep(v3, g3, 1, 16, near3)
    double_rows(r3, v3[:, 8:24, :], 16)
    up = dot2(r3[0], transfers(16, 16, False))
    for b in range(2):
        v2[b, 8:40, :] = v2[b, 8:40, :] + up[:, b * 128 : b * 128 + 128]
    for _ in range(POST):
        sweep(v2, g2, 2, 32, near2)
    double_rows(r1.at[0:2], v2[:, 8:40, :], 32)
    up = dot2(r1[0:2].reshape(128, 128), transfers(16, 32, False))
    for b in range(8):
        part = up[(b // 4) * 64 : (b // 4) * 64 + 64, (b % 4) * 128 : (b % 4) * 128 + 128]
        v[b, 8:72, :] = v[b, 8:72, :] + part
    for _ in range(POST):
        sweep(v, g1, 8, 64, near1)


def finish_kernel(scalars, occ, got_ref, prev_ref, y_ref, next_ref, *refs):
    mat = block_neighbours()
    out_ref = refs[0]
    fx, va, vb, up, g, v, r1, v2, r2, v3, r3, wide = refs[1:13]
    couplings = refs[13:]
    low = lanes_low((8, 128))
    slab, factor = scalars[0], OMEGA * (occ[scalars[1]] / 64.0)

    for s in range(8):
        g[:, 8 + 8 * s : 16 + 8 * s, :] = got_ref[SLAB_DEVICE[s], 0:64, :].reshape(8, 8, 128)
    for s in range(8):
        for xb in range(8):
            if s > 0:
                row = 8 + 8 * s - 1
                g[xb, row : row + 1, :] = g[xb, row : row + 1, :] + got_ref[SLAB_DEVICE[s], 64 + xb : 65 + xb, :]
            if s < 7:
                row = 8 + 8 * s + 8
                g[xb, row : row + 1, :] = g[xb, row : row + 1, :] + got_ref[SLAB_DEVICE[s], 72 + xb : 73 + xb, :]
    coarse_solve(g, v, r1, v2, r2, v3, r3)
    double_rows(wide, v[:, pl.ds(8 * slab + 4, 16), :], 16)
    i = lax.broadcasted_iota(jnp.int32, (128, 128), 0)
    o = lax.broadcasted_iota(jnp.int32, (128, 128), 1)
    apart = i - ((o // 16) % 4) * 32 - (o % 8) // 2
    spread = jnp.concatenate(
        [jnp.where(apart == 4 * yb, 1.0, 0.0).astype(BF16) for yb in range(8)], axis=1
    )
    up[...] = dot2(wide[...].reshape(256, 128), spread).reshape(8, 32, 1024)

    def fill():
        for src in range(64):
            p, o, n = (factor * jnp.square(ref[src]) for ref in (prev_ref, y_ref, next_ref))
            fx[src, 8:16, :] = swap(jnp.where(low, o, p))
            fx[src, 16:24, :] = o
            fx[src, 24:32, :] = swap(jnp.where(low, n, o))
            out_ref[src, 0:8, :] = y_ref[src]

    fill()
    keep = {r: inside_slab_range(slab, r) for r in (14, 18, 15, 17)}

    def second(src, r, c, near):
        va[src, r : r + 8, :] = jnp.where(keep[r], 1.2 * c + OMEGA * near, 0.0)

    def add_up():
        for src in range(64):
            xb, lanes = src // 8, slice(src % 8 * 128, src % 8 * 128 + 128)
            for r, n in ((14, 8), (22, 4)):
                e = jnp.where(
                    lanes_low((n, 128)), up[xb, r - 8 : r - 8 + n, lanes], up[xb, r : r + n, lanes]
                )
                va[src, r : r + n, :] = va[src, r : r + n, :] + e

    def swept(src, r, c, near):
        return c + (fx[src, r : r + 8, :] - DAMPING * c + OMEGA * near)

    def fourth(src, r, c, near):
        vb[src, r : r + 8, :] = jnp.where(keep[r], swept(src, r, c, near), 0.0)

    def fifth(src, r, c, near):
        out_ref[src, 8:16, :] = swept(src, r, c, near)

    relax(fx, (14, 18), mat, couplings, second)
    add_up()
    relax(va, (15, 17), mat, couplings, fourth)
    relax(vb, (16,), mat, couplings, fifth)


def finish_step(scalars, occupations, got, halo, own):
    smem = pl.BlockSpec(memory_space=pltpu.SMEM)
    vmem = pl.BlockSpec(memory_space=pltpu.VMEM)
    ins = [scalars, occupations, got, halo[0], own, halo[1]]
    return pl.pallas_call(
        finish_kernel,
        out_shape=jax.ShapeDtypeStruct((64, 16, 128), F32),
        in_specs=[smem, smem] + [vmem] * (len(ins) - 2),
        out_specs=vmem,
        scratch_shapes=[
            pltpu.VMEM((64, 40, 128), F32),
            pltpu.VMEM((64, 40, 128), F32),
            pltpu.VMEM((64, 40, 128), F32),
            pltpu.VMEM((8, 32, 1024), F32),
            pltpu.VMEM((8, 80, 128), F32),
            pltpu.VMEM((8, 80, 128), F32),
            pltpu.VMEM((8, 64, 128), F32),
            pltpu.VMEM((2, 48, 128), F32),
            pltpu.VMEM((2, 32, 128), F32),
            pltpu.VMEM((1, 32, 128), F32),
            pltpu.VMEM((1, 32, 128), F32),
            pltpu.VMEM((8, 32, 128), F32),
        ]
        + COUPLINGS,
        compiler_params=VMEM,
    )(*ins)


def exchange(value, axes, dim, width, order=None):
    order = order or list(range(8))
    up = [(order[i], order[i + 1]) for i in range(7)]
    down = [(j, i) for i, j in up]
    length = value.shape[dim]
    before = lax.ppermute(lax.slice_in_dim(value, length - width, length, axis=dim), axes, up)
    after = lax.ppermute(lax.slice_in_dim(value, 0, width, axis=dim), axes, down)
    return before, after


def local(
    orbitals, local_potential, occupations, proj_values, proj_strength, atom_block, atom_offset
):
    core, xlo, ylo = (lax.axis_index(a) for a in GROUP)
    slab = 2 * (xlo * (3 - ylo) + (1 - xlo) * ylo) + core
    lists, strength = atom_lists(slab, proj_strength, atom_block, atom_offset)
    high, low = coupling(HALF)
    mats = (jnp.asarray(high), jnp.asarray(low))

    packed = pack(orbitals, local_potential)
    tiles = projector_tiles(proj_values)
    own = lax.all_to_all(packed, PLANE, 0, 0, tiled=True)

    sigma = HALF_WIDTH / (0.0 - CENTER)
    tau = 2.0 / sigma
    coefs = [(sigma / HALF_WIDTH, 0.0)]
    for _ in range(DEGREE - 1):
        following = 1.0 / (tau - sigma)
        coefs.append((2.0 * following / HALF_WIDTH, sigma * following))
        sigma = following
    older = pot = None
    for k in range(0, DEGREE, 2):
        first, last = k == 0, k == DEGREE - 2
        halo = exchange(own, GROUP, 1, own.shape[1], SLAB_DEVICE)
        outs = list(
            double_step(
                first, last, coefs[k], coefs[k + 1], lists, strength, halo, own, older, pot, tiles, mats
            )
        )
        own = outs.pop(0)
        if first:
            pot = outs.pop(0)
        if not last:
            older = outs.pop(0)

    scalars = jnp.stack([slab, 2 * lax.axis_index("yhi") + lax.axis_index("xhi")]).astype(jnp.int32)
    halo = exchange(own, GROUP, 1, 8, SLAB_DEVICE)
    sent = source_step(scalars, occupations, own)
    got = lax.all_to_all(sent, GROUP, 0, 0, tiled=True)
    packed = finish_step(scalars, occupations, got, halo, own)
    back = lax.all_to_all(packed, PLANE, 0, 0, tiled=True)
    filtered, part = unpack(back)
    hartree = jnp.sum(lax.all_to_all(part, BAND, 0, 0, tiled=True), axis=0)
    return filtered.reshape(8, 8, 8, 128), hartree.reshape(8, 8, 128)


def solution(mesh):
    fine = Mesh(
        mesh.devices.reshape(8, 4, 2, 2, 2, 2), (BAND, "yhi", "core", "xhi", "xlo", "ylo")
    )
    bands, grid = P(BAND, GX, GYZ, None), P(GX, GYZ, None)
    return jax.shard_map(
        local,
        mesh=fine,
        in_specs=(bands, grid, P(BAND), P(), P(), P(), P()),
        out_specs=(bands, grid),
        check_vma=False,
    )
```

```python
import functools

import jax
import jax.numpy as jnp
import numpy as np
from jax import lax
from jax.experimental import pallas as pl
from jax.experimental.pallas import tpu as pltpu
from jax.sharding import Mesh
from jax.sharding import PartitionSpec as P

DEGREE = 8
POST = 2
COARSE = 4
STENCIL = (
    -5369.0 / 1800.0,
    12.0 / 7.0,
    -15.0 / 56.0,
    10.0 / 189.0,
    -1.0 / 112.0,
    2.0 / 1925.0,
    -1.0 / 16632.0,
)
HALF = tuple(-0.5 * c for c in STENCIL)
REACH = 6
CENTER = 12.0
HALF_WIDTH = 8.0
DAMPING = 0.8
BAND = "z"
GX = ("yhi", "core")
GYZ = ("xhi", "xlo", "ylo")
PLANE = GX + GYZ
GROUP = ("core", "xlo", "ylo")
CHIPS = ((0, 0), (0, 1), (1, 1), (1, 0))
SLAB_DEVICE = [c * 4 + xl * 2 + yl for xl, yl in CHIPS for c in (0, 1)]
VMEM = pltpu.CompilerParams(vmem_limit_bytes=12 * 1024 * 1024)
HEAD = 3
F32 = jnp.float32
BF16 = jnp.bfloat16


def plane_index(band, slab):
    yhi, xhi = band // 2, band % 2
    xlo, ylo = CHIPS[slab // 2]
    return yhi * 16 + (slab % 2) * 8 + xhi * 4 + xlo * 2 + ylo


def coupling(weights):
    own, xu, xd, yu, yd = (np.zeros((128, 128)) for _ in range(5))
    for zh in range(2):
        for xi in range(8):
            for yi in range(8):
                i = zh * 64 + xi * 8 + yi
                for o in range(8):
                    for m, k in ((own, abs(o - xi)), (xu, o + 8 - xi), (xd, xi + 8 - o)):
                        if 1 <= k < len(weights):
                            m[i, zh * 64 + o * 8 + yi] += weights[k]
                    for m, k in ((own, abs(o - yi)), (yu, o + 8 - yi), (yd, yi + 8 - o)):
                        if 1 <= k < len(weights):
                            m[i, zh * 64 + xi * 8 + o] += weights[k]
    whole = np.concatenate([own, xu, xd, yu, yd], axis=1).astype(np.float32)
    high = whole.astype(jnp.bfloat16)
    low = (whole - high.astype(np.float32)).astype(jnp.bfloat16)
    return high, low


def halves(x, axis):
    high = x.astype(BF16)
    return jnp.concatenate([high, (x - high.astype(F32)).astype(BF16)], axis=axis)


def lanes_low(shape):
    return lax.broadcasted_iota(jnp.int32, shape, len(shape) - 1) < 64


def dot2(x, m):
    return jnp.dot(halves(x, 1), jnp.concatenate([m, m], axis=0), preferred_element_type=F32)


def swap(x):
    return pltpu.roll(x, 64, x.ndim - 1)


def split3(x):
    a = x.astype(BF16)
    r = x - a.astype(F32)
    b = r.astype(BF16)
    c = (r - b.astype(F32)).astype(BF16)
    return a, b, c


def pack_kernel(orb_ref, pot_ref, out_ref):
    low = lanes_low((8, 128))
    for q in range(4):
        turned = orb_ref[q * 128 : (q + 1) * 128, :].T
        for s in range(8):
            a = turned[s * 16 : s * 16 + 8, :]
            b = turned[s * 16 + 8 : s * 16 + 16, :]
            out_ref[plane_index(2 * q, s), 0:8, :] = jnp.where(low, a, swap(b))
            out_ref[plane_index(2 * q + 1, s), 0:8, :] = jnp.where(low, swap(a), b)
    pot = pot_ref[...]
    turned = jnp.concatenate([pot, pot], axis=0).T
    for s in range(8):
        piece = jnp.where(low, turned[s * 16 : s * 16 + 8, :], turned[s * 16 + 8 : s * 16 + 16, :])
        for b in range(8):
            out_ref[plane_index(b, s), 8:16, :] = piece


def pack(orbitals, potential):
    return pl.pallas_call(
        pack_kernel,
        out_shape=jax.ShapeDtypeStruct((64, 16, 128), F32),
        compiler_params=VMEM,
    )(orbitals.reshape(512, 128), potential.reshape(64, 128))


def tiles_kernel(proj_ref, pick_ref, tiles_ref):
    low = lanes_low((8, 2, 8, 128))
    keep = lax.broadcasted_iota(jnp.int32, (4, 8, 512), 2) % 8 == lax.broadcasted_iota(
        jnp.int32, (4, 8, 512), 1
    )

    def body(i, carry):
        parts = [
            jnp.where(keep, proj_ref[i * 8 + u][:, None, :], 0.0).reshape(32, 512)
            for u in range(8)
        ]
        spread = jnp.concatenate(parts, axis=0)
        pick = pick_ref[...]
        total = sum(jnp.dot(part, pick, preferred_element_type=F32) for part in split3(spread))
        total = total.reshape(8, 2, 2, 8, 128)
        tiles_ref[pl.ds(i * 8, 8), :, :, :] = jnp.where(low, total[:, :, 0], total[:, :, 1])
        return carry

    lax.fori_loop(0, 8, body, 0)


def projector_tiles(proj):
    pick = (np.arange(512)[:, None] // 8 == np.arange(128)[None, :] % 64).astype(jnp.bfloat16)
    return pl.pallas_call(
        tiles_kernel,
        out_shape=jax.ShapeDtypeStruct((64, 2, 8, 128), F32),
        compiler_params=VMEM,
    )(proj, pick)


def keep_couplings(couplings, t, y):
    y = y.reshape(64, 8, 640)
    for e, ref in enumerate(couplings):
        ref[t] = y[:, :, e * 128 : e * 128 + 128]


def xy_sum(couplings, t, src):
    own, from_x, to_x, from_y, to_y = couplings
    total = own[t, src]
    if src >= 8:
        total = total + from_x[t, src - 8]
    if src < 56:
        total = total + to_x[t, src + 8]
    if src % 8 > 0:
        total = total + from_y[t, src - 1]
    if src % 8 < 7:
        total = total + to_y[t, src + 1]
    return total


ID, SRC, ROW, UPPER, ROW_L, ON_L, ROW_U, ON_U, META = range(9)


def double_kernel(
    first, last, coef1, coef2, lists, strength, prev_ref, own_ref, next_ref, *refs
):
    refs = list(refs)
    if first:
        older_ref = pot_ref = None
    else:
        older_ref, pot_ref = refs.pop(0), refs.pop(0)
    tiles_ref, mat_ref, mat_low_ref = refs[:3]
    refs = refs[3:]
    out_ref = refs.pop(0)
    if first:
        pot_ref = refs.pop(0)
    mid_ref = None if last else refs.pop(0)
    ext, mid, new, *couplings, weights = refs
    low = lanes_low((8, 128))
    count = lists[META, 0]
    below = lists[META, 1] > 0
    above = lists[META, 2] > 0
    zero8 = jnp.zeros((8, 128), F32)

    def fill():
        for src in range(64):
            p, o, n = prev_ref[src, 0:8, :], own_ref[src, 0:8, :], next_ref[src, 0:8, :]
            ext[src, 0:8, :] = p
            ext[src, 8:16, :] = swap(jnp.where(low, o, p))
            ext[src, 16:24, :] = o
            ext[src, 24:32, :] = swap(jnp.where(low, n, o))
            ext[src, 32:40, :] = n
            if first:
                p, o, n = prev_ref[src, 8:16, :], own_ref[src, 8:16, :], next_ref[src, 8:16, :]
                shift = 3.0 * HALF[0] - CENTER
                pot_ref[src, 0:8, :] = swap(jnp.where(low, o, p)) + shift
                pot_ref[src, 8:16, :] = o + shift
                pot_ref[src, 16:24, :] = swap(jnp.where(low, n, o)) + shift

    fill()

    def products(f_ref, tiles):
        for t in tiles:
            x = halves(f_ref[:, t * 8 + 8 : t * 8 + 16, :].reshape(512, 128), 1)
            m = mat_ref[...]
            y = jnp.dot(x, jnp.concatenate([m, m], axis=0), preferred_element_type=F32)
            y = y + jnp.dot(x[:, 0:128], mat_low_ref[...], preferred_element_type=F32)
            keep_couplings(couplings, t, y)

    def project(f_ref):
        def chunk(i):
            found = []
            for u in range(8):
                ii = i * 8 + u
                w = f_ref[lists[SRC, ii], pl.ds(lists[ROW, ii], 8), :]
                w = jnp.where(low == (lists[UPPER, ii] == 0), w, 0.0)
                w = w + swap(w)
                found.append(jnp.sum(tiles_ref[lists[ID, ii]] * w[None], axis=1))
            return jnp.concatenate(found, axis=0)

        i, o = lane_pairs(128, 128)
        same_half = filled(i // 64 == o // 64, 1.0)
        head = jnp.concatenate([chunk(i) for i in range(HEAD)], axis=0)
        weights[0 : HEAD * 16, :] = dot2(head, same_half)

        def body(i, carry):
            weights[pl.ds(pl.multiple_of(i * 16, 16), 16), :] = dot2(chunk(i), same_half)
            return carry

        lax.fori_loop(HEAD, (count + 7) // 8, body, 0)

    def combine(f_ref, y_ref, older, tiles, coef):
        a, b = coef

        for src in range(64):
            rows = {}
            for t in tiles:
                for o in range(t * 8 + 8 - REACH, t * 8 + 9 + REACH):
                    if o not in rows:
                        rows[o] = f_ref[src, o : o + 8, :]
            for t in tiles:
                r = t * 8 + 8
                total = xy_sum(couplings, t, src)
                for k in range(1, REACH + 1):
                    total = total + HALF[k] * (rows[r + k] + rows[r - k])
                total = a * (total + pot_ref[src, t * 8 : t * 8 + 8, :] * rows[r])
                if older is not None:
                    total = total - b * older(src, t)
                if t == 0:
                    total = jnp.where(jnp.logical_or(below, jnp.logical_not(low)), total, 0.0)
                if t == 2:
                    total = jnp.where(jnp.logical_or(above, low), total, 0.0)
                y_ref[src, r : r + 8, :] = total

    def spread(y_ref, a):
        low_row = lanes_low((1, 128))

        def term(i, u, w):
            ii = i * 8 + u
            atom = lists[ID, ii]
            t = zero8
            for q in range(2):
                scale = jnp.where(low_row, strength[2 * q, ii] * a, strength[2 * q + 1, ii] * a)
                t = t + (scale * w[u * 2 + q : u * 2 + q + 1, :]) * tiles_ref[atom, q]
            return t + swap(t)

        def add(i, u, t):
            ii = i * 8 + u
            src = lists[SRC, ii]
            rows = pl.ds(lists[ROW_L, ii], 8)
            on = jnp.logical_and(low, lists[ON_L, ii] > 0)
            y_ref[src, rows, :] = y_ref[src, rows, :] + jnp.where(on, t, 0.0)
            rows = pl.ds(lists[ROW_U, ii], 8)
            on = jnp.logical_and(jnp.logical_not(low), lists[ON_U, ii] > 0)
            y_ref[src, rows, :] = y_ref[src, rows, :] + jnp.where(on, t, 0.0)

        for i in range(HEAD):
            w = weights[i * 16 : i * 16 + 16, :]
            terms = [term(i, u, w) for u in range(8)]
            for u in range(8):
                add(i, u, terms[u])

        def body(i, carry):
            w = weights[pl.ds(pl.multiple_of(i * 16, 16), 16), :]
            terms = [term(i, u, w) for u in range(8)]
            for u in range(8):
                add(i, u, terms[u])
            return carry

        lax.fori_loop(HEAD, (count + 7) // 8, body, 0)

    products(ext, range(3))
    project(ext)
    older = None if first else (lambda src, t: older_ref[src, t * 8 : t * 8 + 8, :])
    combine(ext, mid, older, (0, 1, 2), coef1)
    spread(mid, coef1[0])
    products(mid, (1,))
    project(mid)
    combine(mid, new, lambda src, t: ext[src, 16:24, :], (1,), coef2)
    spread(new, coef2[0])
    out_ref[...] = new[:, 16:24, :]
    if not last:
        mid_ref[...] = mid[:, 8:32, :]


def double_step(first, last, coef1, coef2, lists, strength, halo, own, older, pot, tiles, mats):
    smem = pl.BlockSpec(memory_space=pltpu.SMEM)
    vmem = pl.BlockSpec(memory_space=pltpu.VMEM)
    ins = [lists, strength, halo[0], own, halo[1]]
    if not first:
        ins += [older, pot]
    ins += [tiles, *mats]
    outs = [jax.ShapeDtypeStruct((64, 8, 128), F32)]
    if first:
        outs.append(jax.ShapeDtypeStruct((64, 24, 128), F32))
    if not last:
        outs.append(jax.ShapeDtypeStruct((64, 24, 128), F32))
    return pl.pallas_call(
        functools.partial(double_kernel, first, last, coef1, coef2),
        out_shape=tuple(outs),
        in_specs=[smem, smem] + [vmem] * (len(ins) - 2),
        out_specs=tuple([vmem] * len(outs)),
        scratch_shapes=[
            pltpu.VMEM((64, 40, 128), F32),
            pltpu.VMEM((64, 40, 128), F32),
            pltpu.VMEM((64, 40, 128), F32),
            *[pltpu.VMEM((3, 64, 8, 128), F32)] * 5,
            pltpu.VMEM((128, 128), F32),
        ],
        compiler_params=VMEM,
    )(*ins)


def atom_lists(slab, proj_strength, atom_block, atom_offset):
    number = jnp.arange(64, dtype=jnp.int32)
    dz = atom_offset[:, 2] - 16 * slab
    near = jnp.logical_and(dz >= -15, dz <= 23)
    before = jnp.sum(
        jnp.logical_and(near[None, :], number[None, :] < number[:, None]).astype(jnp.int32), axis=1
    )
    pick = jnp.logical_and(near[None, :], before[None, :] == number[:, None])

    def listed(values, empty):
        return jnp.sum(jnp.where(pick, values[None, :], 0), axis=1) + jnp.where(
            jnp.any(pick, axis=1), 0, empty
        )

    at = listed(dz, 0)
    valid = jnp.any(pick, axis=1)
    source = listed(jnp.clip(atom_block, 0, 63), 0)
    upper = at > 8
    meta = jnp.zeros((64,), jnp.int32).at[0].set(jnp.sum(near.astype(jnp.int32)))
    meta = meta.at[1].set(slab).at[2].set(7 - slab)
    lists = jnp.stack(
        [
            listed(number, 0),
            source,
            jnp.where(upper, at - 8, at) + 16,
            upper.astype(jnp.int32),
            jnp.clip(at, -16, 16) + 16,
            jnp.logical_and(valid, at <= 15).astype(jnp.int32),
            jnp.clip(at - 8, -16, 16) + 16,
            jnp.logical_and(valid, at >= -7).astype(jnp.int32),
            meta,
        ]
    )
    strength = jnp.sum(jnp.where(pick[None], proj_strength.T[:, None, :], 0.0), axis=2)
    return lists, strength


def unpack_kernel(in_ref, out_ref, hartree_ref):
    low = lanes_low((8, 128))

    def block(pairs):
        rows = []
        for a, b in pairs:
            rows += [jnp.where(low, a, swap(b)), jnp.where(low, swap(a), b)]
        return jnp.concatenate(rows, axis=0).T

    for q in range(4):
        out_ref[q * 128 : (q + 1) * 128, :] = block(
            [
                (in_ref[plane_index(2 * q, s), 0:8, :], in_ref[plane_index(2 * q + 1, s), 0:8, :])
                for s in range(8)
            ]
        )
    pairs = []
    for s in range(8):
        total = in_ref[plane_index(0, s), 8:16, :]
        for b in range(1, 8):
            total = total + in_ref[plane_index(b, s), 8:16, :]
        pairs.append((total, total))
    part = block(pairs)[0:64, :]
    for e in range(8):
        hartree_ref[e] = part


def unpack(slabs):
    return pl.pallas_call(
        unpack_kernel,
        out_shape=(
            jax.ShapeDtypeStruct((512, 128), F32),
            jax.ShapeDtypeStruct((8, 64, 128), F32),
        ),
        compiler_params=VMEM,
    )(slabs)


OMEGA = DAMPING / 6.0


def lane_pairs(rows, columns):
    shape = (rows, columns)
    return lax.broadcasted_iota(jnp.int32, shape, 0), lax.broadcasted_iota(jnp.int32, shape, 1)


def filled(where, value):
    return jnp.where(where, value, 0.0).astype(BF16)


def both(*conditions):
    return functools.reduce(jnp.logical_and, conditions)


def transfers(fine_x, fine_y, down):
    fine, coarse = fine_x * fine_y, 128
    i, o = lane_pairs(fine, coarse) if down else lane_pairs(coarse, fine)
    f, c = (i, o) if down else (o, i)
    same = both(
        (f // fine_y) // 2 == c // (fine_y // 2), (f % fine_y) // 2 == c % (fine_y // 2)
    )
    return filled(same, 0.5 if down else 1.0)


def beside(nx, ny, used):
    i, o = lane_pairs(128, 128)
    dx, dy = o // ny - i // ny, o % ny - i % ny
    parts = [filled(both(jnp.abs(dx) + jnp.abs(dy) == 1, i // ny < used, o // ny < used), 1.0)]
    if used == nx:
        parts += [filled(both(dx == d, dy == 0), 1.0) for d in (1 - nx, nx - 1)]
    return jnp.concatenate(parts, axis=1)


def block_neighbours():
    i, o = lane_pairs(128, 128)
    half = i // 64 == o // 64
    dx, dy = (o // 8) % 8 - (i // 8) % 8, o % 8 - i % 8
    parts = [both(half, jnp.abs(dx) + jnp.abs(dy) == 1)]
    parts += [both(half, dx == d, dy == 0) for d in (-7, 7)]
    parts += [both(half, dx == 0, dy == d) for d in (-7, 7)]
    return jnp.concatenate([filled(p, 1.0) for p in parts], axis=1)


COUPLINGS = [pltpu.VMEM((2, 64, 8, 128), F32)] * 5


def inside_slab_range(slab, r):
    z = (
        lax.broadcasted_iota(jnp.int32, (8, 128), 0)
        + jnp.where(lanes_low((8, 128)), 0, 8)
        + (16 * slab + (r - 16))
    )
    return jnp.logical_and(z >= 0, z < 128)


def relax(ref, rows, mat, couplings, update):
    for t, r in enumerate(rows):
        keep_couplings(couplings, t, dot2(ref[:, r : r + 8, :].reshape(512, 128), mat))
    for src in range(64):
        for t, r in enumerate(rows):
            near = xy_sum(couplings, t, src)
            near = near + ref[src, r - 1 : r + 7, :] + ref[src, r + 1 : r + 9, :]
            update(src, r, ref[src, r : r + 8, :], near)


def source_kernel(scalars, occ, own_ref, sent_ref, up_ref, down_ref, v, w, r0, *couplings):
    mat = block_neighbours()
    low = lanes_low((8, 128))
    slab, occupation = scalars[0], occ[scalars[1]] / 64.0
    zero = jnp.zeros((8, 128), F32)

    def fill():
        for src in range(64):
            y = own_ref[src]
            o = OMEGA * (occupation * y * y)
            v[src, 0:8, :] = zero
            v[src, 8:16, :] = swap(jnp.where(low, o, 0.0))
            v[src, 16:24, :] = o
            v[src, 24:32, :] = swap(jnp.where(low, 0.0, o))
            v[src, 32:40, :] = zero
            w[src, 8:16, :] = zero
            w[src, 24:32, :] = zero

    fill()
    low3 = lanes_low((3, 128))
    for src in range(32):
        rows = slice(src * 3, src * 3 + 3)
        a, b = v[src, 21:24, :], v[src + 32, 21:24, :]
        up_ref[rows, :] = jnp.where(low3, swap(a), b)
        a, b = v[src, 16:19, :], v[src + 32, 16:19, :]
        down_ref[rows, :] = jnp.where(low3, a, swap(b))
    keep = {r: inside_slab_range(slab, r) for r in (13, 19)}

    def second(src, r, c, near):
        w[src, r : r + 8, :] = jnp.where(keep[r], 1.2 * c + OMEGA * near, 0.0)

    def residual(src, r, c, near):
        r0[src, r : r + 8, :] = v[src, r : r + 8, :] * (1.0 / OMEGA) - 6.0 * c + near

    relax(v, (13, 19), mat, couplings, second)
    relax(w, (14, 18), mat, couplings, residual)
    rows = []
    for xb in range(8):
        parts = []
        for yb in range(8):
            src = xb * 8 + yb
            parts.append(r0[src, pl.ds(14, 8, stride=2), :] + r0[src, pl.ds(15, 8, stride=2), :])
        rows.append(jnp.concatenate(parts, axis=1))
    summed = jnp.concatenate(rows, axis=0)

    i = lax.broadcasted_iota(jnp.int32, (128, 256), 0)
    o = lax.broadcasted_iota(jnp.int32, (128, 256), 1)
    apart = (o // 128) * 1000 + o % 128 - (i // 64) * 1000 - ((i // 16) % 4) * 32 - (i % 8) // 2
    down = [jnp.where(apart == 4 * yb, 0.5, 0.0).astype(BF16) for yb in range(8)]
    coarse = jnp.dot(
        halves(summed, 0), jnp.concatenate(down, axis=0), preferred_element_type=F32
    )
    coarse = coarse[0:64] + coarse[64:128]
    below, above = [], []
    own = []
    for xb in range(8):
        part = coarse[xb * 8 : xb * 8 + 8]
        own.append(part[1:5, 0:128])
        own.append(part[1:5, 128:256])
        below.append(part[0:1, 0:128])
        above.append(part[5:6, 128:256])
    sent = jnp.concatenate(own + below + above, axis=0)
    for e in range(8):
        sent_ref[e] = sent


def source_step(scalars, occupations, own):
    smem = pl.BlockSpec(memory_space=pltpu.SMEM)
    vmem = pl.BlockSpec(memory_space=pltpu.VMEM)
    return pl.pallas_call(
        source_kernel,
        out_shape=(
            jax.ShapeDtypeStruct((8, 80, 128), F32),
            jax.ShapeDtypeStruct((96, 128), F32),
            jax.ShapeDtypeStruct((96, 128), F32),
        ),
        in_specs=[smem, smem, vmem],
        out_specs=(vmem, vmem, vmem),
        scratch_shapes=[pltpu.VMEM((64, 40, 128), F32)] * 3 + COUPLINGS,
        compiler_params=VMEM,
    )(scalars, occupations, own)


def double_rows(scratch, value, n):
    scratch[:, pl.ds(0, n, stride=2), :] = value
    scratch[:, pl.ds(1, n, stride=2), :] = value


def coarse_solve(g, v, r1, v2, r2, v3, r3):
    near1, near2, near3 = beside(4, 32, 4), beside(8, 16, 8), beside(16, 8, 8)

    def near(ref, blocks, planes, mat):
        rows = ref[:, 8 : 8 + planes, :]
        y = dot2(rows.reshape(blocks * planes, 128), mat)
        y = y.reshape(blocks, planes, -1)
        total = y[:, :, 0:128] + ref[:, 7 : 7 + planes, :] + ref[:, 9 : 9 + planes, :]
        if blocks > 1:
            none = jnp.zeros((1, planes, 128), F32)
            total = total + jnp.concatenate([none, y[:-1, :, 128:256]], axis=0)
            total = total + jnp.concatenate([y[1:, :, 256:384], none], axis=0)
        return rows, total

    def sweep(ref, source, blocks, planes, mat):
        rows, total = near(ref, blocks, planes, mat)
        ref[:, 8 : 8 + planes, :] = rows + OMEGA * (source() - 6.0 * rows + total)

    def residual(ref, source, blocks, planes, mat):
        rows, total = near(ref, blocks, planes, mat)
        return source() - 6.0 * rows + total

    for ref, planes in ((v, 64), (v2, 32), (v3, 16)):
        border = jnp.zeros((ref.shape[0], 8, 128), F32)
        ref[:, 0:8, :] = border
        ref[:, 8 + planes : 16 + planes, :] = border
    g1 = lambda: g[:, 8:72, :]
    v[:, 8:72, :] = OMEGA * g1()
    sweep(v, g1, 8, 64, near1)
    r1[...] = residual(v, g1, 8, 64, near1)
    pair = r1[:, pl.ds(0, 32, stride=2), :] + r1[:, pl.ds(1, 32, stride=2), :]
    rows = [jnp.concatenate([pair[4 * b + e] for e in range(4)], axis=1) for b in range(2)]
    d = jnp.dot(halves(jnp.concatenate(rows, axis=0), 0), transfers(16, 32, True), preferred_element_type=F32)
    s2 = (d[0:64] + d[64:128]).reshape(2, 32, 128)
    g2 = lambda: s2
    v2[:, 8:40, :] = OMEGA * s2
    sweep(v2, g2, 2, 32, near2)
    r2[...] = residual(v2, g2, 2, 32, near2)
    pair = r2[:, pl.ds(0, 16, stride=2), :] + r2[:, pl.ds(1, 16, stride=2), :]
    both = jnp.concatenate([pair[0], pair[1]], axis=1)
    d = jnp.dot(halves(both, 0), transfers(16, 16, True), preferred_element_type=F32)
    s3 = (d[0:16] + d[16:32]).reshape(1, 16, 128)
    g3 = lambda: s3
    v3[:, 8:24, :] = OMEGA * s3
    for _ in range(COARSE - 1):
        sweep(v3, g3, 1, 16, near3)
    double_rows(r3, v3[:, 8:24, :], 16)
    up = dot2(r3[0], transfers(16, 16, False))
    for b in range(2):
        v2[b, 8:40, :] = v2[b, 8:40, :] + up[:, b * 128 : b * 128 + 128]
    for _ in range(POST):
        sweep(v2, g2, 2, 32, near2)
    double_rows(r1.at[0:2], v2[:, 8:40, :], 32)
    up = dot2(r1[0:2].reshape(128, 128), transfers(16, 32, False))
    for b in range(8):
        part = up[(b // 4) * 64 : (b // 4) * 64 + 64, (b % 4) * 128 : (b % 4) * 128 + 128]
        v[b, 8:72, :] = v[b, 8:72, :] + part
    for _ in range(POST):
        sweep(v, g1, 8, 64, near1)


def finish_kernel(scalars, occ, got_ref, prev_ref, y_ref, next_ref, *refs):
    mat = block_neighbours()
    out_ref = refs[0]
    fx, va, vb, up, g, v, r1, v2, r2, v3, r3, wide = refs[1:13]
    couplings = refs[13:]
    low = lanes_low((8, 128))
    low3 = lanes_low((3, 128))
    slab, factor = scalars[0], OMEGA * (occ[scalars[1]] / 64.0)

    for s in range(8):
        g[:, 8 + 8 * s : 16 + 8 * s, :] = got_ref[SLAB_DEVICE[s], 0:64, :].reshape(8, 8, 128)
    for s in range(8):
        for xb in range(8):
            if s > 0:
                row = 8 + 8 * s - 1
                g[xb, row : row + 1, :] = g[xb, row : row + 1, :] + got_ref[SLAB_DEVICE[s], 64 + xb : 65 + xb, :]
            if s < 7:
                row = 8 + 8 * s + 8
                g[xb, row : row + 1, :] = g[xb, row : row + 1, :] + got_ref[SLAB_DEVICE[s], 72 + xb : 73 + xb, :]
    coarse_solve(g, v, r1, v2, r2, v3, r3)
    double_rows(wide, v[:, pl.ds(8 * slab + 4, 16), :], 16)
    i = lax.broadcasted_iota(jnp.int32, (128, 128), 0)
    o = lax.broadcasted_iota(jnp.int32, (128, 128), 1)
    apart = i - ((o // 16) % 4) * 32 - (o % 8) // 2
    spread = jnp.concatenate(
        [jnp.where(apart == 4 * yb, 1.0, 0.0).astype(BF16) for yb in range(8)], axis=1
    )
    up[...] = dot2(wide[...].reshape(256, 128), spread).reshape(8, 32, 1024)

    def fill():
        for src in range(64):
            o = factor * jnp.square(y_ref[src])
            turned = swap(o)
            rows = slice(src % 32 * 3, src % 32 * 3 + 3)
            p, n = prev_ref[rows, :], next_ref[rows, :]
            p, n = (p, swap(n)) if src < 32 else (swap(p), n)
            fx[src, 8:16, :] = jnp.where(low, 0.0, turned)
            fx[src, 13:16, :] = jnp.where(low3, p, turned[5:8])
            fx[src, 16:24, :] = o
            fx[src, 24:32, :] = jnp.where(low, turned, 0.0)
            fx[src, 24:27, :] = jnp.where(low3, turned[0:3], n)
            out_ref[src, 0:8, :] = y_ref[src]

    fill()
    keep = {r: inside_slab_range(slab, r) for r in (14, 18, 15, 17)}

    def second(src, r, c, near):
        va[src, r : r + 8, :] = jnp.where(keep[r], 1.2 * c + OMEGA * near, 0.0)

    def add_up():
        for src in range(64):
            xb, lanes = src // 8, slice(src % 8 * 128, src % 8 * 128 + 128)
            for r, n in ((14, 8), (22, 4)):
                e = jnp.where(
                    lanes_low((n, 128)), up[xb, r - 8 : r - 8 + n, lanes], up[xb, r : r + n, lanes]
                )
                va[src, r : r + n, :] = va[src, r : r + n, :] + e

    def swept(src, r, c, near):
        return c + (fx[src, r : r + 8, :] - DAMPING * c + OMEGA * near)

    def fourth(src, r, c, near):
        vb[src, r : r + 8, :] = jnp.where(keep[r], swept(src, r, c, near), 0.0)

    def fifth(src, r, c, near):
        out_ref[src, 8:16, :] = swept(src, r, c, near)

    relax(fx, (14, 18), mat, couplings, second)
    add_up()
    relax(va, (15, 17), mat, couplings, fourth)
    relax(vb, (16,), mat, couplings, fifth)


def finish_step(scalars, occupations, got, halo, own):
    smem = pl.BlockSpec(memory_space=pltpu.SMEM)
    vmem = pl.BlockSpec(memory_space=pltpu.VMEM)
    ins = [scalars, occupations, got, halo[0], own, halo[1]]
    return pl.pallas_call(
        finish_kernel,
        out_shape=jax.ShapeDtypeStruct((64, 16, 128), F32),
        in_specs=[smem, smem] + [vmem] * (len(ins) - 2),
        out_specs=vmem,
        scratch_shapes=[
            pltpu.VMEM((64, 40, 128), F32),
            pltpu.VMEM((64, 40, 128), F32),
            pltpu.VMEM((64, 40, 128), F32),
            pltpu.VMEM((8, 32, 1024), F32),
            pltpu.VMEM((8, 80, 128), F32),
            pltpu.VMEM((8, 80, 128), F32),
            pltpu.VMEM((8, 64, 128), F32),
            pltpu.VMEM((2, 48, 128), F32),
            pltpu.VMEM((2, 32, 128), F32),
            pltpu.VMEM((1, 32, 128), F32),
            pltpu.VMEM((1, 32, 128), F32),
            pltpu.VMEM((8, 32, 128), F32),
        ]
        + COUPLINGS,
        compiler_params=VMEM,
    )(*ins)


def exchange(to_next, to_last):
    up = [(SLAB_DEVICE[i], SLAB_DEVICE[i + 1]) for i in range(7)]
    down = [(j, i) for i, j in up]
    return lax.ppermute(to_next, GROUP, up), lax.ppermute(to_last, GROUP, down)


def local(
    orbitals, local_potential, occupations, proj_values, proj_strength, atom_block, atom_offset
):
    core, xlo, ylo = (lax.axis_index(a) for a in GROUP)
    slab = 2 * (xlo * (3 - ylo) + (1 - xlo) * ylo) + core
    lists, strength = atom_lists(slab, proj_strength, atom_block, atom_offset)
    high, low = coupling(HALF)
    mats = (jnp.asarray(high), jnp.asarray(low))

    packed = pack(orbitals, local_potential)
    tiles = projector_tiles(proj_values)
    own = lax.all_to_all(packed, PLANE, 0, 0, tiled=True)

    sigma = HALF_WIDTH / (0.0 - CENTER)
    tau = 2.0 / sigma
    coefs = [(sigma / HALF_WIDTH, 0.0)]
    for _ in range(DEGREE - 1):
        following = 1.0 / (tau - sigma)
        coefs.append((2.0 * following / HALF_WIDTH, sigma * following))
        sigma = following
    older = pot = None
    for k in range(0, DEGREE, 2):
        first, last = k == 0, k == DEGREE - 2
        halo = exchange(own, own)
        outs = list(
            double_step(
                first, last, coefs[k], coefs[k + 1], lists, strength, halo, own, older, pot, tiles, mats
            )
        )
        own = outs.pop(0)
        if first:
            pot = outs.pop(0)
        if not last:
            older = outs.pop(0)

    scalars = jnp.stack([slab, 2 * lax.axis_index("yhi") + lax.axis_index("xhi")]).astype(jnp.int32)
    sent, last_planes, first_planes = source_step(scalars, occupations, own)
    halo = exchange(last_planes, first_planes)
    got = lax.all_to_all(sent, GROUP, 0, 0, tiled=True)
    packed = finish_step(scalars, occupations, got, halo, own)
    back = lax.all_to_all(packed, PLANE, 0, 0, tiled=True)
    filtered, part = unpack(back)
    hartree = jnp.sum(lax.all_to_all(part, BAND, 0, 0, tiled=True), axis=0)
    return filtered.reshape(8, 8, 8, 128), hartree.reshape(8, 8, 128)


def solution(mesh):
    fine = Mesh(
        mesh.devices.reshape(8, 4, 2, 2, 2, 2), (BAND, "yhi", "core", "xhi", "xlo", "ylo")
    )
    bands, grid = P(BAND, GX, GYZ, None), P(GX, GYZ, None)
    return jax.shard_map(
        local,
        mesh=fine,
        in_specs=(bands, grid, P(BAND), P(), P(), P(), P()),
        out_specs=(bands, grid),
        check_vma=False,
    )
```

```python
import functools

import jax
import jax.numpy as jnp
import numpy as np
from jax import lax
from jax.experimental import pallas as pl
from jax.experimental.pallas import tpu as pltpu
from jax.sharding import Mesh
from jax.sharding import PartitionSpec as P

DEGREE = 8
POST = 2
COARSE = 4
STENCIL = (
    -5369.0 / 1800.0,
    12.0 / 7.0,
    -15.0 / 56.0,
    10.0 / 189.0,
    -1.0 / 112.0,
    2.0 / 1925.0,
    -1.0 / 16632.0,
)
HALF = tuple(-0.5 * c for c in STENCIL)
REACH = 6
CENTER = 12.0
HALF_WIDTH = 8.0
DAMPING = 0.8
BAND = "z"
GX = ("yhi", "core")
GYZ = ("xhi", "xlo", "ylo")
PLANE = GX + GYZ
GROUP = ("core", "xlo", "ylo")
CHIPS = ((0, 0), (0, 1), (1, 1), (1, 0))
SLAB_DEVICE = [c * 4 + xl * 2 + yl for xl, yl in CHIPS for c in (0, 1)]
VMEM = pltpu.CompilerParams(vmem_limit_bytes=12 * 1024 * 1024)
HEAD = 4
F32 = jnp.float32
BF16 = jnp.bfloat16


def plane_index(band, slab):
    yhi, xhi = band // 2, band % 2
    xlo, ylo = CHIPS[slab // 2]
    return yhi * 16 + (slab % 2) * 8 + xhi * 4 + xlo * 2 + ylo


def coupling(weights):
    own, xu, xd, yu, yd = (np.zeros((128, 128)) for _ in range(5))
    for zh in range(2):
        for xi in range(8):
            for yi in range(8):
                i = zh * 64 + xi * 8 + yi
                for o in range(8):
                    for m, k in ((own, abs(o - xi)), (xu, o + 8 - xi), (xd, xi + 8 - o)):
                        if 1 <= k < len(weights):
                            m[i, zh * 64 + o * 8 + yi] += weights[k]
                    for m, k in ((own, abs(o - yi)), (yu, o + 8 - yi), (yd, yi + 8 - o)):
                        if 1 <= k < len(weights):
                            m[i, zh * 64 + xi * 8 + o] += weights[k]
    whole = np.concatenate([own, xu, xd, yu, yd], axis=1).astype(np.float32)
    high = whole.astype(jnp.bfloat16)
    low = (whole - high.astype(np.float32)).astype(jnp.bfloat16)
    return high, low


def halves(x, axis):
    high = x.astype(BF16)
    return jnp.concatenate([high, (x - high.astype(F32)).astype(BF16)], axis=axis)


def lanes_low(shape):
    return lax.broadcasted_iota(jnp.int32, shape, len(shape) - 1) < 64


def dot2(x, m):
    return jnp.dot(halves(x, 1), jnp.concatenate([m, m], axis=0), preferred_element_type=F32)


def swap(x):
    return pltpu.roll(x, 64, x.ndim - 1)


def split3(x):
    a = x.astype(BF16)
    r = x - a.astype(F32)
    b = r.astype(BF16)
    c = (r - b.astype(F32)).astype(BF16)
    return a, b, c


def pack_kernel(orb_ref, pot_ref, out_ref):
    low = lanes_low((8, 128))
    for q in range(4):
        turned = orb_ref[q * 128 : (q + 1) * 128, :].T
        for s in range(8):
            a = turned[s * 16 : s * 16 + 8, :]
            b = turned[s * 16 + 8 : s * 16 + 16, :]
            out_ref[plane_index(2 * q, s), 0:8, :] = jnp.where(low, a, swap(b))
            out_ref[plane_index(2 * q + 1, s), 0:8, :] = jnp.where(low, swap(a), b)
    pot = pot_ref[...]
    turned = jnp.concatenate([pot, pot], axis=0).T
    for s in range(8):
        piece = jnp.where(low, turned[s * 16 : s * 16 + 8, :], turned[s * 16 + 8 : s * 16 + 16, :])
        for b in range(8):
            out_ref[plane_index(b, s), 8:16, :] = piece


def pack(orbitals, potential):
    return pl.pallas_call(
        pack_kernel,
        out_shape=jax.ShapeDtypeStruct((64, 16, 128), F32),
        compiler_params=VMEM,
    )(orbitals.reshape(512, 128), potential.reshape(64, 128))


def tiles_kernel(proj_ref, pick_ref, tiles_ref):
    low = lanes_low((8, 2, 8, 128))
    keep = lax.broadcasted_iota(jnp.int32, (4, 8, 512), 2) % 8 == lax.broadcasted_iota(
        jnp.int32, (4, 8, 512), 1
    )

    def body(i, carry):
        parts = [
            jnp.where(keep, proj_ref[i * 8 + u][:, None, :], 0.0).reshape(32, 512)
            for u in range(8)
        ]
        spread = jnp.concatenate(parts, axis=0)
        pick = pick_ref[...]
        total = sum(jnp.dot(part, pick, preferred_element_type=F32) for part in split3(spread))
        total = total.reshape(8, 2, 2, 8, 128)
        tiles_ref[pl.ds(i * 8, 8), :, :, :] = jnp.where(low, total[:, :, 0], total[:, :, 1])
        return carry

    lax.fori_loop(0, 8, body, 0)


def projector_tiles(proj):
    pick = (np.arange(512)[:, None] // 8 == np.arange(128)[None, :] % 64).astype(jnp.bfloat16)
    return pl.pallas_call(
        tiles_kernel,
        out_shape=jax.ShapeDtypeStruct((64, 2, 8, 128), F32),
        compiler_params=VMEM,
    )(proj, pick)


def keep_couplings(couplings, t, y):
    y = y.reshape(64, 8, 640)
    for e, ref in enumerate(couplings):
        ref[t] = y[:, :, e * 128 : e * 128 + 128]


def xy_sum(couplings, t, src):
    own, from_x, to_x, from_y, to_y = couplings
    total = own[t, src]
    if src >= 8:
        total = total + from_x[t, src - 8]
    if src < 56:
        total = total + to_x[t, src + 8]
    if src % 8 > 0:
        total = total + from_y[t, src - 1]
    if src % 8 < 7:
        total = total + to_y[t, src + 1]
    return total


ID, SRC, ROW, UPPER, ROW_L, ON_L, ROW_U, ON_U, META = range(9)


def double_kernel(
    first, last, coef1, coef2, lists, strength, prev_ref, own_ref, next_ref, *refs
):
    refs = list(refs)
    if first:
        older_ref = pot_ref = None
    else:
        older_ref, pot_ref = refs.pop(0), refs.pop(0)
    tiles_ref, mat_ref, mat_low_ref = refs[:3]
    refs = refs[3:]
    out_ref = refs.pop(0)
    if first:
        pot_ref = refs.pop(0)
    mid_ref = None if last else refs.pop(0)
    ext, mid, new, *couplings, weights = refs
    low = lanes_low((8, 128))
    count = lists[META, 0]
    below = lists[META, 1] > 0
    above = lists[META, 2] > 0
    zero8 = jnp.zeros((8, 128), F32)

    def fill():
        for src in range(64):
            p, o, n = prev_ref[src, 0:8, :], own_ref[src, 0:8, :], next_ref[src, 0:8, :]
            ext[src, 0:8, :] = p
            ext[src, 8:16, :] = swap(jnp.where(low, o, p))
            ext[src, 16:24, :] = o
            ext[src, 24:32, :] = swap(jnp.where(low, n, o))
            ext[src, 32:40, :] = n
            if first:
                p, o, n = prev_ref[src, 8:16, :], own_ref[src, 8:16, :], next_ref[src, 8:16, :]
                shift = 3.0 * HALF[0] - CENTER
                pot_ref[src, 0:8, :] = swap(jnp.where(low, o, p)) + shift
                pot_ref[src, 8:16, :] = o + shift
                pot_ref[src, 16:24, :] = swap(jnp.where(low, n, o)) + shift

    fill()

    def products(f_ref, tiles):
        for t in tiles:
            x = halves(f_ref[:, t * 8 + 8 : t * 8 + 16, :].reshape(512, 128), 1)
            m = mat_ref[...]
            y = jnp.dot(x, jnp.concatenate([m, m], axis=0), preferred_element_type=F32)
            y = y + jnp.dot(x[:, 0:128], mat_low_ref[...], preferred_element_type=F32)
            keep_couplings(couplings, t, y)

    def project(f_ref):
        def chunk(i):
            found = []
            for u in range(8):
                ii = i * 8 + u
                w = f_ref[lists[SRC, ii], pl.ds(lists[ROW, ii], 8), :]
                w = jnp.where(low == (lists[UPPER, ii] == 0), w, 0.0)
                w = w + swap(w)
                found.append(jnp.sum(tiles_ref[lists[ID, ii]] * w[None], axis=1))
            return jnp.concatenate(found, axis=0)

        i, o = lane_pairs(128, 128)
        same_half = filled(i // 64 == o // 64, 1.0)
        head = jnp.concatenate([chunk(i) for i in range(HEAD)], axis=0)
        weights[0 : HEAD * 16, :] = dot2(head, same_half)

        def body(i, carry):
            weights[pl.ds(pl.multiple_of(i * 16, 16), 16), :] = dot2(chunk(i), same_half)
            return carry

        lax.fori_loop(HEAD, (count + 7) // 8, body, 0)

    def combine(f_ref, y_ref, older, tiles, coef):
        a, b = coef

        for src in range(64):
            rows = {}
            for t in tiles:
                for o in range(t * 8 + 8 - REACH, t * 8 + 9 + REACH):
                    if o not in rows:
                        rows[o] = f_ref[src, o : o + 8, :]
            for t in tiles:
                r = t * 8 + 8
                total = xy_sum(couplings, t, src)
                for k in range(1, REACH + 1):
                    total = total + HALF[k] * (rows[r + k] + rows[r - k])
                total = a * (total + pot_ref[src, t * 8 : t * 8 + 8, :] * rows[r])
                if older is not None:
                    total = total - b * older(src, t)
                if t == 0:
                    total = jnp.where(jnp.logical_or(below, jnp.logical_not(low)), total, 0.0)
                if t == 2:
                    total = jnp.where(jnp.logical_or(above, low), total, 0.0)
                y_ref[src, r : r + 8, :] = total

    def spread(y_ref, a):
        low_row = lanes_low((1, 128))

        def term(i, u, w):
            ii = i * 8 + u
            atom = lists[ID, ii]
            t = zero8
            for q in range(2):
                scale = jnp.where(low_row, strength[2 * q, ii] * a, strength[2 * q + 1, ii] * a)
                t = t + (scale * w[u * 2 + q : u * 2 + q + 1, :]) * tiles_ref[atom, q]
            return t + swap(t)

        def add(i, u, t):
            ii = i * 8 + u
            src = lists[SRC, ii]
            rows = pl.ds(lists[ROW_L, ii], 8)
            on = jnp.logical_and(low, lists[ON_L, ii] > 0)
            y_ref[src, rows, :] = y_ref[src, rows, :] + jnp.where(on, t, 0.0)
            rows = pl.ds(lists[ROW_U, ii], 8)
            on = jnp.logical_and(jnp.logical_not(low), lists[ON_U, ii] > 0)
            y_ref[src, rows, :] = y_ref[src, rows, :] + jnp.where(on, t, 0.0)

        for i in range(HEAD):
            w = weights[i * 16 : i * 16 + 16, :]
            terms = [term(i, u, w) for u in range(8)]
            for u in range(8):
                add(i, u, terms[u])

        def body(i, carry):
            w = weights[pl.ds(pl.multiple_of(i * 16, 16), 16), :]
            terms = [term(i, u, w) for u in range(8)]
            for u in range(8):
                add(i, u, terms[u])
            return carry

        lax.fori_loop(HEAD, (count + 7) // 8, body, 0)

    products(ext, range(3))
    project(ext)
    older = None if first else (lambda src, t: older_ref[src, t * 8 : t * 8 + 8, :])
    combine(ext, mid, older, (0, 1, 2), coef1)
    spread(mid, coef1[0])
    products(mid, (1,))
    project(mid)
    combine(mid, new, lambda src, t: ext[src, 16:24, :], (1,), coef2)
    spread(new, coef2[0])
    out_ref[...] = new[:, 16:24, :]
    if not last:
        mid_ref[...] = mid[:, 8:32, :]


def double_step(first, last, coef1, coef2, lists, strength, halo, own, older, pot, tiles, mats):
    smem = pl.BlockSpec(memory_space=pltpu.SMEM)
    vmem = pl.BlockSpec(memory_space=pltpu.VMEM)
    ins = [lists, strength, halo[0], own, halo[1]]
    if not first:
        ins += [older, pot]
    ins += [tiles, *mats]
    outs = [jax.ShapeDtypeStruct((64, 8, 128), F32)]
    if first:
        outs.append(jax.ShapeDtypeStruct((64, 24, 128), F32))
    if not last:
        outs.append(jax.ShapeDtypeStruct((64, 24, 128), F32))
    return pl.pallas_call(
        functools.partial(double_kernel, first, last, coef1, coef2),
        out_shape=tuple(outs),
        in_specs=[smem, smem] + [vmem] * (len(ins) - 2),
        out_specs=tuple([vmem] * len(outs)),
        scratch_shapes=[
            pltpu.VMEM((64, 40, 128), F32),
            pltpu.VMEM((64, 40, 128), F32),
            pltpu.VMEM((64, 40, 128), F32),
            *[pltpu.VMEM((3, 64, 8, 128), F32)] * 5,
            pltpu.VMEM((128, 128), F32),
        ],
        compiler_params=VMEM,
    )(*ins)


def atom_lists(slab, proj_strength, atom_block, atom_offset):
    number = jnp.arange(64, dtype=jnp.int32)
    dz = atom_offset[:, 2] - 16 * slab
    near = jnp.logical_and(dz >= -14, dz <= 22)
    before = jnp.sum(
        jnp.logical_and(near[None, :], number[None, :] < number[:, None]).astype(jnp.int32), axis=1
    )
    pick = jnp.logical_and(near[None, :], before[None, :] == number[:, None])

    def listed(values, empty):
        return jnp.sum(jnp.where(pick, values[None, :], 0), axis=1) + jnp.where(
            jnp.any(pick, axis=1), 0, empty
        )

    at = listed(dz, 0)
    valid = jnp.any(pick, axis=1)
    source = listed(jnp.clip(atom_block, 0, 63), 0)
    upper = at > 8
    meta = jnp.zeros((64,), jnp.int32).at[0].set(jnp.sum(near.astype(jnp.int32)))
    meta = meta.at[1].set(slab).at[2].set(7 - slab)
    lists = jnp.stack(
        [
            listed(number, 0),
            source,
            jnp.where(upper, at - 8, at) + 16,
            upper.astype(jnp.int32),
            jnp.clip(at, -16, 16) + 16,
            jnp.logical_and(valid, at <= 15).astype(jnp.int32),
            jnp.clip(at - 8, -16, 16) + 16,
            jnp.logical_and(valid, at >= -7).astype(jnp.int32),
            meta,
        ]
    )
    strength = jnp.sum(jnp.where(pick[None], proj_strength.T[:, None, :], 0.0), axis=2)
    return lists, strength


def unpack_kernel(in_ref, out_ref, hartree_ref):
    low = lanes_low((8, 128))

    def block(pairs):
        rows = []
        for a, b in pairs:
            rows += [jnp.where(low, a, swap(b)), jnp.where(low, swap(a), b)]
        return jnp.concatenate(rows, axis=0).T

    for q in range(4):
        out_ref[q * 128 : (q + 1) * 128, :] = block(
            [
                (in_ref[plane_index(2 * q, s), 0:8, :], in_ref[plane_index(2 * q + 1, s), 0:8, :])
                for s in range(8)
            ]
        )
    pairs = []
    for s in range(8):
        total = in_ref[plane_index(0, s), 8:16, :]
        for b in range(1, 8):
            total = total + in_ref[plane_index(b, s), 8:16, :]
        pairs.append((total, total))
    part = block(pairs)[0:64, :]
    for e in range(8):
        hartree_ref[e] = part


def unpack(slabs):
    return pl.pallas_call(
        unpack_kernel,
        out_shape=(
            jax.ShapeDtypeStruct((512, 128), F32),
            jax.ShapeDtypeStruct((8, 64, 128), F32),
        ),
        compiler_params=VMEM,
    )(slabs)


OMEGA = DAMPING / 6.0


def lane_pairs(rows, columns):
    shape = (rows, columns)
    return lax.broadcasted_iota(jnp.int32, shape, 0), lax.broadcasted_iota(jnp.int32, shape, 1)


def filled(where, value):
    return jnp.where(where, value, 0.0).astype(BF16)


def both(*conditions):
    return functools.reduce(jnp.logical_and, conditions)


def transfers(fine_x, fine_y, down):
    fine, coarse = fine_x * fine_y, 128
    i, o = lane_pairs(fine, coarse) if down else lane_pairs(coarse, fine)
    f, c = (i, o) if down else (o, i)
    same = both(
        (f // fine_y) // 2 == c // (fine_y // 2), (f % fine_y) // 2 == c % (fine_y // 2)
    )
    return filled(same, 0.5 if down else 1.0)


def beside(nx, ny, used):
    i, o = lane_pairs(128, 128)
    dx, dy = o // ny - i // ny, o % ny - i % ny
    parts = [filled(both(jnp.abs(dx) + jnp.abs(dy) == 1, i // ny < used, o // ny < used), 1.0)]
    if used == nx:
        parts += [filled(both(dx == d, dy == 0), 1.0) for d in (1 - nx, nx - 1)]
    return jnp.concatenate(parts, axis=1)


def block_neighbours():
    i, o = lane_pairs(128, 128)
    half = i // 64 == o // 64
    dx, dy = (o // 8) % 8 - (i // 8) % 8, o % 8 - i % 8
    parts = [both(half, jnp.abs(dx) + jnp.abs(dy) == 1)]
    parts += [both(half, dx == d, dy == 0) for d in (-7, 7)]
    parts += [both(half, dx == 0, dy == d) for d in (-7, 7)]
    return jnp.concatenate([filled(p, 1.0) for p in parts], axis=1)


COUPLINGS = [pltpu.VMEM((2, 64, 8, 128), F32)] * 5


def inside_slab_range(slab, r):
    z = (
        lax.broadcasted_iota(jnp.int32, (8, 128), 0)
        + jnp.where(lanes_low((8, 128)), 0, 8)
        + (16 * slab + (r - 16))
    )
    return jnp.logical_and(z >= 0, z < 128)


def relax(ref, rows, mat, couplings, update):
    for t, r in enumerate(rows):
        keep_couplings(couplings, t, dot2(ref[:, r : r + 8, :].reshape(512, 128), mat))
    for src in range(64):
        for t, r in enumerate(rows):
            near = xy_sum(couplings, t, src)
            near = near + ref[src, r - 1 : r + 7, :] + ref[src, r + 1 : r + 9, :]
            update(src, r, ref[src, r : r + 8, :], near)


def source_kernel(scalars, occ, own_ref, sent_ref, up_ref, down_ref, v, w, r0, *couplings):
    mat = block_neighbours()
    low = lanes_low((8, 128))
    slab, occupation = scalars[0], occ[scalars[1]] / 64.0
    zero = jnp.zeros((8, 128), F32)

    def fill():
        for src in range(64):
            y = own_ref[src]
            o = OMEGA * (occupation * y * y)
            v[src, 0:8, :] = zero
            v[src, 8:16, :] = swap(jnp.where(low, o, 0.0))
            v[src, 16:24, :] = o
            v[src, 24:32, :] = swap(jnp.where(low, 0.0, o))
            v[src, 32:40, :] = zero
            w[src, 8:16, :] = zero
            w[src, 24:32, :] = zero

    fill()
    low3 = lanes_low((3, 128))
    for src in range(32):
        rows = slice(src * 3, src * 3 + 3)
        a, b = v[src, 21:24, :], v[src + 32, 21:24, :]
        up_ref[rows, :] = jnp.where(low3, swap(a), b)
        a, b = v[src, 16:19, :], v[src + 32, 16:19, :]
        down_ref[rows, :] = jnp.where(low3, a, swap(b))
    keep = {r: inside_slab_range(slab, r) for r in (13, 19)}

    def second(src, r, c, near):
        w[src, r : r + 8, :] = jnp.where(keep[r], 1.2 * c + OMEGA * near, 0.0)

    def residual(src, r, c, near):
        r0[src, r : r + 8, :] = v[src, r : r + 8, :] * (1.0 / OMEGA) - 6.0 * c + near

    relax(v, (13, 19), mat, couplings, second)
    relax(w, (14, 18), mat, couplings, residual)
    rows = []
    for xb in range(8):
        parts = []
        for yb in range(8):
            src = xb * 8 + yb
            parts.append(r0[src, pl.ds(14, 8, stride=2), :] + r0[src, pl.ds(15, 8, stride=2), :])
        rows.append(jnp.concatenate(parts, axis=1))
    summed = jnp.concatenate(rows, axis=0)

    i = lax.broadcasted_iota(jnp.int32, (128, 256), 0)
    o = lax.broadcasted_iota(jnp.int32, (128, 256), 1)
    apart = (o // 128) * 1000 + o % 128 - (i // 64) * 1000 - ((i // 16) % 4) * 32 - (i % 8) // 2
    down = [jnp.where(apart == 4 * yb, 0.5, 0.0).astype(BF16) for yb in range(8)]
    coarse = jnp.dot(
        halves(summed, 0), jnp.concatenate(down, axis=0), preferred_element_type=F32
    )
    coarse = coarse[0:64] + coarse[64:128]
    below, above = [], []
    own = []
    for xb in range(8):
        part = coarse[xb * 8 : xb * 8 + 8]
        own.append(part[1:5, 0:128])
        own.append(part[1:5, 128:256])
        below.append(part[0:1, 0:128])
        above.append(part[5:6, 128:256])
    sent = jnp.concatenate(own + below + above, axis=0)
    for e in range(8):
        sent_ref[e] = sent


def source_step(scalars, occupations, own):
    smem = pl.BlockSpec(memory_space=pltpu.SMEM)
    vmem = pl.BlockSpec(memory_space=pltpu.VMEM)
    return pl.pallas_call(
        source_kernel,
        out_shape=(
            jax.ShapeDtypeStruct((8, 80, 128), F32),
            jax.ShapeDtypeStruct((96, 128), F32),
            jax.ShapeDtypeStruct((96, 128), F32),
        ),
        in_specs=[smem, smem, vmem],
        out_specs=(vmem, vmem, vmem),
        scratch_shapes=[pltpu.VMEM((64, 40, 128), F32)] * 3 + COUPLINGS,
        compiler_params=VMEM,
    )(scalars, occupations, own)


def double_rows(scratch, value, n):
    scratch[:, pl.ds(0, n, stride=2), :] = value
    scratch[:, pl.ds(1, n, stride=2), :] = value


def coarse_solve(g, v, r1, v2, r2, v3, r3):
    near1, near2, near3 = beside(4, 32, 4), beside(8, 16, 8), beside(16, 8, 8)

    def near(ref, blocks, planes, mat):
        rows = ref[:, 8 : 8 + planes, :]
        y = dot2(rows.reshape(blocks * planes, 128), mat)
        y = y.reshape(blocks, planes, -1)
        total = y[:, :, 0:128] + ref[:, 7 : 7 + planes, :] + ref[:, 9 : 9 + planes, :]
        if blocks > 1:
            none = jnp.zeros((1, planes, 128), F32)
            total = total + jnp.concatenate([none, y[:-1, :, 128:256]], axis=0)
            total = total + jnp.concatenate([y[1:, :, 256:384], none], axis=0)
        return rows, total

    def sweep(ref, source, blocks, planes, mat):
        rows, total = near(ref, blocks, planes, mat)
        ref[:, 8 : 8 + planes, :] = rows + OMEGA * (source() - 6.0 * rows + total)

    def residual(ref, source, blocks, planes, mat):
        rows, total = near(ref, blocks, planes, mat)
        return source() - 6.0 * rows + total

    for ref, planes in ((v, 64), (v2, 32), (v3, 16)):
        border = jnp.zeros((ref.shape[0], 8, 128), F32)
        ref[:, 0:8, :] = border
        ref[:, 8 + planes : 16 + planes, :] = border
    g1 = lambda: g[:, 8:72, :]
    v[:, 8:72, :] = OMEGA * g1()
    sweep(v, g1, 8, 64, near1)
    r1[...] = residual(v, g1, 8, 64, near1)
    pair = r1[:, pl.ds(0, 32, stride=2), :] + r1[:, pl.ds(1, 32, stride=2), :]
    rows = [jnp.concatenate([pair[4 * b + e] for e in range(4)], axis=1) for b in range(2)]
    d = jnp.dot(halves(jnp.concatenate(rows, axis=0), 0), transfers(16, 32, True), preferred_element_type=F32)
    s2 = (d[0:64] + d[64:128]).reshape(2, 32, 128)
    g2 = lambda: s2
    v2[:, 8:40, :] = OMEGA * s2
    sweep(v2, g2, 2, 32, near2)
    r2[...] = residual(v2, g2, 2, 32, near2)
    pair = r2[:, pl.ds(0, 16, stride=2), :] + r2[:, pl.ds(1, 16, stride=2), :]
    both = jnp.concatenate([pair[0], pair[1]], axis=1)
    d = jnp.dot(halves(both, 0), transfers(16, 16, True), preferred_element_type=F32)
    s3 = (d[0:16] + d[16:32]).reshape(1, 16, 128)
    g3 = lambda: s3
    v3[:, 8:24, :] = OMEGA * s3
    for _ in range(COARSE - 1):
        sweep(v3, g3, 1, 16, near3)
    double_rows(r3, v3[:, 8:24, :], 16)
    up = dot2(r3[0], transfers(16, 16, False))
    for b in range(2):
        v2[b, 8:40, :] = v2[b, 8:40, :] + up[:, b * 128 : b * 128 + 128]
    for _ in range(POST):
        sweep(v2, g2, 2, 32, near2)
    double_rows(r1.at[0:2], v2[:, 8:40, :], 32)
    up = dot2(r1[0:2].reshape(128, 128), transfers(16, 32, False))
    for b in range(8):
        part = up[(b // 4) * 64 : (b // 4) * 64 + 64, (b % 4) * 128 : (b % 4) * 128 + 128]
        v[b, 8:72, :] = v[b, 8:72, :] + part
    for _ in range(POST):
        sweep(v, g1, 8, 64, near1)


def finish_kernel(scalars, occ, got_ref, prev_ref, y_ref, next_ref, *refs):
    mat = block_neighbours()
    out_ref = refs[0]
    fx, va, vb, up, g, v, r1, v2, r2, v3, r3, wide = refs[1:13]
    couplings = refs[13:]
    low = lanes_low((8, 128))
    low3 = lanes_low((3, 128))
    slab, factor = scalars[0], OMEGA * (occ[scalars[1]] / 64.0)

    for s in range(8):
        g[:, 8 + 8 * s : 16 + 8 * s, :] = got_ref[SLAB_DEVICE[s], 0:64, :].reshape(8, 8, 128)
    for s in range(8):
        for xb in range(8):
            if s > 0:
                row = 8 + 8 * s - 1
                g[xb, row : row + 1, :] = g[xb, row : row + 1, :] + got_ref[SLAB_DEVICE[s], 64 + xb : 65 + xb, :]
            if s < 7:
                row = 8 + 8 * s + 8
                g[xb, row : row + 1, :] = g[xb, row : row + 1, :] + got_ref[SLAB_DEVICE[s], 72 + xb : 73 + xb, :]
    coarse_solve(g, v, r1, v2, r2, v3, r3)
    double_rows(wide, v[:, pl.ds(8 * slab + 4, 16), :], 16)
    i = lax.broadcasted_iota(jnp.int32, (128, 128), 0)
    o = lax.broadcasted_iota(jnp.int32, (128, 128), 1)
    apart = i - ((o // 16) % 4) * 32 - (o % 8) // 2
    spread = jnp.concatenate(
        [jnp.where(apart == 4 * yb, 1.0, 0.0).astype(BF16) for yb in range(8)], axis=1
    )
    up[...] = dot2(wide[...].reshape(256, 128), spread).reshape(8, 32, 1024)

    def fill():
        for src in range(64):
            o = factor * jnp.square(y_ref[src])
            turned = swap(o)
            rows = slice(src % 32 * 3, src % 32 * 3 + 3)
            p, n = prev_ref[rows, :], next_ref[rows, :]
            p, n = (p, swap(n)) if src < 32 else (swap(p), n)
            fx[src, 8:16, :] = jnp.where(low, 0.0, turned)
            fx[src, 13:16, :] = jnp.where(low3, p, turned[5:8])
            fx[src, 16:24, :] = o
            fx[src, 24:32, :] = jnp.where(low, turned, 0.0)
            fx[src, 24:27, :] = jnp.where(low3, turned[0:3], n)
            out_ref[src, 0:8, :] = y_ref[src]

    fill()
    keep = {r: inside_slab_range(slab, r) for r in (14, 18, 15, 17)}

    def second(src, r, c, near):
        va[src, r : r + 8, :] = jnp.where(keep[r], 1.2 * c + OMEGA * near, 0.0)

    def add_up():
        for src in range(64):
            xb, lanes = src // 8, slice(src % 8 * 128, src % 8 * 128 + 128)
            for r, n in ((14, 8), (22, 4)):
                e = jnp.where(
                    lanes_low((n, 128)), up[xb, r - 8 : r - 8 + n, lanes], up[xb, r : r + n, lanes]
                )
                va[src, r : r + n, :] = va[src, r : r + n, :] + e

    def swept(src, r, c, near):
        return c + (fx[src, r : r + 8, :] - DAMPING * c + OMEGA * near)

    def fourth(src, r, c, near):
        vb[src, r : r + 8, :] = jnp.where(keep[r], swept(src, r, c, near), 0.0)

    def fifth(src, r, c, near):
        out_ref[src, 8:16, :] = swept(src, r, c, near)

    relax(fx, (14, 18), mat, couplings, second)
    add_up()
    relax(va, (15, 17), mat, couplings, fourth)
    relax(vb, (16,), mat, couplings, fifth)


def finish_step(scalars, occupations, got, halo, own):
    smem = pl.BlockSpec(memory_space=pltpu.SMEM)
    vmem = pl.BlockSpec(memory_space=pltpu.VMEM)
    ins = [scalars, occupations, got, halo[0], own, halo[1]]
    return pl.pallas_call(
        finish_kernel,
        out_shape=jax.ShapeDtypeStruct((64, 16, 128), F32),
        in_specs=[smem, smem] + [vmem] * (len(ins) - 2),
        out_specs=vmem,
        scratch_shapes=[
            pltpu.VMEM((64, 40, 128), F32),
            pltpu.VMEM((64, 40, 128), F32),
            pltpu.VMEM((64, 40, 128), F32),
            pltpu.VMEM((8, 32, 1024), F32),
            pltpu.VMEM((8, 80, 128), F32),
            pltpu.VMEM((8, 80, 128), F32),
            pltpu.VMEM((8, 64, 128), F32),
            pltpu.VMEM((2, 48, 128), F32),
            pltpu.VMEM((2, 32, 128), F32),
            pltpu.VMEM((1, 32, 128), F32),
            pltpu.VMEM((1, 32, 128), F32),
            pltpu.VMEM((8, 32, 128), F32),
        ]
        + COUPLINGS,
        compiler_params=VMEM,
    )(*ins)


def exchange(to_next, to_last):
    up = [(SLAB_DEVICE[i], SLAB_DEVICE[i + 1]) for i in range(7)]
    down = [(j, i) for i, j in up]
    return lax.ppermute(to_next, GROUP, up), lax.ppermute(to_last, GROUP, down)


def local(
    orbitals, local_potential, occupations, proj_values, proj_strength, atom_block, atom_offset
):
    core, xlo, ylo = (lax.axis_index(a) for a in GROUP)
    slab = 2 * (xlo * (3 - ylo) + (1 - xlo) * ylo) + core
    lists, strength = atom_lists(slab, proj_strength, atom_block, atom_offset)
    high, low = coupling(HALF)
    mats = (jnp.asarray(high), jnp.asarray(low))

    packed = pack(orbitals, local_potential)
    tiles = projector_tiles(proj_values)
    own = lax.all_to_all(packed, PLANE, 0, 0, tiled=True)

    sigma = HALF_WIDTH / (0.0 - CENTER)
    tau = 2.0 / sigma
    coefs = [(sigma / HALF_WIDTH, 0.0)]
    for _ in range(DEGREE - 1):
        following = 1.0 / (tau - sigma)
        coefs.append((2.0 * following / HALF_WIDTH, sigma * following))
        sigma = following
    older = pot = None
    for k in range(0, DEGREE, 2):
        first, last = k == 0, k == DEGREE - 2
        halo = exchange(own, own)
        outs = list(
            double_step(
                first, last, coefs[k], coefs[k + 1], lists, strength, halo, own, older, pot, tiles, mats
            )
        )
        own = outs.pop(0)
        if first:
            pot = outs.pop(0)
        if not last:
            older = outs.pop(0)

    scalars = jnp.stack([slab, 2 * lax.axis_index("yhi") + lax.axis_index("xhi")]).astype(jnp.int32)
    sent, last_planes, first_planes = source_step(scalars, occupations, own)
    halo = exchange(last_planes, first_planes)
    got = lax.all_to_all(sent, GROUP, 0, 0, tiled=True)
    packed = finish_step(scalars, occupations, got, halo, own)
    back = lax.all_to_all(packed, PLANE, 0, 0, tiled=True)
    filtered, part = unpack(back)
    hartree = jnp.sum(lax.all_to_all(part, BAND, 0, 0, tiled=True), axis=0)
    return filtered.reshape(8, 8, 8, 128), hartree.reshape(8, 8, 128)


def solution(mesh):
    fine = Mesh(
        mesh.devices.reshape(8, 4, 2, 2, 2, 2), (BAND, "yhi", "core", "xhi", "xlo", "ylo")
    )
    bands, grid = P(BAND, GX, GYZ, None), P(GX, GYZ, None)
    return jax.shard_map(
        local,
        mesh=fine,
        in_specs=(bands, grid, P(BAND), P(), P(), P(), P()),
        out_specs=(bands, grid),
        check_vma=False,
    )
```
